128 devices in a mesh: lon: 8 (over x, y_lo), lat: 16 (over z, y_hi, core).
Axes of the slice: x: 4, y: 4 (y_hi: 2, y_lo: 2; y = y_hi * 2 + y_lo), z: 4, core: 2. Of those that a mesh axis runs over, the one named last changes fastest.
Arguments:
- fields: bfloat16 [768, 1024, 128], P('lon', 'lat'), may hold values from -6 to 6
- land_sea: int32 [768, 1024], P('lon', 'lat'), may hold values 0 or 1
- tile_list: int32 [8, 16, 72], P('lon', 'lat'), may hold values from -1 to 95, as said below
- upstream: bfloat16 [768, 1024, 128], P('lon', 'lat'), may hold values from -6 to 6
- dw_weight: float32 [49, 128], replicated, may hold values from -0.875 to 0.875
- dw_bias: float32 [128], replicated, may hold values from -3 to 3
- ln_gain: float32 [128], replicated, may hold values from 0.1 to 1.9
- ln_bias: float32 [128], replicated, may hold values from -3 to 3
- w_in: bfloat16 [128, 512], replicated, may hold values from -0.5 to 0.5
- b_in: float32 [512], replicated, may hold values from -3 to 3
- w_out: bfloat16 [512, 128], replicated, may hold values from -0.25 to 0.25
- b_out: float32 [128], replicated, may hold values from -3 to 3
- layer_scale: float32 [128], replicated, may hold values from 0.3 to 1.5
Outputs:
- mixed: bfloat16 [768, 1024, 128], P('lon', 'lat')
- grad_input: bfloat16 [768, 1024, 128], P('lon', 'lat')
- grad_w_in: float32 [128, 512], P(None, 'lat')
- grad_w_out: float32 [512, 128], P('lat')
- grad_dw: float32 [49, 128], P(None, 'lat')
- grad_channel: float32 [5, 128], P(None, 'lat')
- grad_b_in: float32 [512], P('lat')
The draws below stay inside these ranges and needn't reach their ends.
Inputs may be any that keep to these rules, and one draw needn't show every extreme that they name: `tile_list`: each device's 72 entries hold distinct tile numbers of its block, followed by -1 in unused slots; at least 24 entries are used, and some device uses all 72.
All inputs are finite; a program needn't handle non-finite values. No bound on the sum of `land_sea` on one device may be relied on, other than what follows from the above.
Results may differ from the reference program's by a relative error of at most 0.0064.
Values may be sent and summed in bfloat16 or wider, within the bound.
A program may use at most 128 MiB of HBM per device.

```python
import math
import jax
import jax.numpy as jnp
from jax import lax

C = 128
FF = 512
CLON = 96
CLAT = 64
TPD = 96
TCAP = 72
NLON = 768
NLAT = 1024
N_LON = 8
N_LAT = 16


def draw_tile_list(key, part):
    key = jax.random.fold_in(key, 11)
    key_count, key_full, key_order = jax.random.split(key, 3)
    devices = N_LON * N_LAT
    counts = jax.random.randint(key_count, (devices,), TCAP // 3, TCAP + 1)
    full_dev = jax.random.randint(key_full, (), 0, devices)
    counts = jnp.where(jnp.arange(devices) == full_dev, TCAP, counts)
    orders = jax.vmap(lambda k: jax.random.permutation(k, TPD))(jax.random.split(key_order, devices))
    slot_pos = jnp.arange(TCAP)
    listed = jnp.where(slot_pos[None, :] < counts[:, None], orders[:, :TCAP], -1)
    return listed.reshape(N_LON, N_LAT, TCAP).astype(jnp.int32)


def with_ends(values, stream_key, smallest, top_value):
    extent = values.shape
    index_at = [jax.random.randint(jax.random.fold_in(stream_key, axis), (), 0, extent[axis]) for axis in range(len(extent))]
    values = values.at[tuple(index_at)].set(smallest)
    longest = extent.index(max(extent))
    index_at[longest] = (index_at[longest] + 1) % extent[longest]
    return values.at[tuple(index_at)].set(top_value)


def steps_of(rng, dims, pieces, smallest, largest):
    level = 1.0
    for position, blocks in pieces:
        heights = jax.random.uniform(jax.random.fold_in(jax.random.fold_in(rng, 6), position), (blocks,), jnp.float32, smallest / len(pieces), largest / len(pieces))
        level = level * jnp.repeat(jnp.exp(heights), dims[position] // blocks).reshape((-1,) + (1,) * (len(dims) - 1 - position))
    return level


def noise(stream_key, extent, deviation, most, cuts=(), kind=jnp.bfloat16):
    result = jax.random.normal(stream_key, extent, jnp.float32) * deviation
    if len(cuts) > 0:
        result = steps_of(stream_key, extent, cuts, -0.22, 0.18) * result
    return jnp.clip(result, min=-most, max=most).astype(kind)


def setup_inputs(seed: int = 0) -> dict:
    splits = jax.random.split(jax.random.key(seed), 14)
    fields = noise(splits[0], (NLON, NLAT, C), 1.0, 6.0, ((0, 8), (1, 16)))
    land_sea = with_ends((jax.random.randint(splits[1], (NLON, NLAT), 0, 4) < 3).astype(jnp.int32), jax.random.fold_in(splits[1], 1), 0, 1)
    tile_list = draw_tile_list(jax.random.fold_in(splits[13], 71), 0)
    upstream = noise(splits[3], (NLON, NLAT, C), 1.0, 6.0, ((0, 8), (1, 16)))
    dw_weight = noise(splits[4], (49, C), 49 ** -0.5, 0.875, (), jnp.float32)
    dw_bias = noise(splits[5], (C,), 0.5, 3.0, (), jnp.float32)
    ln_gain = jnp.clip(1.0 + 0.18 * jax.random.normal(splits[6], (C,), jnp.float32), 0.1, 1.9)
    ln_bias = noise(splits[7], (C,), 0.5, 3.0, (), jnp.float32)
    w_in = noise(splits[8], (C, FF), C ** -0.5, 0.5)
    b_in = noise(splits[9], (FF,), 0.5, 3.0, (), jnp.float32)
    w_out = noise(splits[10], (FF, C), FF ** -0.5, 0.25)
    b_out = noise(splits[11], (C,), 0.5, 3.0, (), jnp.float32)
    layer_scale = jnp.clip(jnp.exp(jax.random.uniform(splits[12], (C,), jnp.float32, math.log(0.3), math.log(1.5))), 0.3, 1.5)
    return dict(fields=fields, land_sea=land_sea, tile_list=tile_list, upstream=upstream, dw_weight=dw_weight, dw_bias=dw_bias, ln_gain=ln_gain, ln_bias=ln_bias, w_in=w_in, b_in=b_in, w_out=w_out, b_out=b_out, layer_scale=layer_scale)


LN_EPSILON = 1e-06

def conv_taps(padded, weight, lon_cells, lat_cells):
    running = jnp.zeros((lon_cells, lat_cells, padded.shape[2]), jnp.float32)
    for a in range(7):
        for b in range(7):
            running = running + padded[a:a + lon_cells, b:b + lat_cells].astype(jnp.float32) * weight[a * 7 + b]
    return running

def backward_taps(grad_pad, padded, weight, lon_cells, lat_cells):
    running = jnp.zeros((lon_cells, lat_cells, padded.shape[2]), jnp.float32)
    d_conv = grad_pad[3:3 + lon_cells, 3:3 + lat_cells].astype(jnp.float32)
    tap_sums = []
    for a in range(7):
        for b in range(7):
            running = running + grad_pad[6 - a:6 - a + lon_cells, 6 - b:6 - b + lat_cells].astype(jnp.float32) * weight[a * 7 + b]
            tap_sums.append(lax.optimization_barrier(jnp.sum(padded[a:a + lon_cells, b:b + lat_cells].astype(jnp.float32) * d_conv, axis=(0, 1))))
    return (running, jnp.stack(tap_sums))

def to_tiles(cell_grid):
    shape_in = cell_grid.shape
    trailing = shape_in[2:]
    r = cell_grid.reshape((shape_in[0] // 8, 8, shape_in[1] // 8, 8) + trailing)
    r = jnp.swapaxes(r, 1, 2)
    return r.reshape((shape_in[0] // 8 * (shape_in[1] // 8), 64) + trailing)

def from_tiles(tile_stack, lon_cells, lat_cells):
    trailing = tile_stack.shape[2:]
    r = tile_stack.reshape((lon_cells // 8, lat_cells // 8, 8, 8) + trailing)
    r = jnp.swapaxes(r, 1, 2)
    return r.reshape((lon_cells, lat_cells) + trailing)

def gelu_slope(hidden):
    normal_cdf = 0.5 * (1.0 + lax.erf(hidden * (1.0 / math.sqrt(2.0))))
    normal_pdf = jnp.exp(-0.5 * hidden * hidden) * (1.0 / math.sqrt(2.0 * math.pi))
    return normal_cdf + hidden * normal_pdf

def contract_rows(first_op, second_op):
    return lax.dot_general(first_op, second_op, (((0,), (0,)), ((), ())), preferred_element_type=jnp.float32)

def contract_cols(first_op, second_op):
    return lax.dot_general(first_op, second_op, (((1,), (1,)), ((), ())), preferred_element_type=jnp.float32)

def cell_rows(conv_rows, active, up_rows, params):
    ln_gain, ln_bias, w_in, b_in, w_out, b_out, layer_scale = params
    center = conv_rows - lax.optimization_barrier(jnp.mean(conv_rows, axis=-1, keepdims=True))
    variance = lax.optimization_barrier(jnp.mean(center * center, axis=-1, keepdims=True))
    inv_std = lax.rsqrt(variance + LN_EPSILON)
    normed = center * inv_std
    normed_b = (normed * ln_gain + ln_bias).astype(jnp.bfloat16)
    hidden = jnp.dot(normed_b, w_in, preferred_element_type=jnp.float32) + b_in
    activated = jax.nn.gelu(hidden, approximate=False).astype(jnp.bfloat16)
    output = jnp.dot(activated, w_out, preferred_element_type=jnp.float32) + b_out
    branch = active[:, None] * layer_scale * output
    up_float = up_rows.astype(jnp.float32)
    d_out = active[:, None] * layer_scale * up_float
    d_out_b = d_out.astype(jnp.bfloat16)
    g_wout = contract_rows(activated, d_out_b)
    g_scale = lax.optimization_barrier(jnp.sum(active[:, None] * output * up_float, axis=0))
    d_hidden = contract_cols(d_out_b, w_out) * gelu_slope(hidden)
    d_hidden_b = d_hidden.astype(jnp.bfloat16)
    g_win = contract_rows(normed_b, d_hidden_b)
    d_norm = contract_cols(d_hidden_b, w_in)
    d_scaled = d_norm * ln_gain
    d_conv = inv_std * (d_scaled - lax.optimization_barrier(jnp.mean(d_scaled, axis=-1, keepdims=True)) - normed * lax.optimization_barrier(jnp.mean(d_scaled * normed, axis=-1, keepdims=True)))
    channel_sums = jnp.stack([lax.optimization_barrier(jnp.sum(d_conv, axis=0)), lax.optimization_barrier(jnp.sum(d_norm * normed, axis=0)), lax.optimization_barrier(jnp.sum(d_norm, axis=0)), lax.optimization_barrier(jnp.sum(d_out, axis=0)), g_scale])
    grad_terms = (g_win, g_wout, lax.optimization_barrier(jnp.sum(d_hidden, axis=0)), channel_sums)
    return (branch, d_conv.astype(jnp.bfloat16), grad_terms)

def listed_rows(conv_out, land_float, up_grid, tile_ids, params):
    lon_cells, lat_cells, channels = conv_out.shape
    tile_count = lon_cells // 8 * (lat_cells // 8)
    slot_count = tile_ids.shape[0]
    slot_tile = jnp.maximum(tile_ids, 0)
    slot_live = (tile_ids >= 0).astype(jnp.float32)
    conv_rows = to_tiles(conv_out)[slot_tile].reshape(-1, channels)
    active = (to_tiles(land_float)[slot_tile] * slot_live[:, None]).reshape(-1)
    up_rows = to_tiles(up_grid)[slot_tile].reshape(-1, channels)
    branch, d_conv_b, grad_terms = cell_rows(conv_rows, active, up_rows, params)
    branch_tiles = jnp.zeros((tile_count, 64, channels), jnp.float32).at[slot_tile].add(branch.reshape(slot_count, 64, channels))
    d_conv_tiles = jnp.zeros((tile_count, 64, channels), jnp.bfloat16).at[slot_tile].add(d_conv_b.reshape(slot_count, 64, channels))
    return (from_tiles(branch_tiles, lon_cells, lat_cells), from_tiles(d_conv_tiles, lon_cells, lat_cells), grad_terms)

def reference(fields, land_sea, tile_list, upstream, dw_weight, dw_bias, ln_gain, ln_bias, w_in, b_in, w_out, b_out, layer_scale):
    devices = N_LON * N_LAT
    params = (ln_gain, ln_bias, w_in, b_in, w_out, b_out, layer_scale)

    def to_blocks(arr):
        trailing = arr.shape[2:]
        r = arr.reshape((N_LON, CLON, N_LAT, CLAT) + trailing)
        r = jnp.swapaxes(r, 1, 2)
        return r.reshape((devices, CLON, CLAT) + trailing)

    def from_blocks(arr):
        trailing = arr.shape[3:]
        r = arr.reshape((N_LON, N_LAT, CLON, CLAT) + trailing)
        r = jnp.swapaxes(r, 1, 2)
        return r.reshape((NLON, NLAT) + trailing)

    def pad_grid(arr):
        wrapped = jnp.pad(arr, ((3, 3), (0, 0), (0, 0)), mode='wrap')
        return jnp.pad(wrapped, ((0, 0), (3, 3), (0, 0)))
    masked = fields * land_sea.astype(jnp.bfloat16)[:, :, None]
    padded = pad_grid(masked)
    anchor = jnp.zeros((), jnp.int32)

    def local_slice(source, device):
        lon_idx = (device // N_LAT).astype(jnp.int32)
        lat_idx = (device % N_LAT).astype(jnp.int32)
        return lax.dynamic_slice(source, (lon_idx * CLON, lat_idx * CLAT, anchor), (CLON + 6, CLAT + 6, C))

    def first_pass(running_sum, item):
        device, tile_ids, field_blk, land_blk, up_blk = item
        local = local_slice(padded, device)
        conv_out = conv_taps(local, dw_weight, CLON, CLAT) + dw_bias
        branch_grid, d_conv_grid, grad_terms = listed_rows(conv_out, land_blk.astype(jnp.float32), up_blk, tile_ids, params)
        mixed_blk = (field_blk.astype(jnp.float32) + branch_grid).astype(jnp.bfloat16)
        return (tuple((r + g for r, g in zip(running_sum, grad_terms))), (mixed_blk, d_conv_grid))
    start = (jnp.zeros((C, FF), jnp.float32), jnp.zeros((FF, C), jnp.float32), jnp.zeros((FF,), jnp.float32), jnp.zeros((5, C), jnp.float32))
    device_ids = jnp.arange(devices, dtype=jnp.int32)
    land_blocks = to_blocks(land_sea)
    up_blocks = to_blocks(upstream)
    sums, (mixed_blocks, d_conv_blocks) = lax.scan(first_pass, start, (device_ids, tile_list.reshape(devices, TCAP), to_blocks(fields), land_blocks, up_blocks))
    grad_padded = pad_grid(from_blocks(d_conv_blocks))

    def second_pass(running_sum, item):
        device, land_blk, up_blk = item
        local = local_slice(padded, device)
        grad_local = local_slice(grad_padded, device)
        masked_grad, tap_sums = backward_taps(grad_local, local, dw_weight, CLON, CLAT)
        grad_blk = (up_blk.astype(jnp.float32) + land_blk.astype(jnp.float32)[:, :, None] * masked_grad).astype(jnp.bfloat16)
        return (running_sum + tap_sums, grad_blk)
    tap_total, grad_blocks = lax.scan(second_pass, jnp.zeros((49, C), jnp.float32), (device_ids, land_blocks, up_blocks))
    grad_scale = 1.0 / math.sqrt(NLON * NLAT)
    g_win, g_wout, g_bin, channel_sums = sums
    return (from_blocks(mixed_blocks), from_blocks(grad_blocks), g_win * grad_scale, g_wout * grad_scale, tap_total * grad_scale, channel_sums * grad_scale, g_bin * grad_scale)
```

```python
import functools
import math

import jax
import jax.numpy as jnp
from jax import lax
from jax.experimental import pallas as pl
from jax.experimental.pallas import tpu as pltpu
from jax.sharding import PartitionSpec as P

LN_EPSILON = 1e-06
MESH = pl.DeviceIdType.MESH
F32 = jnp.float32
BF16 = jnp.bfloat16
CLON, CLAT, C, FF = 96, 64, 128, 512
NI, NJ = CLON // 8, CLAT // 8
TILES = NI * NJ
TCAP = 72
NG = 8
ZR = 80
N_LON, N_LAT = 8, 16
SHIFTS = (-4, -2, 0, 2)
GRAD_SCALE = 1.0 / math.sqrt(768 * 1024)
VMEM_LIMIT = 56 * 1024 * 1024
ERF_COEFS = (0.7978822019328625, 0.03634471964933557, -4.4922105999092954e-05,
             -5.0349129465290195e-05, 3.0967343000773035e-06, -6.63025075261232e-08)


def iota(shape, dim):
    return lax.broadcasted_iota(jnp.int32, shape, dim)


def block_transpose(rows):
    block = iota(rows[0].shape, 1) // 16
    turned = [r if n == 0 else pltpu.roll(r, 16 * n, axis=1) for n, r in enumerate(rows)]
    u = [turned[(-n) % 8] for n in range(8)]
    for s in (1, 2, 4):
        bit = (block & s) != 0
        u = [jnp.where(bit, u[(m - s) % 8], u[m]) for m in range(8)]
    return [r if m == 0 else pltpu.roll(r, 128 - 16 * m, axis=1) for m, r in enumerate(u)]


def build_weights(w_ref, W, flip):
    q_row, q_col = iota((56, 49), 0), iota((56, 49), 1)
    a, b = q_row // 8, q_row % 8
    tap = (6 - a) * 7 + (6 - b) if flip else a * 7 + b
    pick = jnp.where((q_col == tap) & (b < 7), 1.0, 0.0).astype(BF16)
    taps = jnp.dot(pick, w_ref[...].astype(BF16), preferred_element_type=F32).astype(BF16)
    lane_i = iota((8, 128), 1) // 16
    same = (iota((16, 128), 0) == iota((16, 128), 1) % 16).astype(F32)

    def group(g, carry):
        spread = jnp.where(iota((128, 128), 0) == 16 * g + iota((128, 128), 1) % 16, 1.0, 0.0).astype(BF16)
        rep = jnp.dot(taps, spread, preferred_element_type=F32)
        for i_in in range(16):
            v = jnp.zeros((8, 128), F32)
            for a in range(7):
                if 0 <= i_in - 1 - a < 8:
                    v = jnp.where(lane_i == i_in - 1 - a, rep[8 * a : 8 * a + 8], v)
            base = (i_in // 8) * 512 + (i_in % 8) * 16
            W[g, base : base + 16, 0:128] = jnp.zeros((16, 128), BF16)
            for b in range(7):
                parity = (b + 1) % 2
                e = (b - 3 - parity + 4) // 2
                row = jnp.broadcast_to(v[b : b + 1], (16, 128)) * same
                W[g, base + 128 * e : base + 128 * e + 16, 128 * parity : 128 * parity + 128] = row.astype(BF16)
        return carry

    lax.fori_loop(0, NG, group, 0)


def pack_edges(X, EL, ER, first):
    low = iota((8, 128), 0) < 4

    def block(n, carry):
        left = X[first + n * NJ].astype(F32)
        right = X[first + n * NJ + NJ - 1].astype(F32)
        el, er = [], []
        for m in range(4):
            even, odd = left[16 * m : 16 * m + 8], left[16 * m + 8 : 16 * m + 16]
            el.append(jnp.where(low, even, pltpu.roll(odd, 4, axis=0)))
            even, odd = right[16 * m : 16 * m + 8], right[16 * m + 8 : 16 * m + 16]
            er.append(jnp.where(low, pltpu.roll(even, 4, axis=0), odd))
        EL[n] = jnp.concatenate(el, axis=0).astype(BF16)
        ER[n] = jnp.concatenate(er, axis=0).astype(BF16)
        return carry

    lax.fori_loop(0, NI, block, 0)


def halo_copies(X, EL, ER, LH, RH, send, recv, lon, lat):
    up, down = lax.rem(lon + 1, N_LON), lax.rem(lon + N_LON - 1, N_LON)
    east, west = lax.rem(lat + 1, N_LAT), lax.rem(lat + N_LAT - 1, N_LAT)
    plan = (
        (EL, RH.at[pl.ds(1, NI)], (lon, west)),
        (ER, LH.at[pl.ds(1, NI)], (lon, east)),
        (X.at[pl.ds(NJ, NJ), pl.ds(0, 32)], X.at[pl.ds(13 * NJ, NJ), pl.ds(0, 32)], (down, lat)),
        (X.at[pl.ds(12 * NJ, NJ), pl.ds(32, 32)], X.at[pl.ds(0, NJ), pl.ds(32, 32)], (up, lat)),
        (EL.at[0, pl.ds(0, 16)], RH.at[13, pl.ds(0, 16)], (down, west)),
        (EL.at[NI - 1, pl.ds(16, 16)], RH.at[0, pl.ds(16, 16)], (up, west)),
        (ER.at[0, pl.ds(0, 16)], LH.at[13, pl.ds(0, 16)], (down, east)),
        (ER.at[NI - 1, pl.ds(16, 16)], LH.at[0, pl.ds(16, 16)], (up, east)),
    )
    return [
        pltpu.make_async_remote_copy(
            src_ref=src, dst_ref=dst, send_sem=send.at[n], recv_sem=recv.at[n], device_id=where, device_id_type=MESH
        )
        for n, (src, dst, where) in enumerate(plan)
    ]


def neighbours(lon, lat):
    up, down = lax.rem(lon + 1, N_LON), lax.rem(lon + N_LON - 1, N_LON)
    east, west = lax.rem(lat + 1, N_LAT), lax.rem(lat + N_LAT - 1, N_LAT)
    return [(lon, west), (lon, east), (down, lat), (up, lat), (down, west), (up, west), (down, east), (up, east)]


def greet(places):
    barrier = pltpu.get_barrier_semaphore()
    for place in places:
        pl.semaphore_signal(barrier, inc=1, device_id=place, device_id_type=MESH)
    pl.semaphore_wait(barrier, len(places))


def spread_blocks(X, LH, RH, PS, Z, keep_left, keep_right):
    PS[:, 0:8] = jnp.zeros((NG, 8, 128), F32)
    PS[:, 88:104] = jnp.zeros((NG, 16, 128), F32)

    def block(k, carry):
        def put(rows, at):
            for g, r in enumerate(block_transpose(rows)):
                PS[g, at : at + rows[0].shape[0]] = r

        for t in range(NJ):
            lower = X[k * NJ + t, 32:64].astype(F32)
            upper = X[(k + 1) * NJ + t, 0:32].astype(F32)
            rows = [lower[8 * i : 8 * i + 8] for i in range(4)] + [upper[8 * i : 8 * i + 8] for i in range(4)]
            put(rows, 16 + 8 * t)
        for H, keep, at, flip in ((LH, keep_left, 8, 0), (RH, keep_right, 80, 1)):
            pairs = []
            for edge in (H[k, 16:32].astype(F32) * keep, H[k + 1, 0:16].astype(F32) * keep):
                pairs += [edge[0:8], edge[8:16]]
            rows = []
            for pair in pairs:
                other = pltpu.roll(pair, 4, axis=0)
                rows += [pair, other] if flip else [other, pair]
            put(rows, at)
        for g in range(NG):
            for e, shift in enumerate(SHIFTS):
                Z[g, k, :, 128 * e : 128 * e + 128] = PS[g, 16 + shift : 16 + shift + ZR].astype(BF16)
        return carry

    lax.fori_loop(0, NI + 1, block, 0)


def banded_conv(Z, W, AB, S):
    def group(g, carry):
        lhs = jnp.concatenate([Z[g, 0:NI].reshape(NI * ZR, 512), Z[g, 1 : NI + 1].reshape(NI * ZR, 512)], axis=1)
        both = jnp.dot(lhs, W[g], preferred_element_type=F32)
        AB[...] = both[:, 128:256]
        for n in range(NI):
            S[g, n] = both[n * ZR : n * ZR + 64, 0:128] + AB[n * ZR + 1 : n * ZR + 65]
        return carry

    lax.fori_loop(0, NG, group, 0)


def conv_kernel(fields, land, w, bias, conv_out, masked_out, X, EL, ER, LH, RH, PS, Z, W, AB, S, land_pad, send, recv):
    lon, lat = lax.axis_index("lon"), lax.axis_index("lat")
    land_pad[...] = jnp.zeros((128, 128), F32)
    land_pad[0:CLON, 0:CLAT] = land[...].astype(F32)
    land_t = land_pad[...].T[0:CLAT]

    def mask_block(n, carry):
        turned = pltpu.roll(land_t, lax.rem(128 - 8 * n, 128), axis=1)
        for m in range(4):
            pair = []
            for i in (2 * m, 2 * m + 1):
                keep = jnp.broadcast_to(turned[:, i : i + 1], (CLAT, C))
                pair.append(fields[8 * n + i].astype(F32) * keep)
            for t in range(NJ):
                both = jnp.concatenate([pair[0][8 * t : 8 * t + 8], pair[1][8 * t : 8 * t + 8]], axis=0)
                X[(n + 1) * NJ + t, 16 * m : 16 * m + 16] = both.astype(BF16)
        return carry

    lax.fori_loop(0, NI, mask_block, 0)
    pack_edges(X, EL, ER, NJ)
    greet(neighbours(lon, lat))
    copies = halo_copies(X, EL, ER, LH, RH, send, recv, lon, lat)
    for copy in copies:
        copy.start()
    build_weights(w, W, False)
    masked_out[...] = X[NJ : NJ + TILES]
    for copy in copies:
        copy.wait()
    keep_left = jnp.where(lat > 0, 1.0, 0.0)
    keep_right = jnp.where(lat < N_LAT - 1, 1.0, 0.0)
    spread_blocks(X, LH, RH, PS, Z, keep_left, keep_right)
    banded_conv(Z, W, AB, S)
    offset = jnp.broadcast_to(bias[...], (8, C))

    def back(n, carry):
        for t in range(NJ):
            rows = block_transpose([S[g, n, 8 * t : 8 * t + 8] for g in range(NG)])
            for i in range(8):
                conv_out[n * NJ + t, 8 * i : 8 * i + 8] = rows[i] + offset
        return carry

    lax.fori_loop(0, NI, back, 0)


def vmem(n):
    return [pl.BlockSpec(memory_space=pltpu.VMEM)] * n


def halo_scratch():
    return [
        pltpu.VMEM((14 * NJ, 64, C), BF16),
        pltpu.VMEM((NI, 32, C), BF16),
        pltpu.VMEM((NI, 32, C), BF16),
        pltpu.VMEM((14, 32, C), BF16),
        pltpu.VMEM((14, 32, C), BF16),
        pltpu.VMEM((NG, 104, 128), F32),
        pltpu.VMEM((NG, NI + 1, ZR, 512), BF16),
        pltpu.VMEM((NG, 1024, 256), BF16),
        pltpu.VMEM((NI * ZR, 128), F32),
        pltpu.VMEM((NG, NI, 64, 128), F32),
    ]


def forward_conv(fields, land, w, bias):
    return pl.pallas_call(
        conv_kernel,
        name="forward_conv",
        out_shape=(jax.ShapeDtypeStruct((TILES, 64, C), F32), jax.ShapeDtypeStruct((TILES, 64, C), BF16)),
        in_specs=vmem(4),
        out_specs=tuple(vmem(2)),
        scratch_shapes=halo_scratch()
        + [pltpu.VMEM((128, 128), F32), pltpu.SemaphoreType.DMA((8,)), pltpu.SemaphoreType.DMA((8,))],
        compiler_params=pltpu.CompilerParams(collective_id=0, has_side_effects=True, vmem_limit_bytes=VMEM_LIMIT),
    )(fields, land, w, bias)


def transposed_land(land, land_pad):
    land_pad[...] = jnp.zeros((128, 128), F32)
    land_pad[0:CLON, 0:CLAT] = land[...].astype(F32)
    return land_pad[...].T[0:CLAT]


def normal_cdf(h, square):
    q = jnp.full(h.shape, ERF_COEFS[-1], F32)
    for coef in ERF_COEFS[-2::-1]:
        q = q * square + coef
    return 0.5 + 0.5 * jnp.tanh(h * q)


def mlp_kernel(tile_ids, conv, fields, upstream, land, gain, shift, w_in, b_in, w_out, b_out, scale,
               mixed, d_conv_out, shares, branch, w_in_t, w_out_t, g_in, g_out, g_bin, sums, land_pad, land_tr):
    slots = 4
    rows = slots * 64
    land_tr[...] = transposed_land(land, land_pad)
    w_in_t[...] = w_in[...].astype(F32).T.astype(BF16)
    w_out_t[...] = w_out[...].astype(F32).T.astype(BF16)
    branch[...] = jnp.zeros(branch.shape, F32)
    d_conv_out[...] = jnp.zeros(d_conv_out.shape, BF16)
    for acc in (g_in, g_out, g_bin, sums):
        acc[...] = jnp.zeros(acc.shape, F32)
    gain_row, shift_row, scale_row = gain[...], shift[...], scale[...]

    def step(n, carry):
        ids = [tile_ids[slots * n + q] for q in range(slots)]
        tiles = [jnp.maximum(t, 0) for t in ids]
        conv_parts, up_parts, active_parts = [], [], []
        for q in range(slots):
            t = tiles[q]
            big, small = t // NJ, lax.rem(t, NJ)
            conv_parts.append(conv[t])
            pair = upstream[pl.ds(8 * big, 8), pl.ds(16 * (small // 2), 16), :].astype(F32)
            odd = lax.rem(small, 2) == 1
            up_parts.append(jnp.where(odd, pair[:, 8:16], pair[:, 0:8]).reshape(64, C))
            strip = pltpu.roll(land_tr[pl.ds(8 * small, 8), :], lax.rem(128 - 8 * big, 128), axis=1)
            live = jnp.where(ids[q] >= 0, 1.0, 0.0)
            strip = strip * live
            active_parts += [jnp.broadcast_to(strip[:, i : i + 1], (8, C)) for i in range(8)]
        conv_rows = jnp.concatenate(conv_parts, axis=0)
        up = jnp.concatenate(up_parts, axis=0)
        active = jnp.concatenate(active_parts, axis=0)
        center = conv_rows - jnp.mean(conv_rows, axis=-1, keepdims=True)
        inv_std = lax.rsqrt(jnp.mean(center * center, axis=-1, keepdims=True) + LN_EPSILON)
        normed = center * inv_std
        normed_b = (normed * gain_row + shift_row).astype(BF16)
        hidden = jnp.dot(normed_b, w_in[...], preferred_element_type=F32) + b_in[...]
        bounded = jnp.clip(hidden, -5.0, 5.0)
        square = bounded * bounded
        cdf = normal_cdf(bounded, square)
        activated = (hidden * cdf).astype(BF16)
        output = jnp.dot(activated, w_out[...], preferred_element_type=F32) + b_out[...]
        gate = active * scale_row
        branch_rows = gate * output
        d_out = gate * up
        d_out_b = d_out.astype(BF16)
        g_out[...] += lax.dot_general(d_out_b, activated, (((0,), (0,)), ((), ())), preferred_element_type=F32)
        pdf = jnp.exp(-0.5 * (hidden * hidden)) * (1.0 / math.sqrt(2.0 * math.pi))
        d_hidden = jnp.dot(d_out_b, w_out_t[...], preferred_element_type=F32) * (cdf + hidden * pdf)
        d_hidden_b = d_hidden.astype(BF16)
        g_in[...] += lax.dot_general(normed_b, d_hidden_b, (((0,), (0,)), ((), ())), preferred_element_type=F32)
        g_bin[...] += jnp.sum(d_hidden.reshape(rows // 8, 8, FF), axis=0)
        d_norm = jnp.dot(d_hidden_b, w_in_t[...], preferred_element_type=F32)
        d_scaled = d_norm * gain_row
        d_conv = inv_std * (
            d_scaled
            - jnp.mean(d_scaled, axis=-1, keepdims=True)
            - normed * jnp.mean(d_scaled * normed, axis=-1, keepdims=True)
        )
        for k, term in enumerate((d_conv, d_norm * normed, d_norm, d_out, active * output * up)):
            sums[k] += jnp.sum(term.reshape(rows // 8, 8, C), axis=0)
        d_conv_b = d_conv.astype(BF16)
        for q in range(slots):

            @pl.when(ids[q] >= 0)
            def _(q=q):
                branch[tiles[q]] = branch_rows[64 * q : 64 * q + 64]
                d_conv_out[tiles[q]] = d_conv_b[64 * q : 64 * q + 64]

        return carry

    lax.fori_loop(0, TCAP // slots, step, 0)

    def mix(n, carry):
        for i in range(8):
            rows_i = jnp.concatenate([branch[n * NJ + t, 8 * i : 8 * i + 8] for t in range(NJ)], axis=0)
            mixed[8 * n + i] = (fields[8 * n + i].astype(F32) + rows_i).astype(BF16)
        return carry

    lax.fori_loop(0, NI, mix, 0)
    bin_row = jnp.sum(g_bin[...], axis=0, keepdims=True)
    tail = jnp.concatenate([jnp.sum(sums[k], axis=0, keepdims=True) for k in range(5)], axis=0)
    for n in range(4):
        turned_in = g_in[:, 128 * n : 128 * n + 128].T
        turned_out = g_out[:, 128 * n : 128 * n + 128].T
        for m in range(4):
            q = 4 * n + m
            shares[q, 0:32] = turned_in[32 * m : 32 * m + 32]
            shares[q, 32:64] = turned_out[32 * m : 32 * m + 32]
            shares[q, 64:65] = bin_row[:, 128 * n : 128 * n + 128]
            shares[q, 65:70] = tail
            shares[q, 70:72] = jnp.zeros((2, 128), F32)


def listed_mlp(tile_ids, conv, fields, upstream, land, gain, shift, w_in, b_in, w_out, b_out, scale):
    return pl.pallas_call(
        mlp_kernel,
        name="listed_mlp",
        out_shape=(
            jax.ShapeDtypeStruct((CLON, CLAT, C), BF16),
            jax.ShapeDtypeStruct((TILES, 64, C), BF16),
            jax.ShapeDtypeStruct((N_LAT, 72, 128), F32),
        ),
        in_specs=[pl.BlockSpec(memory_space=pltpu.SMEM)] + vmem(11),
        out_specs=tuple(vmem(3)),
        scratch_shapes=[
            pltpu.VMEM((TILES, 64, C), F32),
            pltpu.VMEM((FF, C), BF16),
            pltpu.VMEM((C, FF), BF16),
            pltpu.VMEM((C, FF), F32),
            pltpu.VMEM((C, FF), F32),
            pltpu.VMEM((8, FF), F32),
            pltpu.VMEM((5, 8, C), F32),
            pltpu.VMEM((128, 128), F32),
            pltpu.VMEM((CLAT, 128), F32),
        ],
        compiler_params=pltpu.CompilerParams(vmem_limit_bytes=VMEM_LIMIT),
    )(tile_ids, conv, fields, upstream, land, gain, shift, w_in, b_in, w_out, b_out, scale)


def spread_masked(masked, PS, MP):
    PS[:, 0:8] = jnp.zeros((NG, 8, 128), F32)
    PS[:, 72:104] = jnp.zeros((NG, 32, 128), F32)

    def block(n, carry):
        for t in range(NJ):
            tile = masked[n * NJ + t].astype(F32)
            rows = block_transpose([tile[8 * i : 8 * i + 8] for i in range(8)])
            for g in range(NG):
                PS[g, 8 + 8 * t : 16 + 8 * t] = rows[g]
        for g in range(NG):
            MP[g, n, :, 0:128] = PS[g, 8 : 8 + ZR].astype(BF16)
            MP[g, n, :, 128:256] = PS[g, 7 : 7 + ZR].astype(BF16)
        return carry

    lax.fori_loop(0, NI, block, 0)


def tap_gradients(Z, MP, G, taps):
    lane = iota((16, 128), 1)
    same = (iota((16, 128), 0) == lane % 16).astype(F32)
    block = lane // 16
    taps[...] = jnp.zeros(taps.shape, F32)

    def group(g, carry):
        lhs = MP[g].reshape(NI * ZR, 256)
        for half in range(2):
            rhs = Z[g, half : half + NI].reshape(NI * ZR, 512)
            G[half] = lax.dot_general(lhs, rhs, (((0,), (0,)), ((), ())), preferred_element_type=F32)
        for e in range(4):
            for parity in range(2):
                b = 3 - SHIFTS[e] - parity
                if not 0 <= b < 7:
                    continue
                for a in range(7):
                    total = None
                    for i_out in range(8):
                        half, k = divmod(i_out + 7 - a, 8)
                        at = 128 * parity + 16 * i_out
                        piece = G[half, at : at + 16, 128 * e : 128 * e + 128]
                        total = piece if total is None else jnp.where(block == k, piece, total)
                    taps[g, 7 * a + b : 7 * a + b + 1] = jnp.sum(total * same, axis=0, keepdims=True)
        return carry

    lax.fori_loop(0, NG, group, 0)


def gather_taps(taps, square, tap_shares):
    total = jnp.zeros((56, 128), F32)
    for g in range(NG):
        row, col = iota((128, 128), 0), iota((128, 128), 1)
        pick = jnp.where((col // 16 == g) & (row % 16 == col % 16), 1.0, 0.0).astype(BF16)
        value = taps[g]
        head = value.astype(BF16)
        tail = (value - head.astype(F32)).astype(BF16)
        total += jnp.dot(head, pick, preferred_element_type=F32) + jnp.dot(tail, pick, preferred_element_type=F32)
    square[...] = jnp.zeros((128, 128), F32)
    square[0:56] = total
    turned = square[...].T
    for q in range(N_LAT):
        tap_shares[q] = turned[8 * q : 8 * q + 8]


def grad_kernel(d_conv, masked, upstream, land, w, shares,
                grad_input, out_win, out_wout, out_dw, out_channel, out_bin,
                X, EL, ER, LH, RH, PS, Z, W, AB, S, MP, G, taps, square, tap_shares, parts, tap_parts, mine, whole,
                send, recv, send_one, recv_one, send_tap, recv_tap, send_two, recv_two):
    lon, lat = lax.axis_index("lon"), lax.axis_index("lat")
    X[NJ : NJ + TILES] = d_conv[...]
    pack_edges(X, EL, ER, NJ)
    around = neighbours(lon, lat)
    others = [(lon, lax.rem(lat + d, N_LAT)) for d in range(2, N_LAT - 1)]
    others += [(lax.rem(lon + d, N_LON), lat) for d in range(2, N_LON - 1)]
    greet(around + others)
    copies = halo_copies(X, EL, ER, LH, RH, send, recv, lon, lat)
    for copy in copies:
        copy.start()
    share_copies, tap_copies = [], []
    for d in range(1, N_LAT):
        to = lax.rem(lat + d, N_LAT)
        share_copies.append(pltpu.make_async_remote_copy(
            src_ref=shares.at[to], dst_ref=parts.at[d], send_sem=send_one.at[d], recv_sem=recv_one.at[d],
            device_id=(lon, to), device_id_type=MESH))
        tap_copies.append(pltpu.make_async_remote_copy(
            src_ref=tap_shares.at[to], dst_ref=tap_parts.at[d], send_sem=send_tap.at[d], recv_sem=recv_tap.at[d],
            device_id=(lon, to), device_id_type=MESH))
    for copy in share_copies:
        copy.start()
    build_weights(w, W, True)
    spread_masked(masked, PS, MP)
    for copy in copies:
        copy.wait()
    keep_left = jnp.where(lat > 0, 1.0, 0.0)
    keep_right = jnp.where(lat < N_LAT - 1, 1.0, 0.0)
    spread_blocks(X, LH, RH, PS, Z, keep_left, keep_right)
    tap_gradients(Z, MP, G, taps)
    gather_taps(taps, square, tap_shares)
    for copy in tap_copies:
        copy.start()
    banded_conv(Z, W, AB, S)
    for copy in share_copies:
        copy.wait()
    for copy in tap_copies:
        copy.wait()
    total = shares[lat]
    tap_total = tap_shares[lat]
    for d in range(1, N_LAT):
        total += parts[d]
        tap_total += tap_parts[d]
    mine[0:72] = total * GRAD_SCALE
    mine[72:80] = tap_total * GRAD_SCALE
    last_copies = [
        pltpu.make_async_remote_copy(
            src_ref=mine, dst_ref=whole.at[d], send_sem=send_two.at[d], recv_sem=recv_two.at[d],
            device_id=(lax.rem(lon + d, N_LON), lat), device_id_type=MESH)
        for d in range(1, N_LON)
    ]
    for copy in last_copies:
        copy.start()
    square[...] = jnp.zeros((128, 128), F32)
    square[0:CLON, 0:CLAT] = land[...].astype(F32)
    land_t = square[...].T[0:CLAT]

    def back(n, carry):
        turned = pltpu.roll(land_t, lax.rem(128 - 8 * n, 128), axis=1)
        for t in range(NJ // 2):
            low = block_transpose([S[g, n, 16 * t : 16 * t + 8] for g in range(NG)])
            high = block_transpose([S[g, n, 16 * t + 8 : 16 * t + 16] for g in range(NG)])
            for i in range(8):
                keep = jnp.broadcast_to(turned[16 * t : 16 * t + 16, i : i + 1], (16, C))
                value = jnp.concatenate([low[i], high[i]], axis=0) * keep
                up = upstream[8 * n + i, 16 * t : 16 * t + 16].astype(F32)
                grad_input[8 * n + i, 16 * t : 16 * t + 16] = (up + value).astype(BF16)
        return carry

    lax.fori_loop(0, NI, back, 0)
    for copy in last_copies:
        copy.wait()
    total = mine[...]
    for d in range(1, N_LON):
        total += whole[d]
    square[...] = jnp.zeros((128, 128), F32)
    square[0:32] = total[0:32]
    out_win[...] = square[...].T[:, 0:32]
    out_wout[...] = total[32:64]
    small = total[64:72]
    out_bin[...] = pltpu.roll(small, lax.rem(128 - 32 * lax.rem(lat, 4), 128), axis=1)[0:1, 0:32]
    out_channel[...] = pltpu.roll(small, lax.rem(128 - 8 * lat, 128), axis=1)[1:6, 0:8]
    square[0:8] = total[72:80]
    out_dw[...] = square[...].T[0:49, 0:8]


def backward_conv(d_conv, masked, upstream, land, w, shares):
    dma = pltpu.SemaphoreType.DMA
    return pl.pallas_call(
        grad_kernel,
        name="backward_conv",
        out_shape=(
            jax.ShapeDtypeStruct((CLON, CLAT, C), BF16),
            jax.ShapeDtypeStruct((C, 32), F32),
            jax.ShapeDtypeStruct((32, C), F32),
            jax.ShapeDtypeStruct((49, 8), F32),
            jax.ShapeDtypeStruct((5, 8), F32),
            jax.ShapeDtypeStruct((1, 32), F32),
        ),
        in_specs=vmem(6),
        out_specs=tuple(vmem(6)),
        scratch_shapes=halo_scratch()
        + [
            pltpu.VMEM((NG, NI, ZR, 256), BF16),
            pltpu.VMEM((2, 256, 512), F32),
            pltpu.VMEM((NG, 56, 128), F32),
            pltpu.VMEM((128, 128), F32),
            pltpu.VMEM((N_LAT, 8, 128), F32),
            pltpu.VMEM((N_LAT, 72, 128), F32),
            pltpu.VMEM((N_LAT, 8, 128), F32),
            pltpu.VMEM((80, 128), F32),
            pltpu.VMEM((N_LON, 80, 128), F32),
            dma((8,)), dma((8,)), dma((N_LAT,)), dma((N_LAT,)), dma((N_LAT,)), dma((N_LAT,)), dma((N_LON,)), dma((N_LON,)),
        ],
        compiler_params=pltpu.CompilerParams(collective_id=1, has_side_effects=True, vmem_limit_bytes=VMEM_LIMIT),
    )(d_conv, masked, upstream, land, w, shares)


def per_device(fields, land_sea, tile_list, upstream, dw_weight, dw_bias, ln_gain, ln_bias, w_in, b_in, w_out, b_out,
               layer_scale):
    def row(v):
        return v.reshape(1, -1)

    conv, masked = forward_conv(fields, land_sea, dw_weight, row(dw_bias))
    mixed, d_conv, shares = listed_mlp(
        tile_list.reshape(-1), conv, fields, upstream, land_sea, row(ln_gain), row(ln_bias), w_in, row(b_in), w_out,
        row(b_out), row(layer_scale))
    grad_input, g_win, g_wout, g_dw, g_channel, g_bin = backward_conv(
        d_conv, masked, upstream, land_sea, dw_weight, shares)
    return mixed, grad_input, g_win, g_wout, g_dw, g_channel, g_bin.reshape(-1)


def solution(mesh):
    cells = P("lon", "lat", None)
    return jax.shard_map(
        per_device,
        mesh=mesh,
        in_specs=(cells, P("lon", "lat"), cells, cells) + (P(),) * 9,
        out_specs=(cells, cells, P(None, "lat"), P("lat", None), P(None, "lat"), P(None, "lat"), P("lat")),
        check_vma=False,
    )
```

```python
import functools
import math

import jax
import jax.numpy as jnp
from jax import lax
from jax.experimental import pallas as pl
from jax.experimental.pallas import tpu as pltpu
from jax.sharding import PartitionSpec as P

LN_EPSILON = 1e-06
MESH = pl.DeviceIdType.MESH
F32 = jnp.float32
BF16 = jnp.bfloat16
CLON, CLAT, C, FF = 96, 64, 128, 512
NI, NJ = CLON // 8, CLAT // 8
TILES = NI * NJ
TCAP = 72
NG = 8
ZR = 80
N_LON, N_LAT = 8, 16
SHIFTS = (-4, -2, 0, 2)
GRAD_SCALE = 1.0 / math.sqrt(768 * 1024)
VMEM_LIMIT = 56 * 1024 * 1024
ERF_COEFS = (0.7978822019328625, 0.03634471964933557, -4.4922105999092954e-05,
             -5.0349129465290195e-05, 3.0967343000773035e-06, -6.63025075261232e-08)


def iota(shape, dim):
    return lax.broadcasted_iota(jnp.int32, shape, dim)


def block_transpose(rows):
    block = iota(rows[0].shape, 1) // 16
    turned = [r if n == 0 else pltpu.roll(r, 16 * n, axis=1) for n, r in enumerate(rows)]
    u = [turned[(-n) % 8] for n in range(8)]
    for s in (1, 2, 4):
        bit = (block & s) != 0
        u = [jnp.where(bit, u[(m - s) % 8], u[m]) for m in range(8)]
    return [r if m == 0 else pltpu.roll(r, 128 - 16 * m, axis=1) for m, r in enumerate(u)]


def build_weights(w_ref, W, flip):
    q_row, q_col = iota((56, 49), 0), iota((56, 49), 1)
    a, b = q_row // 8, q_row % 8
    tap = (6 - a) * 7 + (6 - b) if flip else a * 7 + b
    pick = jnp.where((q_col == tap) & (b < 7), 1.0, 0.0).astype(BF16)
    taps = jnp.dot(pick, w_ref[...].astype(BF16), preferred_element_type=F32).astype(BF16)
    lane_i = iota((8, 128), 1) // 16
    same = (iota((16, 128), 0) == iota((16, 128), 1) % 16).astype(F32)

    def group(g, carry):
        spread = jnp.where(iota((128, 128), 0) == 16 * g + iota((128, 128), 1) % 16, 1.0, 0.0).astype(BF16)
        rep = jnp.dot(taps, spread, preferred_element_type=F32)
        for i_in in range(16):
            v = jnp.zeros((8, 128), F32)
            for a in range(7):
                if 0 <= i_in - 1 - a < 8:
                    v = jnp.where(lane_i == i_in - 1 - a, rep[8 * a : 8 * a + 8], v)
            base = (i_in // 8) * 512 + (i_in % 8) * 16
            W[g, base : base + 16, 0:128] = jnp.zeros((16, 128), BF16)
            for b in range(7):
                parity = (b + 1) % 2
                e = (b - 3 - parity + 4) // 2
                row = jnp.broadcast_to(v[b : b + 1], (16, 128)) * same
                W[g, base + 128 * e : base + 128 * e + 16, 128 * parity : 128 * parity + 128] = row.astype(BF16)
        return carry

    lax.fori_loop(0, NG, group, 0)


def build_permutation(PM):
    def clear(n, carry):
        PM[pl.ds(pl.multiple_of(64 * n, 64), 64), :] = jnp.zeros((64, 1024), BF16)
        return carry

    lax.fori_loop(0, 16, clear, 0)
    row, lane = iota((16, 128), 0), iota((16, 128), 1)
    for p in range(8):
        unit = jnp.where(lane == 16 * p + row, 1.0, 0.0).astype(BF16)
        for q in range(8):
            PM[128 * p + 16 * q : 128 * p + 16 * q + 16, 128 * q : 128 * q + 128] = unit


def expand_mask(land_ext, M, count):
    value = land_ext.astype(BF16)
    row, block = iota((128, 128), 0), iota((128, 128), 1) // 16

    def one(k, carry):
        pick = jnp.where(row == 8 * k + block, 1.0, 0.0).astype(BF16)
        M[k] = jnp.dot(value, pick, preferred_element_type=F32)
        return carry

    lax.fori_loop(0, count, one, 0)


def pack_edges(X, EL, ER, masks):
    low = iota((8, 128), 0) < 4

    def block(n, carry):
        for east, E in ((0, EL), (1, ER)):
            out = []
            keep = None if masks is None else pltpu.roll(masks[east], lax.rem(128 - 8 * n, 128), axis=1)
            for m in range(4):
                pair = []
                for i in (2 * m, 2 * m + 1):
                    cells = X[1 + 2 * n + i // 4, i % 4, 48 * east : 48 * east + 16].astype(F32)
                    pair.append(cells[8 * east : 8 * east + 8])
                if east:
                    value = jnp.where(low, pltpu.roll(pair[0], 4, axis=0), pair[1])
                else:
                    value = jnp.where(low, pair[0], pltpu.roll(pair[1], 4, axis=0))
                if keep is not None:
                    value = value * jnp.broadcast_to(keep[:, 2 * m : 2 * m + 1], (8, 128))
                out.append(value)
            E[n] = jnp.concatenate(out, axis=0).astype(BF16)
        return carry

    lax.fori_loop(0, NI, block, 0)


def halo_copies(X, EL, ER, LH, RH, send, recv, lon, lat):
    up, down = lax.rem(lon + 1, N_LON), lax.rem(lon + N_LON - 1, N_LON)
    east, west = lax.rem(lat + 1, N_LAT), lax.rem(lat + N_LAT - 1, N_LAT)
    plan = (
        (EL, RH.at[pl.ds(1, NI)], (lon, west)),
        (ER, LH.at[pl.ds(1, NI)], (lon, east)),
        (X.at[1], X.at[25], (down, lat)),
        (X.at[24], X.at[0], (up, lat)),
        (EL.at[0, pl.ds(0, 16)], RH.at[13, pl.ds(0, 16)], (down, west)),
        (EL.at[NI - 1, pl.ds(16, 16)], RH.at[0, pl.ds(16, 16)], (up, west)),
        (ER.at[0, pl.ds(0, 16)], LH.at[13, pl.ds(0, 16)], (down, east)),
        (ER.at[NI - 1, pl.ds(16, 16)], LH.at[0, pl.ds(16, 16)], (up, east)),
    )
    return [
        pltpu.make_async_remote_copy(
            src_ref=src, dst_ref=dst, send_sem=send.at[n], recv_sem=recv.at[n], device_id=where, device_id_type=MESH
        )
        for n, (src, dst, where) in enumerate(plan)
    ]


def neighbours(lon, lat):
    up, down = lax.rem(lon + 1, N_LON), lax.rem(lon + N_LON - 1, N_LON)
    east, west = lax.rem(lat + 1, N_LAT), lax.rem(lat + N_LAT - 1, N_LAT)
    return [(lon, west), (lon, east), (down, lat), (up, lat), (down, west), (up, west), (down, east), (up, east)]


def greet(places):
    barrier = pltpu.get_barrier_semaphore()
    for place in places:
        pl.semaphore_signal(barrier, inc=1, device_id=place, device_id_type=MESH)


def greeted(places):
    pl.semaphore_wait(pltpu.get_barrier_semaphore(), len(places))


def clear_margins(PS):
    def block(k, carry):
        PS[:, k, 8:16] = jnp.zeros((NG, 8, 128), F32)
        PS[:, k, 80:104] = jnp.zeros((NG, 24, 128), F32)
        return carry

    lax.fori_loop(0, NI + 1, block, 0)


def group_blocks(cells, blocks, PM, PS, M):
    rows = len(blocks) * 64
    lhs = jnp.concatenate([jnp.concatenate([cells(k, i) for k in blocks], axis=0) for i in range(8)], axis=1)

    def pair(n, carry):
        both = jnp.dot(lhs, PM[:, pl.ds(pl.multiple_of(256 * n, 256), 256)], preferred_element_type=F32)
        for h in range(2):
            for m, k in enumerate(blocks):
                part = both[64 * m : 64 * m + 64, 128 * h : 128 * h + 128]
                PS[2 * n + h, k, 16:80] = part if M is None else part * M[k]
        return carry

    lax.fori_loop(0, NG // 2, pair, 0)


def group_halos(LH, RH, EH, PM, PS, lat):
    low = iota((8, 128), 0) < 4
    keep = jnp.where(low, jnp.where(lat < N_LAT - 1, 1.0, 0.0), jnp.where(lat > 0, 1.0, 0.0))

    def rows_of(k):
        rows = []
        for m in range(4):
            at = (16, 24, 0, 8)[m]
            left = LH[k + m // 2, at // 16 * 16 : at // 16 * 16 + 16].astype(F32)[at % 16 : at % 16 + 8]
            right = RH[k + m // 2, at // 16 * 16 : at // 16 * 16 + 16].astype(F32)[at % 16 : at % 16 + 8]
            rows.append(jnp.where(low, right, pltpu.roll(left, 4, axis=0)) * keep)
            rows.append(jnp.where(low, pltpu.roll(right, 4, axis=0), left) * keep)
        return rows

    for n in range(7):
        first = rows_of(2 * n)
        second = rows_of(2 * n + 1) if 2 * n + 1 <= NI else first
        for i in range(8):
            EH[n, :, 128 * i : 128 * i + 128] = jnp.concatenate([first[i], second[i]], axis=0).astype(BF16)

    def pair(n, carry):
        both = jnp.dot(EH[...].reshape(112, 1024), PM[:, pl.ds(pl.multiple_of(256 * n, 256), 256)],
                       preferred_element_type=F32)
        for h in range(2):
            for k in range(NI + 1):
                part = both[8 * k : 8 * k + 8, 128 * h : 128 * h + 128]
                PS[2 * n + h, k, 8:16] = part
                PS[2 * n + h, k, 80:88] = part
        return carry

    lax.fori_loop(0, NG // 2, pair, 0)


def shift_blocks(PS, Z):
    def block(k, carry):
        for g in range(NG):
            for e, shift in enumerate(SHIFTS):
                Z[g, k, :, 128 * e : 128 * e + 128] = PS[g, k, 16 + shift : 16 + shift + ZR].astype(BF16)
        return carry

    lax.fori_loop(0, NI + 1, block, 0)


INNER = ((1, 2, 3, 4), (5, 6, 7, 8), (9, 10, 11))


def banded_conv(Z, W, AB, S, M):
    def group(g, carry):
        lhs = jnp.concatenate([Z[g, 0:NI].reshape(NI * ZR, 512), Z[g, 1 : NI + 1].reshape(NI * ZR, 512)], axis=1)
        both = jnp.dot(lhs, W[g], preferred_element_type=F32)
        AB[...] = both[:, 128:256]
        for n in range(NI):
            value = both[n * ZR : n * ZR + 64, 0:128] + AB[n * ZR + 1 : n * ZR + 65]
            S[g, n] = value if M is None else (value * M[n]).astype(S.dtype)
        return carry

    lax.fori_loop(0, NG, group, 0)


def conv_kernel(fields, land, w, bias, conv_out, X, EL, ER, LH, RH, EH, PS, Z, W, PM, AB, S, M, land_pad, send, recv,
                load):
    lon, lat = lax.axis_index("lon"), lax.axis_index("lat")
    around = neighbours(lon, lat)
    greet(around)
    copy_in = pltpu.make_async_copy(fields, X.at[pl.ds(1, 24)], load)
    copy_in.start()
    land_pad[...] = jnp.zeros((CLAT, 128), F32)
    land_pad[:, 0:CLON] = land[...].astype(F32)
    land_t = land_pad[...]
    lane = iota((CLAT, 128), 1)
    expand_mask(jnp.where((lane < 4) | (lane >= CLON + 4), 1.0, pltpu.roll(land_t, 4, axis=1)), M, NI + 1)
    low = iota((8, 128), 0) < 4
    masks = []
    for east in range(2):
        edge = land_pad[56 * east : 56 * east + 8]
        turned = pltpu.roll(edge, 4, axis=0)
        edge = jnp.where(low, turned, edge) if east else jnp.where(low, edge, turned)
        masks.append(jnp.where(low, edge, pltpu.roll(edge, 127, axis=1)))
    copy_in.wait()
    pack_edges(X, EL, ER, masks)
    for at, first in ((1, 0), (24, CLON - 4)):
        for i in range(4):
            keep = jnp.broadcast_to(land_t[:, first + i : first + i + 1], (CLAT, C))
            X[at, i] = (X[at, i].astype(F32) * keep).astype(BF16)
    greeted(around)
    copies = halo_copies(X, EL, ER, LH, RH, send, recv, lon, lat)
    for copy in copies:
        copy.start()
    build_permutation(PM)
    clear_margins(PS)

    def cells(k, i):
        return X[2 * k + i // 4, i % 4]

    for blocks in INNER:
        group_blocks(cells, blocks, PM, PS, M)
    build_weights(w, W, False)
    for copy in copies:
        copy.wait()
    group_blocks(cells, (0, NI), PM, PS, M)
    group_halos(LH, RH, EH, PM, PS, lat)
    shift_blocks(PS, Z)
    banded_conv(Z, W, AB, S, None)
    offset = jnp.broadcast_to(bias[...], (8, C))

    def back(n, carry):
        for t in range(NJ):
            rows = block_transpose([S[g, n, 8 * t : 8 * t + 8] for g in range(NG)])
            for i in range(8):
                conv_out[n * NJ + t, 8 * i : 8 * i + 8] = rows[i] + offset
        return carry

    lax.fori_loop(0, NI, back, 0)


def vmem(n):
    return [pl.BlockSpec(memory_space=pltpu.VMEM)] * n


def hbm(n):
    return [pl.BlockSpec(memory_space=pl.ANY)] * n


def halo_scratch(kind):
    return [
        pltpu.VMEM((26, 4, CLAT, C), BF16),
        pltpu.VMEM((NI, 32, C), BF16),
        pltpu.VMEM((NI, 32, C), BF16),
        pltpu.VMEM((14, 32, C), BF16),
        pltpu.VMEM((14, 32, C), BF16),
        pltpu.VMEM((7, 16, 1024), BF16),
        pltpu.VMEM((NG, NI + 1, 104, 128), F32),
        pltpu.VMEM((NG, NI + 1, ZR, 512), BF16),
        pltpu.VMEM((NG, 1024, 256), BF16),
        pltpu.VMEM((1024, 1024), BF16),
        pltpu.VMEM((NI * ZR, 128), F32),
        pltpu.VMEM((NG, NI, 64, 128), kind),
        pltpu.VMEM((NI + 1, 64, 128), F32),
        pltpu.VMEM((CLAT, 128), F32),
    ]


def forward_conv(fields, land, w, bias):
    dma = pltpu.SemaphoreType.DMA
    return pl.pallas_call(
        conv_kernel,
        name="forward_conv",
        out_shape=jax.ShapeDtypeStruct((TILES, 64, C), F32),
        in_specs=hbm(1) + vmem(3),
        out_specs=vmem(1)[0],
        scratch_shapes=halo_scratch(F32) + [dma((8,)), dma((8,)), dma],
        compiler_params=pltpu.CompilerParams(collective_id=0, has_side_effects=True, vmem_limit_bytes=VMEM_LIMIT),
    )(fields, land, w, bias)


def normal_cdf(h, square):
    q = jnp.full(h.shape, ERF_COEFS[-1], F32)
    for coef in ERF_COEFS[-2::-1]:
        q = q * square + coef
    return 0.5 + 0.5 * jnp.tanh(h * q)


def mlp_kernel(tile_ids, conv, fields, upstream, land, gain, shift, w_in, b_in, w_out, b_out, scale,
               mixed, d_conv_out, shares, branch, d_conv, w_in_t, w_out_t, g_in, g_out, g_bin, sums, land_tr, own, load):
    slots = 4
    rows = slots * 64
    copy_in = pltpu.make_async_copy(fields, own, load)
    copy_in.start()
    land_tr[...] = jnp.zeros((CLAT, 128), F32)
    land_tr[:, 0:CLON] = land[...].astype(F32)
    w_in_t[...] = w_in[...].astype(F32).T.astype(BF16)
    w_out_t[...] = w_out[...].astype(F32).T.astype(BF16)
    branch[...] = jnp.zeros(branch.shape, F32)
    d_conv[...] = jnp.zeros(d_conv.shape, F32)
    for acc in (g_in, g_out, g_bin, sums):
        acc[...] = jnp.zeros(acc.shape, F32)
    gain_row, shift_row, scale_row = gain[...], shift[...], scale[...]

    def step(n, carry):
        ids = [tile_ids[slots * n + q] for q in range(slots)]
        tiles = [jnp.maximum(t, 0) for t in ids]
        conv_parts, up_parts, active_parts = [], [], []
        for q in range(slots):
            t = tiles[q]
            big, small = t // NJ, lax.rem(t, NJ)
            conv_parts.append(conv[t])
            pair = upstream[pl.ds(8 * big, 8), pl.ds(16 * (small // 2), 16), :].astype(F32)
            odd = lax.rem(small, 2) == 1
            up_parts.append(jnp.where(odd, pair[:, 8:16], pair[:, 0:8]).reshape(64, C))
            strip = pltpu.roll(land_tr[pl.ds(8 * small, 8), :], lax.rem(128 - 8 * big, 128), axis=1)
            live = jnp.where(ids[q] >= 0, 1.0, 0.0)
            strip = strip * live
            active_parts += [jnp.broadcast_to(strip[:, i : i + 1], (8, C)) for i in range(8)]
        conv_rows = jnp.concatenate(conv_parts, axis=0)
        up = jnp.concatenate(up_parts, axis=0)
        active = jnp.concatenate(active_parts, axis=0)
        center = conv_rows - jnp.mean(conv_rows, axis=-1, keepdims=True)
        inv_std = lax.rsqrt(jnp.mean(center * center, axis=-1, keepdims=True) + LN_EPSILON)
        normed = center * inv_std
        normed_b = (normed * gain_row + shift_row).astype(BF16)
        hidden = jnp.dot(normed_b, w_in[...], preferred_element_type=F32) + b_in[...]
        bounded = jnp.clip(hidden, -5.0, 5.0)
        square = bounded * bounded
        cdf = normal_cdf(bounded, square)
        activated = (hidden * cdf).astype(BF16)
        output = jnp.dot(activated, w_out[...], preferred_element_type=F32) + b_out[...]
        gate = active * scale_row
        branch_rows = gate * output
        d_out = gate * up
        d_out_b = d_out.astype(BF16)
        g_out[...] += lax.dot_general(d_out_b, activated, (((0,), (0,)), ((), ())), preferred_element_type=F32)
        pdf = jnp.exp(-0.5 * (hidden * hidden)) * (1.0 / math.sqrt(2.0 * math.pi))
        d_hidden = jnp.dot(d_out_b, w_out_t[...], preferred_element_type=F32) * (cdf + hidden * pdf)
        d_hidden_b = d_hidden.astype(BF16)
        g_in[...] += lax.dot_general(normed_b, d_hidden_b, (((0,), (0,)), ((), ())), preferred_element_type=F32)
        g_bin[...] += jnp.sum(d_hidden.reshape(rows // 8, 8, FF), axis=0)
        d_norm = jnp.dot(d_hidden_b, w_in_t[...], preferred_element_type=F32)
        d_scaled = d_norm * gain_row
        d_cells = inv_std * (
            d_scaled
            - jnp.mean(d_scaled, axis=-1, keepdims=True)
            - normed * jnp.mean(d_scaled * normed, axis=-1, keepdims=True)
        )
        for k, term in enumerate((d_cells, d_norm * normed, d_norm, d_out, active * output * up)):
            sums[k] += jnp.sum(term.reshape(rows // 8, 8, C), axis=0)
        for q in range(slots):

            @pl.when(ids[q] >= 0)
            def _(q=q):
                branch[tiles[q]] = branch_rows[64 * q : 64 * q + 64]
                d_conv[tiles[q]] = d_cells[64 * q : 64 * q + 64]

        return carry

    lax.fori_loop(0, TCAP // slots, step, 0)

    copy_in.wait()

    def mix(n, carry):
        for i in range(8):
            rows_i = jnp.concatenate([branch[n * NJ + t, 8 * i : 8 * i + 8] for t in range(NJ)], axis=0)
            mixed[8 * n + i] = (own[2 * n + i // 4, i % 4].astype(F32) + rows_i).astype(BF16)
            rows_i = jnp.concatenate([d_conv[n * NJ + t, 8 * i : 8 * i + 8] for t in range(NJ)], axis=0)
            d_conv_out[2 * n + i // 4, i % 4] = rows_i.astype(BF16)
        return carry

    lax.fori_loop(0, NI, mix, 0)
    bin_row = jnp.sum(g_bin[...], axis=0, keepdims=True)
    tail = jnp.concatenate([jnp.sum(sums[k], axis=0, keepdims=True) for k in range(5)], axis=0)
    for n in range(4):
        turned_in = g_in[:, 128 * n : 128 * n + 128].T
        turned_out = g_out[:, 128 * n : 128 * n + 128].T
        for m in range(4):
            q = 4 * n + m
            shares[q, 0:32] = turned_in[32 * m : 32 * m + 32]
            shares[q, 32:64] = turned_out[32 * m : 32 * m + 32]
            shares[q, 64:65] = bin_row[:, 128 * n : 128 * n + 128]
            shares[q, 65:70] = tail
            shares[q, 70:72] = jnp.zeros((2, 128), F32)


def listed_mlp(tile_ids, conv, fields, upstream, land, gain, shift, w_in, b_in, w_out, b_out, scale):
    return pl.pallas_call(
        mlp_kernel,
        name="listed_mlp",
        out_shape=(
            jax.ShapeDtypeStruct((CLON, CLAT, C), BF16),
            jax.ShapeDtypeStruct((24, 4, CLAT, C), BF16),
            jax.ShapeDtypeStruct((N_LAT, 72, 128), F32),
        ),
        in_specs=[pl.BlockSpec(memory_space=pltpu.SMEM)] + vmem(1) + hbm(1) + vmem(9),
        out_specs=tuple(vmem(3)),
        scratch_shapes=[
            pltpu.VMEM((TILES, 64, C), F32),
            pltpu.VMEM((TILES, 64, C), F32),
            pltpu.VMEM((FF, C), BF16),
            pltpu.VMEM((C, FF), BF16),
            pltpu.VMEM((C, FF), F32),
            pltpu.VMEM((C, FF), F32),
            pltpu.VMEM((8, FF), F32),
            pltpu.VMEM((5, 8, C), F32),
            pltpu.VMEM((CLAT, 128), F32),
            pltpu.VMEM((24, 4, CLAT, C), BF16),
            pltpu.SemaphoreType.DMA,
        ],
        compiler_params=pltpu.CompilerParams(vmem_limit_bytes=VMEM_LIMIT),
    )(tile_ids, conv, fields, upstream, land, gain, shift, w_in, b_in, w_out, b_out, scale)


def pair_masked(PS, MP):
    def block(n, carry):
        for g in range(NG):
            MP[g, n, :, 0:128] = PS[g, n, 16 : 16 + ZR].astype(BF16)
            MP[g, n, :, 128:256] = PS[g, n, 15 : 15 + ZR].astype(BF16)
        return carry

    lax.fori_loop(0, NI, block, 0)


def tap_gradients(Z, MP, G, taps):
    lane = iota((16, 128), 1)
    same = (iota((16, 128), 0) == lane % 16).astype(F32)
    block = lane // 16
    taps[...] = jnp.zeros(taps.shape, F32)

    def group(g, carry):
        lhs = MP[g].reshape(NI * ZR, 256)
        for half in range(2):
            rhs = Z[g, half : half + NI].reshape(NI * ZR, 512)
            G[half] = lax.dot_general(lhs, rhs, (((0,), (0,)), ((), ())), preferred_element_type=F32)
        for e in range(4):
            for parity in range(2):
                b = 3 - SHIFTS[e] - parity
                if not 0 <= b < 7:
                    continue
                for a in range(7):
                    total = None
                    for i_out in range(8):
                        half, k = divmod(i_out + 7 - a, 8)
                        at = 128 * parity + 16 * i_out
                        piece = G[half, at : at + 16, 128 * e : 128 * e + 128]
                        total = piece if total is None else jnp.where(block == k, piece, total)
                    taps[g, 7 * a + b : 7 * a + b + 1] = jnp.sum(total * same, axis=0, keepdims=True)
        return carry

    lax.fori_loop(0, NG, group, 0)


def gather_taps(taps, square, tap_shares):
    total = jnp.zeros((56, 128), F32)
    for g in range(NG):
        row, col = iota((128, 128), 0), iota((128, 128), 1)
        pick = jnp.where((col // 16 == g) & (row % 16 == col % 16), 1.0, 0.0).astype(BF16)
        value = taps[g]
        head = value.astype(BF16)
        tail = (value - head.astype(F32)).astype(BF16)
        total += jnp.dot(head, pick, preferred_element_type=F32) + jnp.dot(tail, pick, preferred_element_type=F32)
    square[...] = jnp.zeros((128, 128), F32)
    square[0:56] = total
    turned = square[...].T
    for q in range(N_LAT):
        tap_shares[q] = turned[8 * q : 8 * q + 8]


def grad_kernel(d_conv, fields, upstream, land, w, shares,
                grad_input, out_win, out_wout, out_dw, out_channel, out_bin,
                X, EL, ER, LH, RH, EH, PS, Z, W, PM, AB, S, M, land_pad,
                own, up, MP, G, taps, square, tap_shares, parts, tap_parts, mine, whole,
                send, recv, send_one, recv_one, send_tap, recv_tap, send_two, recv_two, load):
    lon, lat = lax.axis_index("lon"), lax.axis_index("lat")
    around = neighbours(lon, lat)
    around += [(lon, lax.rem(lat + d, N_LAT)) for d in range(2, N_LAT - 1)]
    around += [(lax.rem(lon + d, N_LON), lat) for d in range(2, N_LON - 1)]
    greet(around)
    copy_in = pltpu.make_async_copy(d_conv, X.at[pl.ds(1, 24)], load.at[0])
    copy_own = pltpu.make_async_copy(fields, own, load.at[1])
    copy_up = pltpu.make_async_copy(upstream, up, load.at[2])
    copy_in.start()
    copy_own.start()
    copy_up.start()
    copy_in.wait()
    pack_edges(X, EL, ER, None)
    greeted(around)
    copies = halo_copies(X, EL, ER, LH, RH, send, recv, lon, lat)
    for copy in copies:
        copy.start()
    share_copies, tap_copies = [], []
    for d in range(1, N_LAT):
        to = lax.rem(lat + d, N_LAT)
        share_copies.append(pltpu.make_async_remote_copy(
            src_ref=shares.at[to], dst_ref=parts.at[d], send_sem=send_one.at[d], recv_sem=recv_one.at[d],
            device_id=(lon, to), device_id_type=MESH))
        tap_copies.append(pltpu.make_async_remote_copy(
            src_ref=tap_shares.at[to], dst_ref=tap_parts.at[d], send_sem=send_tap.at[d], recv_sem=recv_tap.at[d],
            device_id=(lon, to), device_id_type=MESH))
    for copy in share_copies:
        copy.start()
    build_permutation(PM)
    clear_margins(PS)
    land_pad[...] = jnp.zeros((CLAT, 128), F32)
    land_pad[:, 0:CLON] = land[...].astype(F32)
    expand_mask(land_pad[...], M, NI)
    copy_own.wait()
    for blocks in ((0, 1, 2, 3), (4, 5, 6, 7), (8, 9, 10, 11)):
        group_blocks(lambda k, i: own[2 * k + i // 4, i % 4], blocks, PM, PS, M)
    pair_masked(PS, MP)
    build_weights(w, W, True)

    def cells(k, i):
        return X[2 * k + i // 4, i % 4]

    for blocks in INNER:
        group_blocks(cells, blocks, PM, PS, None)
    for copy in copies:
        copy.wait()
    group_blocks(cells, (0, NI), PM, PS, None)
    group_halos(LH, RH, EH, PM, PS, lat)
    shift_blocks(PS, Z)
    tap_gradients(Z, MP, G, taps)
    gather_taps(taps, square, tap_shares)
    for copy in tap_copies:
        copy.start()
    banded_conv(Z, W, AB, S, M)
    for copy in share_copies:
        copy.wait()
    for copy in tap_copies:
        copy.wait()
    total = shares[lat]
    tap_total = tap_shares[lat]
    for d in range(1, N_LAT):
        total += parts[d]
        tap_total += tap_parts[d]
    mine[0:72] = total * GRAD_SCALE
    mine[72:80] = tap_total * GRAD_SCALE
    last_copies = [
        pltpu.make_async_remote_copy(
            src_ref=mine, dst_ref=whole.at[d], send_sem=send_two.at[d], recv_sem=recv_two.at[d],
            device_id=(lax.rem(lon + d, N_LON), lat), device_id_type=MESH)
        for d in range(1, N_LON)
    ]
    for copy in last_copies:
        copy.start()
    copy_up.wait()
    for first in range(0, NI, 4):
        rows = [S[g, first : first + 4].reshape(256, 128) for g in range(NG)]
        lhs = jnp.concatenate(rows, axis=1)

        def back(n, carry, lhs=lhs, first=first):
            both = jnp.dot(lhs, PM[:, pl.ds(pl.multiple_of(256 * n, 256), 256)], preferred_element_type=F32)
            for h in range(2):
                for m in range(4):
                    at = 8 * (first + m) + 2 * n + h
                    value = up[at].astype(F32) + both[64 * m : 64 * m + 64, 128 * h : 128 * h + 128]
                    grad_input[at] = value.astype(BF16)
            return carry

        lax.fori_loop(0, 4, back, 0)
    for copy in last_copies:
        copy.wait()
    total = mine[...]
    for d in range(1, N_LON):
        total += whole[d]
    out_win[...] = total[0:32]
    out_wout[...] = total[32:64]
    small = total[64:72]
    out_bin[...] = pltpu.roll(small, lax.rem(128 - 32 * lax.rem(lat, 4), 128), axis=1)[0:1, 0:32]
    out_channel[...] = pltpu.roll(small, lax.rem(128 - 8 * lat, 128), axis=1)[1:6, 0:8]
    out_dw[...] = total[72:80, 0:49]


def backward_conv(d_conv, fields, upstream, land, w, shares):
    dma = pltpu.SemaphoreType.DMA
    return pl.pallas_call(
        grad_kernel,
        name="backward_conv",
        out_shape=(
            jax.ShapeDtypeStruct((CLON, CLAT, C), BF16),
            jax.ShapeDtypeStruct((32, C), F32),
            jax.ShapeDtypeStruct((32, C), F32),
            jax.ShapeDtypeStruct((8, 49), F32),
            jax.ShapeDtypeStruct((5, 8), F32),
            jax.ShapeDtypeStruct((1, 32), F32),
        ),
        in_specs=hbm(3) + vmem(3),
        out_specs=tuple(vmem(6)),
        scratch_shapes=halo_scratch(BF16)
        + [
            pltpu.VMEM((24, 4, CLAT, C), BF16),
            pltpu.VMEM((CLON, CLAT, C), BF16),
            pltpu.VMEM((NG, NI, ZR, 256), BF16),
            pltpu.VMEM((2, 256, 512), F32),
            pltpu.VMEM((NG, 56, 128), F32),
            pltpu.VMEM((128, 128), F32),
            pltpu.VMEM((N_LAT, 8, 128), F32),
            pltpu.VMEM((N_LAT, 72, 128), F32),
            pltpu.VMEM((N_LAT, 8, 128), F32),
            pltpu.VMEM((80, 128), F32),
            pltpu.VMEM((N_LON, 80, 128), F32),
            dma((8,)), dma((8,)), dma((N_LAT,)), dma((N_LAT,)), dma((N_LAT,)), dma((N_LAT,)), dma((N_LON,)), dma((N_LON,)), dma((3,)),
        ],
        compiler_params=pltpu.CompilerParams(collective_id=1, has_side_effects=True, vmem_limit_bytes=VMEM_LIMIT),
    )(d_conv, fields, upstream, land, w, shares)


def per_device(fields, land_sea, tile_list, upstream, dw_weight, dw_bias, ln_gain, ln_bias, w_in, b_in, w_out, b_out,
               layer_scale):
    def row(v):
        return v.reshape(1, -1)

    fours = fields.reshape(24, 4, CLAT, C)
    land = land_sea.T
    conv = forward_conv(fours, land, dw_weight, row(dw_bias))
    mixed, d_conv, shares = listed_mlp(
        tile_list.reshape(-1), conv, fours, upstream, land, row(ln_gain), row(ln_bias), w_in, row(b_in), w_out,
        row(b_out), row(layer_scale))
    grad_input, g_win, g_wout, g_dw, g_channel, g_bin = backward_conv(d_conv, fours, upstream, land, dw_weight, shares)
    return mixed, grad_input, g_win.T, g_wout, g_dw.T, g_channel, g_bin.reshape(-1)


def solution(mesh):
    cells = P("lon", "lat", None)
    return jax.shard_map(
        per_device,
        mesh=mesh,
        in_specs=(cells, P("lon", "lat"), cells, cells) + (P(),) * 9,
        out_specs=(cells, cells, P(None, "lat"), P("lat", None), P(None, "lat"), P(None, "lat"), P("lat")),
        check_vma=False,
    )
```

```python
import functools
import math

import jax
import jax.numpy as jnp
from jax import lax
from jax.experimental import pallas as pl
from jax.experimental.pallas import tpu as pltpu
from jax.sharding import PartitionSpec as P

LN_EPSILON = 1e-06
MESH = pl.DeviceIdType.MESH
F32 = jnp.float32
BF16 = jnp.bfloat16
CLON, CLAT, C, FF = 96, 64, 128, 512
NI, NJ = CLON // 8, CLAT // 8
TILES = NI * NJ
TCAP = 72
NG = 8
ZR = 80
N_LON, N_LAT = 8, 16
SHIFTS = (-4, -2, 0, 2)
GRAD_SCALE = 1.0 / math.sqrt(768 * 1024)
VMEM_LIMIT = 50 * 1024 * 1024
ERF_COEFS = (0.7978822019328625, 0.03634471964933557, -4.4922105999092954e-05,
             -5.0349129465290195e-05, 3.0967343000773035e-06, -6.63025075261232e-08)


def iota(shape, dim):
    return lax.broadcasted_iota(jnp.int32, shape, dim)


def build_weights(w_ref, W, flip):
    q_row, q_col = iota((56, 49), 0), iota((56, 49), 1)
    a, b = q_row // 8, q_row % 8
    tap = (6 - a) * 7 + (6 - b) if flip else a * 7 + b
    pick = jnp.where((q_col == tap) & (b < 7), 1.0, 0.0).astype(BF16)
    taps = jnp.dot(pick, w_ref[...].astype(BF16), preferred_element_type=F32).astype(BF16)
    lane_i = iota((8, 128), 1) // 16
    same = (iota((16, 128), 0) == iota((16, 128), 1) % 16).astype(F32)

    def group(g):
        spread = jnp.where(iota((128, 128), 0) == 16 * g + iota((128, 128), 1) % 16, 1.0, 0.0).astype(BF16)
        rep = jnp.dot(taps, spread, preferred_element_type=F32)
        for i_in in range(16):
            v = jnp.zeros((8, 128), F32)
            for a in range(7):
                if 0 <= i_in - 1 - a < 8:
                    v = jnp.where(lane_i == i_in - 1 - a, rep[8 * a : 8 * a + 8], v)
            base = (i_in // 8) * 512 + (i_in % 8) * 16
            W[g, base : base + 16, 0:128] = jnp.zeros((16, 128), BF16)
            for b in range(7):
                parity = (b + 1) % 2
                e = (b - 3 - parity + 4) // 2
                row = jnp.broadcast_to(v[b : b + 1], (16, 128)) * same
                W[g, base + 128 * e : base + 128 * e + 16, 128 * parity : 128 * parity + 128] = row.astype(BF16)

    for g in range(NG):
        group(g)


def build_permutation(PM):
    def clear(n, carry):
        PM[pl.ds(pl.multiple_of(64 * n, 64), 64), :] = jnp.zeros((64, 1024), BF16)
        return carry

    lax.fori_loop(0, 16, clear, 0)
    row, lane = iota((16, 128), 0), iota((16, 128), 1)
    for p in range(8):
        unit = jnp.where(lane == 16 * p + row, 1.0, 0.0).astype(BF16)
        for q in range(8):
            PM[128 * p + 16 * q : 128 * p + 16 * q + 16, 128 * q : 128 * q + 128] = unit


def expand_mask(land_ext, M, count):
    value = land_ext.astype(BF16)
    row, block = iota((128, 128), 0), iota((128, 128), 1) // 16

    for k in range(count):
        pick = jnp.where(row == 8 * k + block, 1.0, 0.0).astype(BF16)
        M[k] = jnp.dot(value, pick, preferred_element_type=F32)


def with_ones(land_t):
    lane = iota((CLAT, 128), 1)
    return jnp.where((lane < 4) | (lane >= CLON + 4), 1.0, pltpu.roll(land_t, 4, axis=1))


def pack_edges(X, EL, ER, masks):
    low = iota((8, 128), 0) < 4

    def block(n, carry):
        for east, E in ((0, EL), (1, ER)):
            out = []
            keep = None if masks is None else pltpu.roll(masks[east], lax.rem(128 - 8 * n, 128), axis=1)
            for m in range(4):
                pair = []
                for i in (2 * m, 2 * m + 1):
                    cells = X[1 + 2 * n + i // 4, i % 4, 48 * east : 48 * east + 16].astype(F32)
                    pair.append(cells[8 * east : 8 * east + 8])
                if east:
                    value = jnp.where(low, pltpu.roll(pair[0], 4, axis=0), pair[1])
                else:
                    value = jnp.where(low, pair[0], pltpu.roll(pair[1], 4, axis=0))
                if keep is not None:
                    value = value * jnp.broadcast_to(keep[:, 2 * m : 2 * m + 1], (8, 128))
                out.append(value)
            E[n] = jnp.concatenate(out, axis=0).astype(BF16)
        return carry

    lax.fori_loop(0, NI, block, 0)


def halo_copies(X, EL, ER, LH, RH, send, recv, lon, lat):
    up, down = lax.rem(lon + 1, N_LON), lax.rem(lon + N_LON - 1, N_LON)
    east, west = lax.rem(lat + 1, N_LAT), lax.rem(lat + N_LAT - 1, N_LAT)
    plan = (
        (EL, RH.at[pl.ds(1, NI)], (lon, west)),
        (ER, LH.at[pl.ds(1, NI)], (lon, east)),
        (X.at[1], X.at[25], (down, lat)),
        (X.at[24], X.at[0], (up, lat)),
        (EL.at[0, pl.ds(0, 16)], RH.at[13, pl.ds(0, 16)], (down, west)),
        (EL.at[NI - 1, pl.ds(16, 16)], RH.at[0, pl.ds(16, 16)], (up, west)),
        (ER.at[0, pl.ds(0, 16)], LH.at[13, pl.ds(0, 16)], (down, east)),
        (ER.at[NI - 1, pl.ds(16, 16)], LH.at[0, pl.ds(16, 16)], (up, east)),
    )
    return [
        pltpu.make_async_remote_copy(
            src_ref=src, dst_ref=dst, send_sem=send.at[n], recv_sem=recv.at[n], device_id=where, device_id_type=MESH
        )
        for n, (src, dst, where) in enumerate(plan)
    ]


def neighbours(lon, lat):
    up, down = lax.rem(lon + 1, N_LON), lax.rem(lon + N_LON - 1, N_LON)
    east, west = lax.rem(lat + 1, N_LAT), lax.rem(lat + N_LAT - 1, N_LAT)
    return [(lon, west), (lon, east), (down, lat), (up, lat), (down, west), (up, west), (down, east), (up, east)]


def greet(places):
    barrier = pltpu.get_barrier_semaphore()
    for place in places:
        pl.semaphore_signal(barrier, inc=1, device_id=place, device_id_type=MESH)


def greeted(places):
    pl.semaphore_wait(pltpu.get_barrier_semaphore(), len(places))


def clear_margins(PS):
    def block(k, carry):
        PS[:, k, 8:16] = jnp.zeros((NG, 8, 128), F32)
        PS[:, k, 80:104] = jnp.zeros((NG, 24, 128), F32)
        return carry

    lax.fori_loop(0, NI + 1, block, 0)


def group_blocks(cells, blocks, PM, PS, M):
    lhs = jnp.concatenate([jnp.concatenate([cells(k, i) for k in blocks], axis=0) for i in range(8)], axis=1)

    for n in range(NG // 2):
        both = jnp.dot(lhs, PM[:, 256 * n : 256 * n + 256], preferred_element_type=F32)
        for h in range(2):
            for m, k in enumerate(blocks):
                part = both[64 * m : 64 * m + 64, 128 * h : 128 * h + 128]
                PS[2 * n + h, k, 16:80] = part if M is None else part * M[k]


def group_halos(LH, RH, EH, PM, PS, lat):
    low = iota((8, 128), 0) < 4
    keep = jnp.where(low, jnp.where(lat < N_LAT - 1, 1.0, 0.0), jnp.where(lat > 0, 1.0, 0.0))

    def rows_of(k):
        rows = []
        for m in range(4):
            at = (16, 24, 0, 8)[m]
            left = LH[k + m // 2, at // 16 * 16 : at // 16 * 16 + 16].astype(F32)[at % 16 : at % 16 + 8]
            right = RH[k + m // 2, at // 16 * 16 : at // 16 * 16 + 16].astype(F32)[at % 16 : at % 16 + 8]
            rows.append(jnp.where(low, right, pltpu.roll(left, 4, axis=0)) * keep)
            rows.append(jnp.where(low, pltpu.roll(right, 4, axis=0), left) * keep)
        return rows

    for n in range(7):
        first = rows_of(2 * n)
        second = rows_of(2 * n + 1) if 2 * n + 1 <= NI else first
        for i in range(8):
            EH[n, :, 128 * i : 128 * i + 128] = jnp.concatenate([first[i], second[i]], axis=0).astype(BF16)

    edges = EH[...].reshape(112, 1024)
    for n in range(NG // 2):
        both = jnp.dot(edges, PM[:, 256 * n : 256 * n + 256], preferred_element_type=F32)
        for h in range(2):
            for k in range(NI + 1):
                part = both[8 * k : 8 * k + 8, 128 * h : 128 * h + 128]
                PS[2 * n + h, k, 8:16] = part
                PS[2 * n + h, k, 80:88] = part


def shift_blocks(PS, Z, g):
    for k in range(NI + 1):
        for e, shift in enumerate(SHIFTS):
            Z[g, k, :, 128 * e : 128 * e + 128] = PS[g, k, 16 + shift : 16 + shift + ZR].astype(BF16)


INNER = ((1, 2, 3, 4), (5, 6, 7, 8), (9, 10, 11))


def banded_conv(Z, W, AB, S, M, g):
    lhs = jnp.concatenate([Z[g, 0:NI].reshape(NI * ZR, 512), Z[g, 1 : NI + 1].reshape(NI * ZR, 512)], axis=1)
    both = jnp.dot(lhs, W[g], preferred_element_type=F32)
    AB[g % 2] = both[:, 128:256]
    for n in range(NI):
        value = both[n * ZR : n * ZR + 64, 0:128] + AB[g % 2, n * ZR + 1 : n * ZR + 65]
        S[g, n] = (value if M is None else value * M[n]).astype(BF16)


def ungroup(S, PM, blocks, put):
    rows = [jnp.concatenate([S[g, k] for k in blocks], axis=0) for g in range(NG)]
    lhs = jnp.concatenate(rows, axis=1)
    for n in range(NG // 2):
        put(n, jnp.dot(lhs, PM[:, 256 * n : 256 * n + 256], preferred_element_type=F32))


def conv_kernel(fields, land, w, conv_out, lon_halo, left_halo, right_halo, X, EL, ER, LH, RH, EH, PS, Z, W, PM, AB, S, M, land_pad, send, recv,
                load):
    lon, lat = lax.axis_index("lon"), lax.axis_index("lat")
    around = neighbours(lon, lat)
    greet(around)
    copy_in = pltpu.make_async_copy(fields, X.at[pl.ds(1, 24)], load)
    copy_in.start()
    land_pad[...] = jnp.zeros((CLAT, 128), F32)
    land_pad[:, 0:CLON] = land[...].astype(F32)
    land_t = land_pad[...]
    expand_mask(with_ones(land_t), M, NI + 1)
    low = iota((8, 128), 0) < 4
    masks = []
    for east in range(2):
        edge = land_pad[56 * east : 56 * east + 8]
        turned = pltpu.roll(edge, 4, axis=0)
        edge = jnp.where(low, turned, edge) if east else jnp.where(low, edge, turned)
        masks.append(jnp.where(low, edge, pltpu.roll(edge, 127, axis=1)))
    copy_in.wait()
    pack_edges(X, EL, ER, masks)
    for at, first in ((1, 0), (24, CLON - 4)):
        for i in range(4):
            keep = jnp.broadcast_to(land_t[:, first + i : first + i + 1], (CLAT, C))
            X[at, i] = (X[at, i].astype(F32) * keep).astype(BF16)
    greeted(around)
    copies = halo_copies(X, EL, ER, LH, RH, send, recv, lon, lat)
    for copy in copies:
        copy.start()
    build_permutation(PM)
    clear_margins(PS)

    def cells(k, i):
        return X[2 * k + i // 4, i % 4]

    for blocks in INNER:
        group_blocks(cells, blocks, PM, PS, M)
    build_weights(w, W, False)
    for copy in copies:
        copy.wait()
    lon_halo[0] = X[0]
    lon_halo[1] = X[25]
    left_halo[...] = LH[...]
    right_halo[...] = RH[...]
    group_blocks(cells, (0, NI), PM, PS, M)
    group_halos(LH, RH, EH, PM, PS, lat)
    for g in range(NG):
        shift_blocks(PS, Z, g)
        banded_conv(Z, W, AB, S, None, g)
    for first in range(0, NI, 4):

        def put(n, both, first=first):
            for m in range(4):
                for t in range(NJ):
                    at = 64 * m + 8 * t
                    value = jnp.concatenate([both[at : at + 8, 0:128], both[at : at + 8, 128:256]], axis=0)
                    conv_out[(first + m) * NJ + t, 16 * n : 16 * n + 16] = value.astype(BF16)

        ungroup(S, PM, range(first, first + 4), put)


def vmem(n):
    return [pl.BlockSpec(memory_space=pltpu.VMEM)] * n


def hbm(n):
    return [pl.BlockSpec(memory_space=pl.ANY)] * n


def halo_scratch():
    return [
        pltpu.VMEM((26, 4, CLAT, C), BF16),
        pltpu.VMEM((NI, 32, C), BF16),
        pltpu.VMEM((NI, 32, C), BF16),
        pltpu.VMEM((14, 32, C), BF16),
        pltpu.VMEM((14, 32, C), BF16),
        pltpu.VMEM((7, 16, 1024), BF16),
        pltpu.VMEM((NG, NI + 1, 104, 128), F32),
        pltpu.VMEM((NG, NI + 1, ZR, 512), BF16),
        pltpu.VMEM((NG, 1024, 256), BF16),
        pltpu.VMEM((1024, 1024), BF16),
        pltpu.VMEM((2, NI * ZR, 128), F32),
        pltpu.VMEM((NG, NI, 64, 128), BF16),
        pltpu.VMEM((NI + 1, 64, 128), F32),
        pltpu.VMEM((CLAT, 128), F32),
    ]


def forward_conv(fields, land, w):
    dma = pltpu.SemaphoreType.DMA
    return pl.pallas_call(
        conv_kernel,
        name="forward_conv",
        out_shape=(
            pltpu.VMEM((TILES, 64, C), BF16),
            pltpu.VMEM((2, 4, CLAT, C), BF16),
            pltpu.VMEM((14, 32, C), BF16),
            pltpu.VMEM((14, 32, C), BF16),
        ),
        in_specs=hbm(1) + vmem(2),
        out_specs=tuple(vmem(4)),
        scratch_shapes=halo_scratch() + [dma((8,)), dma((8,)), dma],
        compiler_params=pltpu.CompilerParams(collective_id=0, has_side_effects=True, vmem_limit_bytes=VMEM_LIMIT),
    )(fields, land, w)


def normal_cdf(h, square):
    q = jnp.full(h.shape, ERF_COEFS[-1], F32)
    for coef in ERF_COEFS[-2::-1]:
        q = q * square + coef
    return 0.5 + 0.5 * jnp.tanh(h * q)


def mlp_kernel(tile_ids, conv, fields, upstream, land, offset, gain, shift, w_in, b_in, w_out, b_out, scale,
               mixed, d_conv_out, shares, branch, d_conv, w_in_t, w_out_t, g_in, g_out, g_bin, sums, land_tr, own, load):
    slots = 18
    rows = slots * 64
    copy_in = pltpu.make_async_copy(fields, own, load)
    copy_in.start()
    land_tr[...] = jnp.zeros((CLAT, 128), F32)
    land_tr[:, 0:CLON] = land[...].astype(F32)
    w_in_t[...] = w_in[...].astype(F32).T.astype(BF16)
    w_out_t[...] = w_out[...].astype(F32).T.astype(BF16)
    branch[...] = jnp.zeros(branch.shape, F32)
    d_conv[...] = jnp.zeros(d_conv.shape, F32)
    for acc in (g_in, g_out, g_bin, sums):
        acc[...] = jnp.zeros(acc.shape, F32)
    gain_row, shift_row, scale_row = gain[...], shift[...], scale[...]

    def step(n, carry):
        ids = [tile_ids[slots * n + q] for q in range(slots)]
        tiles = [jnp.maximum(t, 0) for t in ids]
        conv_parts, up_parts, active_parts = [], [], []
        for q in range(slots):
            t = tiles[q]
            big, small = t // NJ, lax.rem(t, NJ)
            conv_parts.append(conv[t].astype(F32))
            pair = upstream[pl.ds(8 * big, 8), pl.ds(16 * (small // 2), 16), :].astype(F32)
            odd = lax.rem(small, 2) == 1
            up_parts.append(jnp.where(odd, pair[:, 8:16], pair[:, 0:8]).reshape(64, C))
            strip = pltpu.roll(land_tr[pl.ds(8 * small, 8), :], lax.rem(128 - 8 * big, 128), axis=1)
            live = jnp.where(ids[q] >= 0, 1.0, 0.0)
            strip = strip * live
            active_parts += [jnp.broadcast_to(strip[:, i : i + 1], (8, C)) for i in range(8)]
        conv_rows = jnp.concatenate(conv_parts, axis=0) + offset[...]
        up = jnp.concatenate(up_parts, axis=0)
        active = jnp.concatenate(active_parts, axis=0)
        center = conv_rows - jnp.mean(conv_rows, axis=-1, keepdims=True)
        inv_std = lax.rsqrt(jnp.mean(center * center, axis=-1, keepdims=True) + LN_EPSILON)
        normed = center * inv_std
        normed_b = (normed * gain_row + shift_row).astype(BF16)
        hidden = jnp.dot(normed_b, w_in[...], preferred_element_type=F32) + b_in[...]
        bounded = jnp.clip(hidden, -5.0, 5.0)
        square = bounded * bounded
        cdf = normal_cdf(bounded, square)
        activated = (hidden * cdf).astype(BF16)
        output = jnp.dot(activated, w_out[...], preferred_element_type=F32) + b_out[...]
        gate = active * scale_row
        branch_rows = gate * output
        d_out = gate * up
        d_out_b = d_out.astype(BF16)
        g_out[...] += lax.dot_general(d_out_b, activated, (((0,), (0,)), ((), ())), preferred_element_type=F32)
        pdf = jnp.exp(-0.5 * (hidden * hidden)) * (1.0 / math.sqrt(2.0 * math.pi))
        d_hidden = jnp.dot(d_out_b, w_out_t[...], preferred_element_type=F32) * (cdf + hidden * pdf)
        d_hidden_b = d_hidden.astype(BF16)
        g_in[...] += lax.dot_general(normed_b, d_hidden_b, (((0,), (0,)), ((), ())), preferred_element_type=F32)
        g_bin[...] += jnp.sum(d_hidden.reshape(rows // 8, 8, FF), axis=0)
        d_norm = jnp.dot(d_hidden_b, w_in_t[...], preferred_element_type=F32)
        d_scaled = d_norm * gain_row
        d_cells = inv_std * (
            d_scaled
            - jnp.mean(d_scaled, axis=-1, keepdims=True)
            - normed * jnp.mean(d_scaled * normed, axis=-1, keepdims=True)
        )
        for k, term in enumerate((d_cells, d_norm * normed, d_norm, d_out, active * output * up)):
            sums[k] += jnp.sum(term.reshape(rows // 8, 8, C), axis=0)
        for q in range(slots):

            @pl.when(ids[q] >= 0)
            def _(q=q):
                branch[tiles[q]] = branch_rows[64 * q : 64 * q + 64]
                d_conv[tiles[q]] = d_cells[64 * q : 64 * q + 64]

        return carry

    lax.fori_loop(0, TCAP // slots, step, 0)

    copy_in.wait()

    def mix(n, carry):
        for i in range(8):
            rows_i = jnp.concatenate([branch[n * NJ + t, 8 * i : 8 * i + 8] for t in range(NJ)], axis=0)
            mixed[8 * n + i] = (own[2 * n + i // 4, i % 4].astype(F32) + rows_i).astype(BF16)
            rows_i = jnp.concatenate([d_conv[n * NJ + t, 8 * i : 8 * i + 8] for t in range(NJ)], axis=0)
            d_conv_out[2 * n + i // 4, i % 4] = rows_i.astype(BF16)
        return carry

    lax.fori_loop(0, NI, mix, 0)
    bin_row = jnp.sum(g_bin[...], axis=0, keepdims=True)
    tail = jnp.concatenate([jnp.sum(sums[k], axis=0, keepdims=True) for k in range(5)], axis=0)
    for n in range(4):
        turned_in = g_in[:, 128 * n : 128 * n + 128].T
        turned_out = g_out[:, 128 * n : 128 * n + 128].T
        for m in range(4):
            q = 4 * n + m
            shares[q, 0:32] = turned_in[32 * m : 32 * m + 32].astype(BF16)
            shares[q, 32:64] = turned_out[32 * m : 32 * m + 32].astype(BF16)
            rest = [bin_row[:, 128 * n : 128 * n + 128], tail, jnp.zeros((10, 128), F32)]
            shares[q, 64:80] = jnp.concatenate(rest, axis=0).astype(BF16)


def listed_mlp(tile_ids, conv, fields, upstream, land, offset, gain, shift, w_in, b_in, w_out, b_out, scale):
    return pl.pallas_call(
        mlp_kernel,
        name="listed_mlp",
        out_shape=(
            jax.ShapeDtypeStruct((CLON, CLAT, C), BF16),
            pltpu.VMEM((24, 4, CLAT, C), BF16),
            pltpu.VMEM((N_LAT, 80, 128), BF16),
        ),
        in_specs=[pl.BlockSpec(memory_space=pltpu.SMEM)] + vmem(1) + hbm(1) + vmem(10),
        out_specs=tuple(vmem(3)),
        scratch_shapes=[
            pltpu.VMEM((TILES, 64, C), F32),
            pltpu.VMEM((TILES, 64, C), F32),
            pltpu.VMEM((FF, C), BF16),
            pltpu.VMEM((C, FF), BF16),
            pltpu.VMEM((C, FF), F32),
            pltpu.VMEM((C, FF), F32),
            pltpu.VMEM((8, FF), F32),
            pltpu.VMEM((5, 8, C), F32),
            pltpu.VMEM((CLAT, 128), F32),
            pltpu.VMEM((24, 4, CLAT, C), BF16),
            pltpu.SemaphoreType.DMA,
        ],
        compiler_params=pltpu.CompilerParams(vmem_limit_bytes=VMEM_LIMIT),
    )(tile_ids, conv, fields, upstream, land, offset, gain, shift, w_in, b_in, w_out, b_out, scale)


def pair_rows(PS, MP):
    for g in range(NG):
        for n in range(NI):
            MP[g, n, :, 0:128] = PS[g, n, 16 : 16 + ZR].astype(BF16)
            MP[g, n, :, 128:256] = PS[g, n, 15 : 15 + ZR].astype(BF16)


def tap_gradients(Z, MP, G, taps, groups):
    lane = iota((16, 128), 1)
    same = (iota((16, 128), 0) == lane % 16).astype(F32)
    block = lane // 16
    for g in groups:
        taps[g] = jnp.zeros(taps.shape[1:], F32)
        lhs = MP[g].reshape(NI * ZR, 256)
        for half in range(2):
            rhs = Z[g, half : half + NI].reshape(NI * ZR, 512)
            G[g % 2, half] = lax.dot_general(lhs, rhs, (((0,), (0,)), ((), ())), preferred_element_type=F32)
        for e in range(4):
            for parity in range(2):
                b = 3 + SHIFTS[e] + parity
                if not 0 <= b < 7:
                    continue
                for a in range(7):
                    total = None
                    for i_out in range(8):
                        half, k = divmod(i_out + a + 1, 8)
                        at = 128 * parity + 16 * i_out
                        piece = G[g % 2, half, at : at + 16, 128 * e : 128 * e + 128]
                        total = piece if total is None else jnp.where(block == k, piece, total)
                    taps[g, 7 * a + b : 7 * a + b + 1] = jnp.sum(total * same, axis=0, keepdims=True)


def gather_taps(taps, square, tap_shares):
    total = jnp.zeros((56, 128), F32)
    for g in range(NG):
        row, col = iota((128, 128), 0), iota((128, 128), 1)
        pick = jnp.where((col // 16 == g) & (row % 16 == col % 16), 1.0, 0.0).astype(BF16)
        value = taps[g]
        head = value.astype(BF16)
        tail = (value - head.astype(F32)).astype(BF16)
        total += jnp.dot(head, pick, preferred_element_type=F32) + jnp.dot(tail, pick, preferred_element_type=F32)
    square[...] = jnp.zeros((128, 128), F32)
    square[0:56] = total
    turned = square[...].T
    for q in range(N_LAT):
        tap_shares[q] = turned[8 * q : 8 * q + 8]


def grad_kernel(d_conv, fields, lon_halo, left_halo, right_halo, land, w, shares,
                S, total_out,
                X, EL, ER, LH, RH, EH, PS, Z, W, PM, AB, M, land_pad,
                own, MP, G, taps, square, tap_shares, parts, tap_parts, mine, whole, tap_mine, tap_whole,
                send, recv, send_one, recv_one, send_tap, recv_tap, send_two, recv_two, send_last, recv_last, load):
    lon, lat = lax.axis_index("lon"), lax.axis_index("lat")
    around = neighbours(lon, lat)
    around += [(lon, lax.rem(lat + d, N_LAT)) for d in range(2, N_LAT - 1)]
    around += [(lax.rem(lon + d, N_LON), lat) for d in range(2, N_LON - 1)]
    greet(around)
    copy_in = pltpu.make_async_copy(d_conv, X.at[pl.ds(1, 24)], load.at[0])
    copies_own = [
        pltpu.make_async_copy(fields, own.at[pl.ds(1, 24)], load.at[1]),
        pltpu.make_async_copy(lon_halo.at[0], own.at[0], load.at[2]),
        pltpu.make_async_copy(lon_halo.at[1], own.at[25], load.at[3]),
    ]
    copy_in.start()
    for copy in copies_own:
        copy.start()
    copy_in.wait()
    pack_edges(X, EL, ER, None)
    greeted(around)
    copies = halo_copies(X, EL, ER, LH, RH, send, recv, lon, lat)
    for copy in copies:
        copy.start()
    share_copies, tap_copies = [], []
    for d in range(1, N_LAT):
        to = lax.rem(lat + d, N_LAT)
        share_copies.append(pltpu.make_async_remote_copy(
            src_ref=shares.at[to], dst_ref=parts.at[d], send_sem=send_one.at[d], recv_sem=recv_one.at[d],
            device_id=(lon, to), device_id_type=MESH))
        tap_copies.append(pltpu.make_async_remote_copy(
            src_ref=tap_shares.at[to], dst_ref=tap_parts.at[d], send_sem=send_tap.at[d], recv_sem=recv_tap.at[d],
            device_id=(lon, to), device_id_type=MESH))
    for copy in share_copies:
        copy.start()
    build_permutation(PM)
    clear_margins(PS)
    land_pad[...] = jnp.zeros((CLAT, 128), F32)
    land_pad[:, 0:CLON] = land[...].astype(F32)
    land_t = land_pad[...]
    expand_mask(with_ones(land_t), M, NI + 1)
    for copy in copies_own:
        copy.wait()
    for blocks in INNER + ((0, NI),):
        group_blocks(lambda k, i: own[2 * k + i // 4, i % 4], blocks, PM, PS, M)
    group_halos(left_halo, right_halo, EH, PM, PS, lat)
    for g in range(NG):
        shift_blocks(PS, Z, g)
    clear_margins(PS)
    for blocks in ((0, 1, 2, 3), (4, 5, 6, 7), (8, 9, 10, 11)):
        group_blocks(lambda k, i: X[1 + 2 * k + i // 4, i % 4], blocks, PM, PS, None)
    pair_rows(PS, MP)
    for g in range(NG):
        tap_gradients(Z, MP, G, taps, (g,))
    gather_taps(taps, square, tap_shares)
    for copy in tap_copies:
        copy.start()
    build_weights(w, W, True)
    expand_mask(land_t, M, NI)

    def cells(k, i):
        return X[2 * k + i // 4, i % 4]

    for blocks in INNER:
        group_blocks(cells, blocks, PM, PS, None)
    for copy in copies:
        copy.wait()
    group_blocks(cells, (0, NI), PM, PS, None)
    group_halos(LH, RH, EH, PM, PS, lat)
    for copy in share_copies:
        copy.wait()
    total = shares[lat].astype(F32)
    for d in range(1, N_LAT):
        total += parts[d].astype(F32)
    mine[...] = total * GRAD_SCALE

    def spread(block, parts, send_sem, recv_sem):
        made = [
            pltpu.make_async_remote_copy(
                src_ref=block, dst_ref=parts.at[d], send_sem=send_sem.at[d], recv_sem=recv_sem.at[d],
                device_id=(lax.rem(lon + d, N_LON), lat), device_id_type=MESH)
            for d in range(1, N_LON)
        ]
        for copy in made:
            copy.start()
        return made

    last_copies = spread(mine, whole, send_two, recv_two)
    for g in range(NG // 2):
        shift_blocks(PS, Z, g)
        banded_conv(Z, W, AB, S, M, g)
    for copy in tap_copies:
        copy.wait()
    total = tap_shares[lat]
    for d in range(1, N_LAT):
        total += tap_parts[d]
    tap_mine[...] = total * GRAD_SCALE
    last_copies += spread(tap_mine, tap_whole, send_last, recv_last)
    for g in range(NG // 2, NG):
        shift_blocks(PS, Z, g)
        banded_conv(Z, W, AB, S, M, g)
    for copy in last_copies:
        copy.wait()
    total, tap_total = mine[...], tap_mine[...]
    for d in range(1, N_LON):
        total += whole[d]
        tap_total += tap_whole[d]
    total_out[0:80] = total
    total_out[80:88] = tap_total


def backward_conv(d_conv, fields, lon_halo, left_halo, right_halo, land, w, shares):
    dma = pltpu.SemaphoreType.DMA
    scratch = halo_scratch()
    scratch.pop(11)
    return pl.pallas_call(
        grad_kernel,
        name="backward_conv",
        out_shape=(pltpu.VMEM((NG, NI, 64, 128), BF16), pltpu.VMEM((88, C), F32)),
        in_specs=hbm(3) + vmem(5),
        out_specs=tuple(vmem(2)),
        scratch_shapes=scratch
        + [
            pltpu.VMEM((26, 4, CLAT, C), BF16),
            pltpu.VMEM((NG, NI, ZR, 256), BF16),
            pltpu.VMEM((2, 2, 256, 512), F32),
            pltpu.VMEM((NG, 56, 128), F32),
            pltpu.VMEM((128, 128), F32),
            pltpu.VMEM((N_LAT, 8, 128), F32),
            pltpu.VMEM((N_LAT, 80, 128), BF16),
            pltpu.VMEM((N_LAT, 8, 128), F32),
            pltpu.VMEM((80, 128), F32),
            pltpu.VMEM((N_LON, 80, 128), F32),
            pltpu.VMEM((8, 128), F32),
            pltpu.VMEM((N_LON, 8, 128), F32),
            dma((8,)), dma((8,)), dma((N_LAT,)), dma((N_LAT,)), dma((N_LAT,)), dma((N_LAT,)),
            dma((N_LON,)), dma((N_LON,)), dma((N_LON,)), dma((N_LON,)), dma((4,)),
        ],
        compiler_params=pltpu.CompilerParams(collective_id=1, has_side_effects=True, vmem_limit_bytes=VMEM_LIMIT),
    )(d_conv, fields, lon_halo, left_halo, right_halo, land, w, shares)


def finish_kernel(place, S, up, total, grad_input, out_win, out_wout, out_dw, out_channel, out_bin,
                  S_in, up_in, made, PM, load_s, load_up, store):
    copies = []
    for n in range(3):
        copies.append((
            pltpu.make_async_copy(S.at[:, pl.ds(4 * n, 4)], S_in.at[n], load_s.at[n]),
            pltpu.make_async_copy(up.at[pl.ds(32 * n, 32)], up_in.at[n], load_up.at[n]),
            pltpu.make_async_copy(made.at[n], grad_input.at[pl.ds(32 * n, 32)], store.at[n]),
        ))
        copies[n][0].start()
        copies[n][1].start()
    build_permutation(PM)
    lat = place[0]
    out_win[...] = total[0:32]
    out_wout[...] = total[32:64]
    small = total[64:72]
    out_bin[...] = pltpu.roll(small, lax.rem(128 - 32 * lax.rem(lat, 4), 128), axis=1)[0:1, 0:32]
    out_channel[...] = pltpu.roll(small, lax.rem(128 - 8 * lat, 128), axis=1)[1:6, 0:8]
    out_dw[...] = total[80:88, 0:49]
    for chunk in range(3):
        copies[chunk][0].wait()
        copies[chunk][1].wait()

        def put(n, both, chunk=chunk):
            for m in range(4):
                for h in range(2):
                    at = 8 * m + 2 * n + h
                    value = up_in[chunk, at].astype(F32) + both[64 * m : 64 * m + 64, 128 * h : 128 * h + 128]
                    made[chunk, at] = value.astype(BF16)

        ungroup(S_in.at[chunk], PM, range(4), put)
        copies[chunk][2].start()
    for chunk in range(3):
        copies[chunk][2].wait()


def finish(place, S, upstream, total):
    dma = pltpu.SemaphoreType.DMA
    return pl.pallas_call(
        finish_kernel,
        name="finish",
        out_shape=(
            jax.ShapeDtypeStruct((CLON, CLAT, C), BF16),
            jax.ShapeDtypeStruct((32, C), F32),
            jax.ShapeDtypeStruct((32, C), F32),
            jax.ShapeDtypeStruct((8, 49), F32),
            jax.ShapeDtypeStruct((5, 8), F32),
            jax.ShapeDtypeStruct((1, 32), F32),
        ),
        in_specs=[pl.BlockSpec(memory_space=pltpu.SMEM)] + hbm(2) + vmem(1),
        out_specs=tuple(hbm(1) + vmem(5)),
        scratch_shapes=[
            pltpu.VMEM((3, NG, 4, 64, 128), BF16),
            pltpu.VMEM((3, 32, CLAT, C), BF16),
            pltpu.VMEM((3, 32, CLAT, C), BF16),
            pltpu.VMEM((1024, 1024), BF16),
            dma((3,)), dma((3,)), dma((3,)),
        ],
        compiler_params=pltpu.CompilerParams(vmem_limit_bytes=VMEM_LIMIT),
    )(place, S, upstream, total)


def per_device(fields, land_sea, tile_list, upstream, dw_weight, dw_bias, ln_gain, ln_bias, w_in, b_in, w_out, b_out,
               layer_scale):
    def row(v):
        return v.reshape(1, -1)

    fours = fields.reshape(24, 4, CLAT, C)
    land = land_sea.T
    conv, lon_halo, left_halo, right_halo = forward_conv(fours, land, dw_weight)
    mixed, d_conv, shares = listed_mlp(
        tile_list.reshape(-1), conv, fours, upstream, land, row(dw_bias), row(ln_gain), row(ln_bias), w_in, row(b_in), w_out,
        row(b_out), row(layer_scale))
    grouped, total = backward_conv(d_conv, fours, lon_halo, left_halo, right_halo, land, dw_weight, shares)
    place = lax.axis_index("lat").astype(jnp.int32).reshape(1)
    grad_input, g_win, g_wout, g_dw, g_channel, g_bin = finish(place, grouped, upstream, total)
    return mixed, grad_input, g_win.T, g_wout, g_dw.T, g_channel, g_bin.reshape(-1)


def solution(mesh):
    cells = P("lon", "lat", None)
    return jax.shard_map(
        per_device,
        mesh=mesh,
        in_specs=(cells, P("lon", "lat"), cells, cells) + (P(),) * 9,
        out_specs=(cells, cells, P(None, "lat"), P("lat", None), P(None, "lat"), P(None, "lat"), P("lat")),
        check_vma=False,
    )
```

```python
import functools
import math

import jax
import jax.numpy as jnp
from jax import lax
from jax.experimental import pallas as pl
from jax.experimental.pallas import tpu as pltpu
from jax.sharding import PartitionSpec as P

LN_EPSILON = 1e-06
MESH = pl.DeviceIdType.MESH
F32 = jnp.float32
BF16 = jnp.bfloat16
CLON, CLAT, C, FF = 96, 64, 128, 512
NI, NJ = CLON // 8, CLAT // 8
TILES = NI * NJ
TCAP = 72
NG = 8
ZR = 80
N_LON, N_LAT = 8, 16
SHIFTS = (-4, -2, 0, 2)
GRAD_SCALE = 1.0 / math.sqrt(768 * 1024)
VMEM_LIMIT = 42 * 1024 * 1024
ERF_COEFS = (0.7978697125817803, 0.03639228534613075, -8.782596074631976e-05, -3.669357312826199e-05,
             1.4250137713525853e-06)
PDF_SCALE = -0.5 / math.log(2.0)
PDF_SHIFT = -0.5 * math.log2(2.0 * math.pi)


def iota(shape, dim):
    return lax.broadcasted_iota(jnp.int32, shape, dim)


def build_weights(w_ref, W, flip):
    q_row, q_col = iota((56, 49), 0), iota((56, 49), 1)
    a, b = q_row // 8, q_row % 8
    tap = (6 - a) * 7 + (6 - b) if flip else a * 7 + b
    pick = jnp.where((q_col == tap) & (b < 7), 1.0, 0.0).astype(BF16)
    taps = jnp.dot(pick, w_ref[...].astype(BF16), preferred_element_type=F32).astype(BF16)
    lane_i = iota((8, 128), 1) // 16
    same = (iota((16, 128), 0) == iota((16, 128), 1) % 16).astype(F32)

    def group(g):
        spread = jnp.where(iota((128, 128), 0) == 16 * g + iota((128, 128), 1) % 16, 1.0, 0.0).astype(BF16)
        rep = jnp.dot(taps, spread, preferred_element_type=F32)
        for i_in in range(16):
            v = jnp.zeros((8, 128), F32)
            for a in range(7):
                if 0 <= i_in - 1 - a < 8:
                    v = jnp.where(lane_i == i_in - 1 - a, rep[8 * a : 8 * a + 8], v)
            base = (i_in // 8) * 512 + (i_in % 8) * 16
            W[g, base : base + 16, 0:128] = jnp.zeros((16, 128), BF16)
            for b in range(7):
                parity = (b + 1) % 2
                e = (b - 3 - parity + 4) // 2
                row = jnp.broadcast_to(v[b : b + 1], (16, 128)) * same
                W[g, base + 128 * e : base + 128 * e + 16, 128 * parity : 128 * parity + 128] = row.astype(BF16)

    for g in range(NG):
        group(g)


def build_permutation(PM):
    def clear(n, carry):
        PM[pl.ds(pl.multiple_of(64 * n, 64), 64), :] = jnp.zeros((64, 1024), BF16)
        return carry

    lax.fori_loop(0, 16, clear, 0)
    row, lane = iota((16, 128), 0), iota((16, 128), 1)
    for p in range(8):
        unit = jnp.where(lane == 16 * p + row, 1.0, 0.0).astype(BF16)
        for q in range(8):
            PM[128 * p + 16 * q : 128 * p + 16 * q + 16, 128 * q : 128 * q + 128] = unit


def expand_mask(land_ext, M, count):
    value = land_ext.astype(BF16)
    row, block = iota((128, 128), 0), iota((128, 128), 1) // 16

    for k in range(count):
        pick = jnp.where(row == 8 * k + block, 1.0, 0.0).astype(BF16)
        M[k] = jnp.dot(value, pick, preferred_element_type=F32)


def with_ones(land_t):
    lane = iota((CLAT, 128), 1)
    return jnp.where((lane < 4) | (lane >= CLON + 4), 1.0, pltpu.roll(land_t, 4, axis=1))


def pack_edges(X, EL, ER, masks):
    low = iota((8, 128), 0) < 4

    def block(n, carry):
        for east, E in ((0, EL), (1, ER)):
            out = []
            keep = None if masks is None else pltpu.roll(masks[east], lax.rem(128 - 8 * n, 128), axis=1)
            for m in range(4):
                pair = []
                for i in (2 * m, 2 * m + 1):
                    cells = X[2 * n + i // 4, i % 4, 48 * east : 48 * east + 16].astype(F32)
                    pair.append(cells[8 * east : 8 * east + 8])
                if east:
                    value = jnp.where(low, pltpu.roll(pair[0], 4, axis=0), pair[1])
                else:
                    value = jnp.where(low, pair[0], pltpu.roll(pair[1], 4, axis=0))
                if keep is not None:
                    value = value * jnp.broadcast_to(keep[:, 2 * m : 2 * m + 1], (8, 128))
                out.append(value)
            E[n] = jnp.concatenate(out, axis=0).astype(BF16)
        return carry

    lax.fori_loop(0, NI, block, 0)


def halo_copies(first, last, XH, EL, ER, LH, RH, send, recv, lon, lat):
    up, down = lax.rem(lon + 1, N_LON), lax.rem(lon + N_LON - 1, N_LON)
    east, west = lax.rem(lat + 1, N_LAT), lax.rem(lat + N_LAT - 1, N_LAT)
    plan = (
        (EL, RH.at[pl.ds(1, NI)], (lon, west)),
        (ER, LH.at[pl.ds(1, NI)], (lon, east)),
        (first, XH.at[1], (down, lat)),
        (last, XH.at[0], (up, lat)),
        (EL.at[0, pl.ds(0, 16)], RH.at[13, pl.ds(0, 16)], (down, west)),
        (EL.at[NI - 1, pl.ds(16, 16)], RH.at[0, pl.ds(16, 16)], (up, west)),
        (ER.at[0, pl.ds(0, 16)], LH.at[13, pl.ds(0, 16)], (down, east)),
        (ER.at[NI - 1, pl.ds(16, 16)], LH.at[0, pl.ds(16, 16)], (up, east)),
    )
    return [
        pltpu.make_async_remote_copy(
            src_ref=src, dst_ref=dst, send_sem=send.at[n], recv_sem=recv.at[n], device_id=where, device_id_type=MESH
        )
        for n, (src, dst, where) in enumerate(plan)
    ]


def neighbours(lon, lat):
    up, down = lax.rem(lon + 1, N_LON), lax.rem(lon + N_LON - 1, N_LON)
    east, west = lax.rem(lat + 1, N_LAT), lax.rem(lat + N_LAT - 1, N_LAT)
    return [(lon, west), (lon, east), (down, lat), (up, lat), (down, west), (up, west), (down, east), (up, east)]


def greet(places):
    barrier = pltpu.get_barrier_semaphore()
    for place in places:
        pl.semaphore_signal(barrier, inc=1, device_id=place, device_id_type=MESH)


def greeted(places):
    pl.semaphore_wait(pltpu.get_barrier_semaphore(), len(places))


def clear_margins(PS):
    def block(k, carry):
        PS[:, k, 8:16] = jnp.zeros((NG, 8, 128), F32)
        PS[:, k, 80:104] = jnp.zeros((NG, 24, 128), F32)
        return carry

    lax.fori_loop(0, NI + 1, block, 0)


def padded_cells(X, XH):
    def cells(k, i):
        at = 2 * k + i // 4 - 1
        if at < 0:
            return XH[0, i]
        return XH[1, i - 4] if at > 23 else X[at, i % 4]

    return cells


def group_blocks(cells, blocks, PM, PS, M):
    lhs = jnp.concatenate([jnp.concatenate([cells(k, i) for k in blocks], axis=0) for i in range(8)], axis=1)

    for n in range(NG // 2):
        both = jnp.dot(lhs, PM[:, 256 * n : 256 * n + 256], preferred_element_type=F32)
        for h in range(2):
            for m, k in enumerate(blocks):
                part = both[64 * m : 64 * m + 64, 128 * h : 128 * h + 128]
                PS[2 * n + h, k, 16:80] = part if M is None else part * M[k]


def group_halos(LH, RH, EH, PM, PS, lat):
    low = iota((8, 128), 0) < 4
    keep = jnp.where(low, jnp.where(lat < N_LAT - 1, 1.0, 0.0), jnp.where(lat > 0, 1.0, 0.0))

    def rows_of(k):
        rows = []
        for m in range(4):
            at = (16, 24, 0, 8)[m]
            left = LH[k + m // 2, at // 16 * 16 : at // 16 * 16 + 16].astype(F32)[at % 16 : at % 16 + 8]
            right = RH[k + m // 2, at // 16 * 16 : at // 16 * 16 + 16].astype(F32)[at % 16 : at % 16 + 8]
            rows.append(jnp.where(low, right, pltpu.roll(left, 4, axis=0)) * keep)
            rows.append(jnp.where(low, pltpu.roll(right, 4, axis=0), left) * keep)
        return rows

    for n in range(7):
        first = rows_of(2 * n)
        second = rows_of(2 * n + 1) if 2 * n + 1 <= NI else first
        for i in range(8):
            EH[n, :, 128 * i : 128 * i + 128] = jnp.concatenate([first[i], second[i]], axis=0).astype(BF16)

    edges = EH[...].reshape(112, 1024)
    for n in range(NG // 2):
        both = jnp.dot(edges, PM[:, 256 * n : 256 * n + 256], preferred_element_type=F32)
        for h in range(2):
            for k in range(NI + 1):
                part = both[8 * k : 8 * k + 8, 128 * h : 128 * h + 128]
                PS[2 * n + h, k, 8:16] = part
                PS[2 * n + h, k, 80:88] = part


def shift_blocks(PS, Z, g):
    for k in range(NI + 1):
        for e, shift in enumerate(SHIFTS):
            Z[g, k, :, 128 * e : 128 * e + 128] = PS[g, k, 16 + shift : 16 + shift + ZR].astype(BF16)


INNER = ((1, 2, 3, 4), (5, 6, 7, 8), (9, 10, 11))


def banded_conv(Z, W, AB, S, M, g):
    lhs = jnp.concatenate([Z[g, 0:NI].reshape(NI * ZR, 512), Z[g, 1 : NI + 1].reshape(NI * ZR, 512)], axis=1)
    both = jnp.dot(lhs, W[g], preferred_element_type=F32)
    AB[g % 2] = both[:, 128:256]
    for n in range(NI):
        value = both[n * ZR : n * ZR + 64, 0:128] + AB[g % 2, n * ZR + 1 : n * ZR + 65]
        S[g, n] = (value if M is None else value * M[n]).astype(BF16)


def ungroup(S, PM, blocks, put):
    rows = [jnp.concatenate([S[g, k] for k in blocks], axis=0) for g in range(NG)]
    lhs = jnp.concatenate(rows, axis=1)
    for n in range(NG // 2):
        put(n, jnp.dot(lhs, PM[:, 256 * n : 256 * n + 256], preferred_element_type=F32))


def conv_kernel(fields, upstream, w_in, w_out, land_far, w_far,
                conv_out, lon_halo, left_halo, right_halo, X, near_up, near_in, near_out,
                land, w, EX, XH, EL, ER, LH, RH, EH, PS, Z, W, PM, AB, S, M, land_pad, send, recv, load):
    lon, lat = lax.axis_index("lon"), lax.axis_index("lat")
    around = neighbours(lon, lat)
    greet(around)
    pairs = ((land_far, land), (fields, X), (w_far, w), (upstream, near_up), (w_in, near_in), (w_out, near_out))
    loads = [pltpu.make_async_copy(far, near, load.at[n]) for n, (far, near) in enumerate(pairs)]
    for copy in loads:
        copy.start()
    land_pad[...] = jnp.zeros((CLAT, 128), F32)
    loads[0].wait()
    land_pad[:, 0:CLON] = land[...].astype(F32)
    land_t = land_pad[...]
    expand_mask(with_ones(land_t), M, NI + 1)
    low = iota((8, 128), 0) < 4
    masks = []
    for east in range(2):
        edge = land_pad[56 * east : 56 * east + 8]
        turned = pltpu.roll(edge, 4, axis=0)
        edge = jnp.where(low, turned, edge) if east else jnp.where(low, edge, turned)
        masks.append(jnp.where(low, edge, pltpu.roll(edge, 127, axis=1)))
    loads[1].wait()
    pack_edges(X, EL, ER, masks)
    for at, first in ((0, 0), (23, CLON - 4)):
        for i in range(4):
            keep = jnp.broadcast_to(land_t[:, first + i : first + i + 1], (CLAT, C))
            EX[at // 23, i] = (X[at, i].astype(F32) * keep).astype(BF16)
    greeted(around)
    copies = halo_copies(EX.at[0], EX.at[1], XH, EL, ER, LH, RH, send, recv, lon, lat)
    for copy in copies:
        copy.start()
    build_permutation(PM)
    clear_margins(PS)
    cells = padded_cells(X, XH)

    for blocks in INNER:
        group_blocks(cells, blocks, PM, PS, M)
    loads[2].wait()
    build_weights(w, W, False)
    for copy in copies:
        copy.wait()
    lon_halo[...] = XH[...]
    left_halo[...] = LH[...]
    right_halo[...] = RH[...]
    group_blocks(cells, (0, NI), PM, PS, M)
    group_halos(LH, RH, EH, PM, PS, lat)
    for g in range(NG):
        shift_blocks(PS, Z, g)
        banded_conv(Z, W, AB, S, None, g)
    for first in range(0, NI, 4):

        def put(n, both, first=first):
            for m in range(4):
                for t in range(NJ):
                    at = 64 * m + 8 * t
                    value = jnp.concatenate([both[at : at + 8, 0:128], both[at : at + 8, 128:256]], axis=0)
                    conv_out[(first + m) * NJ + t, 16 * n : 16 * n + 16] = value.astype(BF16)

        ungroup(S, PM, range(first, first + 4), put)
    for copy in loads[3:]:
        copy.wait()


def vmem(n):
    return [pl.BlockSpec(memory_space=pltpu.VMEM)] * n


def hbm(n):
    return [pl.BlockSpec(memory_space=pl.ANY)] * n


def halo_scratch():
    return [
        pltpu.VMEM((2, 4, CLAT, C), BF16),
        pltpu.VMEM((NI, 32, C), BF16),
        pltpu.VMEM((NI, 32, C), BF16),
        pltpu.VMEM((14, 32, C), BF16),
        pltpu.VMEM((14, 32, C), BF16),
        pltpu.VMEM((7, 16, 1024), BF16),
        pltpu.VMEM((NG, NI + 1, 104, 128), F32),
        pltpu.VMEM((NG, NI + 1, ZR, 512), BF16),
        pltpu.VMEM((NG, 1024, 256), BF16),
        pltpu.VMEM((1024, 1024), BF16),
        pltpu.VMEM((2, NI * ZR, 128), F32),
        pltpu.VMEM((NG, NI, 64, 128), BF16),
        pltpu.VMEM((NI + 1, 64, 128), F32),
        pltpu.VMEM((CLAT, 128), F32),
    ]


def forward_conv(fields, upstream, w_in, w_out, land, w):
    dma = pltpu.SemaphoreType.DMA
    return pl.pallas_call(
        conv_kernel,
        name="forward_conv",
        out_shape=(
            pltpu.VMEM((TILES, 64, C), BF16),
            pltpu.VMEM((2, 4, CLAT, C), BF16),
            pltpu.VMEM((14, 32, C), BF16),
            pltpu.VMEM((14, 32, C), BF16),
            pltpu.VMEM((24, 4, CLAT, C), BF16),
            pltpu.VMEM((CLON, CLAT, C), BF16),
            pltpu.VMEM((C, FF), BF16),
            pltpu.VMEM((FF, C), BF16),
        ),
        in_specs=hbm(6),
        out_specs=tuple(vmem(8)),
        scratch_shapes=[
            pltpu.VMEM((CLAT, CLON), jnp.int32),
            pltpu.VMEM((49, C), F32),
            pltpu.VMEM((2, 4, CLAT, C), BF16),
        ]
        + halo_scratch()
        + [dma((8,)), dma((8,)), dma((6,))],
        compiler_params=pltpu.CompilerParams(collective_id=0, has_side_effects=True, vmem_limit_bytes=VMEM_LIMIT),
    )(fields, upstream, w_in, w_out, land, w)


def normal_cdf(h, square):
    q = jnp.full(h.shape, ERF_COEFS[-1], F32)
    for coef in ERF_COEFS[-2::-1]:
        q = q * square + coef
    return 0.5 + 0.5 * jnp.tanh(h * q)


def mlp_kernel(tile_ids, conv, fields, upstream, land, offset, gain, shift, w_in, b_in, w_out, b_out, scale,
               mixed, d_conv_out, shares, branch, d_conv, w_in_t, w_out_t, g_in, g_out, g_bin, sums, land_tr, mixed_part, store):
    slots = 18
    rows = slots * 64
    land_tr[...] = jnp.zeros((CLAT, 128), F32)
    land_tr[:, 0:CLON] = land[...].astype(F32)
    w_in_t[...] = w_in[...].astype(F32).T.astype(BF16)
    w_out_t[...] = w_out[...].astype(F32).T.astype(BF16)
    branch[...] = jnp.zeros(branch.shape, F32)
    d_conv[...] = jnp.zeros(d_conv.shape, F32)
    for acc in (g_in, g_out, g_bin, sums):
        acc[...] = jnp.zeros(acc.shape, F32)
    gain_row, shift_row, scale_row = gain[...], shift[...], scale[...]

    def step(n, carry):
        ids = [tile_ids[slots * n + q] for q in range(slots)]
        tiles = [jnp.maximum(t, 0) for t in ids]
        conv_parts, up_parts, active_parts = [], [], []
        for q in range(slots):
            t = tiles[q]
            big, small = t // NJ, lax.rem(t, NJ)
            conv_parts.append(conv[t].astype(F32))
            pair = upstream[pl.ds(8 * big, 8), pl.ds(16 * (small // 2), 16), :].astype(F32)
            odd = lax.rem(small, 2) == 1
            up_parts.append(jnp.where(odd, pair[:, 8:16], pair[:, 0:8]).reshape(64, C))
            strip = pltpu.roll(land_tr[pl.ds(8 * small, 8), :], lax.rem(128 - 8 * big, 128), axis=1)
            live = jnp.where(ids[q] >= 0, 1.0, 0.0)
            strip = strip * live
            active_parts += [jnp.broadcast_to(strip[:, i : i + 1], (8, C)) for i in range(8)]
        conv_rows = jnp.concatenate(conv_parts, axis=0) + offset[...]
        up = jnp.concatenate(up_parts, axis=0)
        active = jnp.concatenate(active_parts, axis=0)
        center = conv_rows - jnp.mean(conv_rows, axis=-1, keepdims=True)
        inv_std = lax.rsqrt(jnp.mean(center * center, axis=-1, keepdims=True) + LN_EPSILON)
        normed = center * inv_std
        normed_b = (normed * gain_row + shift_row).astype(BF16)
        hidden = jnp.dot(normed_b, w_in[...], preferred_element_type=F32) + b_in[...]
        square = hidden * hidden
        cdf = normal_cdf(hidden, square)
        activated = (hidden * cdf).astype(BF16)
        output = jnp.dot(activated, w_out[...], preferred_element_type=F32) + b_out[...]
        gate = active * scale_row
        branch_rows = gate * output
        d_out = gate * up
        d_out_b = d_out.astype(BF16)
        g_out[...] += lax.dot_general(d_out_b, activated, (((0,), (0,)), ((), ())), preferred_element_type=F32)
        pdf = jnp.exp2(square * PDF_SCALE + PDF_SHIFT)
        d_hidden = jnp.dot(d_out_b, w_out_t[...], preferred_element_type=F32) * (cdf + hidden * pdf)
        d_hidden_b = d_hidden.astype(BF16)
        g_in[...] += lax.dot_general(normed_b, d_hidden_b, (((0,), (0,)), ((), ())), preferred_element_type=F32)
        g_bin[...] += jnp.sum(d_hidden.reshape(rows // 8, 8, FF), axis=0)
        d_norm = jnp.dot(d_hidden_b, w_in_t[...], preferred_element_type=F32)
        d_scaled = d_norm * gain_row
        d_cells = inv_std * (
            d_scaled
            - jnp.mean(d_scaled, axis=-1, keepdims=True)
            - normed * jnp.mean(d_scaled * normed, axis=-1, keepdims=True)
        )
        for k, term in enumerate((d_cells, d_norm * normed, d_norm, d_out, active * output * up)):
            sums[k] += jnp.sum(term.reshape(rows // 8, 8, C), axis=0)
        for q in range(slots):
            to = jnp.where(ids[q] >= 0, ids[q], TILES)
            branch[to] = branch_rows[64 * q : 64 * q + 64]
            d_conv[to] = d_cells[64 * q : 64 * q + 64]

        return carry

    lax.fori_loop(0, TCAP // slots, step, 0)

    stores = [
        pltpu.make_async_copy(mixed_part.at[n], mixed.at[pl.ds(32 * n, 32)], store.at[n]) for n in range(3)
    ]
    for chunk in range(3):

        def mix(n, carry, chunk=chunk):
            for i in range(8):
                rows_i = jnp.concatenate([branch[n * NJ + t, 8 * i : 8 * i + 8] for t in range(NJ)], axis=0)
                total = fields[2 * n + i // 4, i % 4].astype(F32) + rows_i
                mixed_part[chunk, 8 * (n - 4 * chunk) + i] = total.astype(BF16)
                rows_i = jnp.concatenate([d_conv[n * NJ + t, 8 * i : 8 * i + 8] for t in range(NJ)], axis=0)
                d_conv_out[2 * n + i // 4, i % 4] = rows_i.astype(BF16)
            return carry

        lax.fori_loop(4 * chunk, 4 * chunk + 4, mix, 0)
        stores[chunk].start()
    bin_row = jnp.sum(g_bin[...], axis=0, keepdims=True)
    tail = jnp.concatenate([jnp.sum(sums[k], axis=0, keepdims=True) for k in range(5)], axis=0)
    for n in range(4):
        turned_in = g_in[:, 128 * n : 128 * n + 128].T
        turned_out = g_out[:, 128 * n : 128 * n + 128].T
        for m in range(4):
            q = 4 * n + m
            shares[q, 0:32] = turned_in[32 * m : 32 * m + 32].astype(BF16)
            shares[q, 32:64] = turned_out[32 * m : 32 * m + 32].astype(BF16)
            rest = [bin_row[:, 128 * n : 128 * n + 128], tail, jnp.zeros((10, 128), F32)]
            shares[q, 64:80] = jnp.concatenate(rest, axis=0).astype(BF16)
    for copy in stores:
        copy.wait()


def listed_mlp(tile_ids, conv, fields, upstream, land, offset, gain, shift, w_in, b_in, w_out, b_out, scale):
    return pl.pallas_call(
        mlp_kernel,
        name="listed_mlp",
        out_shape=(
            jax.ShapeDtypeStruct((CLON, CLAT, C), BF16),
            pltpu.VMEM((24, 4, CLAT, C), BF16),
            pltpu.VMEM((N_LAT, 80, 128), BF16),
        ),
        in_specs=[pl.BlockSpec(memory_space=pltpu.SMEM)] + vmem(12),
        out_specs=tuple(hbm(1) + vmem(2)),
        scratch_shapes=[
            pltpu.VMEM((TILES + 1, 64, C), F32),
            pltpu.VMEM((TILES + 1, 64, C), F32),
            pltpu.VMEM((FF, C), BF16),
            pltpu.VMEM((C, FF), BF16),
            pltpu.VMEM((C, FF), F32),
            pltpu.VMEM((C, FF), F32),
            pltpu.VMEM((8, FF), F32),
            pltpu.VMEM((5, 8, C), F32),
            pltpu.VMEM((CLAT, 128), F32),
            pltpu.VMEM((3, 32, CLAT, C), BF16),
            pltpu.SemaphoreType.DMA((3,)),
        ],
        compiler_params=pltpu.CompilerParams(vmem_limit_bytes=VMEM_LIMIT),
    )(tile_ids, conv, fields, upstream, land, offset, gain, shift, w_in, b_in, w_out, b_out, scale)


def pair_rows(PS, MP):
    for g in range(NG):
        for n in range(NI):
            MP[g, n, :, 0:128] = PS[g, n, 16 : 16 + ZR].astype(BF16)
            MP[g, n, :, 128:256] = PS[g, n, 15 : 15 + ZR].astype(BF16)


def tap_gradients(Z, MP, G, taps, groups):
    lane = iota((16, 128), 1)
    same = (iota((16, 128), 0) == lane % 16).astype(F32)
    block = lane // 16
    for g in groups:
        taps[g] = jnp.zeros(taps.shape[1:], F32)
        lhs = MP[g].reshape(NI * ZR, 256)
        for half in range(2):
            rhs = Z[g, half : half + NI].reshape(NI * ZR, 512)
            G[g % 2, half] = lax.dot_general(lhs, rhs, (((0,), (0,)), ((), ())), preferred_element_type=F32)
        for e in range(4):
            for parity in range(2):
                b = 3 + SHIFTS[e] + parity
                if not 0 <= b < 7:
                    continue
                for a in range(7):
                    total = None
                    for i_out in range(8):
                        half, k = divmod(i_out + a + 1, 8)
                        at = 128 * parity + 16 * i_out
                        piece = G[g % 2, half, at : at + 16, 128 * e : 128 * e + 128]
                        total = piece if total is None else jnp.where(block == k, piece, total)
                    taps[g, 7 * a + b : 7 * a + b + 1] = jnp.sum(total * same, axis=0, keepdims=True)


def gather_taps(taps, square, tap_shares):
    total = jnp.zeros((56, 128), F32)
    for g in range(NG):
        row, col = iota((128, 128), 0), iota((128, 128), 1)
        pick = jnp.where((col // 16 == g) & (row % 16 == col % 16), 1.0, 0.0).astype(BF16)
        value = taps[g]
        head = value.astype(BF16)
        tail = (value - head.astype(F32)).astype(BF16)
        total += jnp.dot(head, pick, preferred_element_type=F32) + jnp.dot(tail, pick, preferred_element_type=F32)
    square[...] = jnp.zeros((128, 128), F32)
    square[0:56] = total
    turned = square[...].T
    for q in range(N_LAT):
        tap_shares[q] = turned[8 * q : 8 * q + 8]


def grad_kernel(d_conv, fields, lon_halo, left_halo, right_halo, land, w, shares,
                S, total_out,
                XH, EL, ER, LH, RH, EH, PS, Z, W, PM, AB, M, land_pad, MP, G, taps, square, tap_shares, parts, tap_parts, mine, whole, tap_mine, tap_whole,
                send, recv, send_one, recv_one, send_tap, recv_tap, send_two, recv_two, send_last, recv_last):
    lon, lat = lax.axis_index("lon"), lax.axis_index("lat")
    around = neighbours(lon, lat)
    around += [(lon, lax.rem(lat + d, N_LAT)) for d in range(2, N_LAT - 1)]
    around += [(lax.rem(lon + d, N_LON), lat) for d in range(2, N_LON - 1)]
    greet(around)
    pack_edges(d_conv, EL, ER, None)
    greeted(around)
    copies = halo_copies(d_conv.at[0], d_conv.at[23], XH, EL, ER, LH, RH, send, recv, lon, lat)
    for copy in copies:
        copy.start()
    share_copies, tap_copies = [], []
    for d in range(1, N_LAT):
        to = lax.rem(lat + d, N_LAT)
        share_copies.append(pltpu.make_async_remote_copy(
            src_ref=shares.at[to], dst_ref=parts.at[d], send_sem=send_one.at[d], recv_sem=recv_one.at[d],
            device_id=(lon, to), device_id_type=MESH))
        tap_copies.append(pltpu.make_async_remote_copy(
            src_ref=tap_shares.at[to], dst_ref=tap_parts.at[d], send_sem=send_tap.at[d], recv_sem=recv_tap.at[d],
            device_id=(lon, to), device_id_type=MESH))
    for copy in share_copies:
        copy.start()
    build_permutation(PM)
    clear_margins(PS)
    land_pad[...] = jnp.zeros((CLAT, 128), F32)
    land_pad[:, 0:CLON] = land[...].astype(F32)
    land_t = land_pad[...]
    expand_mask(with_ones(land_t), M, NI + 1)
    cells = padded_cells(fields, lon_halo)
    for blocks in INNER + ((0, NI),):
        group_blocks(cells, blocks, PM, PS, M)
    group_halos(left_halo, right_halo, EH, PM, PS, lat)
    for g in range(NG):
        shift_blocks(PS, Z, g)
    clear_margins(PS)
    for blocks in ((0, 1, 2, 3), (4, 5, 6, 7), (8, 9, 10, 11)):
        group_blocks(lambda k, i: d_conv[2 * k + i // 4, i % 4], blocks, PM, PS, None)
    pair_rows(PS, MP)
    for g in range(NG):
        tap_gradients(Z, MP, G, taps, (g,))
    gather_taps(taps, square, tap_shares)
    for copy in tap_copies:
        copy.start()
    build_weights(w, W, True)
    expand_mask(land_t, M, NI)
    cells = padded_cells(d_conv, XH)
    for blocks in INNER:
        group_blocks(cells, blocks, PM, PS, None)
    for copy in copies:
        copy.wait()
    group_blocks(cells, (0, NI), PM, PS, None)
    group_halos(LH, RH, EH, PM, PS, lat)
    for copy in share_copies:
        copy.wait()
    total = shares[lat].astype(F32)
    for d in range(1, N_LAT):
        total += parts[d].astype(F32)
    mine[...] = total * GRAD_SCALE

    def spread(block, parts, send_sem, recv_sem):
        made = [
            pltpu.make_async_remote_copy(
                src_ref=block, dst_ref=parts.at[d], send_sem=send_sem.at[d], recv_sem=recv_sem.at[d],
                device_id=(lax.rem(lon + d, N_LON), lat), device_id_type=MESH)
            for d in range(1, N_LON)
        ]
        for copy in made:
            copy.start()
        return made

    last_copies = spread(mine, whole, send_two, recv_two)
    for g in range(NG // 2):
        shift_blocks(PS, Z, g)
        banded_conv(Z, W, AB, S, M, g)
    for copy in tap_copies:
        copy.wait()
    total = tap_shares[lat]
    for d in range(1, N_LAT):
        total += tap_parts[d]
    tap_mine[...] = total * GRAD_SCALE
    last_copies += spread(tap_mine, tap_whole, send_last, recv_last)
    for g in range(NG // 2, NG):
        shift_blocks(PS, Z, g)
        banded_conv(Z, W, AB, S, M, g)
    for copy in last_copies:
        copy.wait()
    total, tap_total = mine[...], tap_mine[...]
    for d in range(1, N_LON):
        total += whole[d]
        tap_total += tap_whole[d]
    total_out[0:80] = total
    total_out[80:88] = tap_total


def backward_conv(d_conv, fields, lon_halo, left_halo, right_halo, land, w, shares):
    dma = pltpu.SemaphoreType.DMA
    scratch = halo_scratch()
    scratch.pop(11)
    return pl.pallas_call(
        grad_kernel,
        name="backward_conv",
        out_shape=(pltpu.VMEM((NG, NI, 64, 128), BF16), pltpu.VMEM((88, C), F32)),
        in_specs=vmem(8),
        out_specs=tuple(vmem(2)),
        scratch_shapes=scratch
        + [
            pltpu.VMEM((NG, NI, ZR, 256), BF16),
            pltpu.VMEM((2, 2, 256, 512), F32),
            pltpu.VMEM((NG, 56, 128), F32),
            pltpu.VMEM((128, 128), F32),
            pltpu.VMEM((N_LAT, 8, 128), F32),
            pltpu.VMEM((N_LAT, 80, 128), BF16),
            pltpu.VMEM((N_LAT, 8, 128), F32),
            pltpu.VMEM((80, 128), F32),
            pltpu.VMEM((N_LON, 80, 128), F32),
            pltpu.VMEM((8, 128), F32),
            pltpu.VMEM((N_LON, 8, 128), F32),
            dma((8,)), dma((8,)), dma((N_LAT,)), dma((N_LAT,)), dma((N_LAT,)), dma((N_LAT,)),
            dma((N_LON,)), dma((N_LON,)), dma((N_LON,)), dma((N_LON,)),
        ],
        compiler_params=pltpu.CompilerParams(collective_id=1, has_side_effects=True, vmem_limit_bytes=VMEM_LIMIT),
    )(d_conv, fields, lon_halo, left_halo, right_halo, land, w, shares)


def finish_kernel(place, S, up, total, grad_input, out_win, out_wout, out_dw, out_channel, out_bin,
                  made, PM, store):
    copies = [
        pltpu.make_async_copy(made.at[n], grad_input.at[pl.ds(32 * n, 32)], store.at[n]) for n in range(3)
    ]
    build_permutation(PM)
    lat = place[0]
    out_win[...] = total[0:32]
    out_wout[...] = total[32:64]
    small = total[64:72]
    out_bin[...] = pltpu.roll(small, lax.rem(128 - 32 * lax.rem(lat, 4), 128), axis=1)[0:1, 0:32]
    out_channel[...] = pltpu.roll(small, lax.rem(128 - 8 * lat, 128), axis=1)[1:6, 0:8]
    out_dw[...] = total[80:88, 0:49]
    for chunk in range(3):

        def put(n, both, chunk=chunk):
            for m in range(4):
                for h in range(2):
                    at = 8 * m + 2 * n + h
                    value = up[32 * chunk + at].astype(F32) + both[64 * m : 64 * m + 64, 128 * h : 128 * h + 128]
                    made[chunk, at] = value.astype(BF16)

        ungroup(S, PM, range(4 * chunk, 4 * chunk + 4), put)
        copies[chunk].start()
    for copy in copies:
        copy.wait()


def finish(place, S, upstream, total):
    dma = pltpu.SemaphoreType.DMA
    return pl.pallas_call(
        finish_kernel,
        name="finish",
        out_shape=(
            jax.ShapeDtypeStruct((CLON, CLAT, C), BF16),
            jax.ShapeDtypeStruct((32, C), F32),
            jax.ShapeDtypeStruct((32, C), F32),
            jax.ShapeDtypeStruct((8, 49), F32),
            jax.ShapeDtypeStruct((5, 8), F32),
            jax.ShapeDtypeStruct((1, 32), F32),
        ),
        in_specs=[pl.BlockSpec(memory_space=pltpu.SMEM)] + vmem(3),
        out_specs=tuple(hbm(1) + vmem(5)),
        scratch_shapes=[
            pltpu.VMEM((3, 32, CLAT, C), BF16),
            pltpu.VMEM((1024, 1024), BF16),
            dma((3,)),
        ],
        compiler_params=pltpu.CompilerParams(vmem_limit_bytes=VMEM_LIMIT),
    )(place, S, upstream, total)


def per_device(fields, land_sea, tile_list, upstream, dw_weight, dw_bias, ln_gain, ln_bias, w_in, b_in, w_out, b_out,
               layer_scale):
    def row(v):
        return v.reshape(1, -1)

    fours = fields.reshape(24, 4, CLAT, C)
    land = land_sea.T
    far = [pltpu.with_memory_space_constraint(v, pltpu.HBM) for v in (fours, upstream, w_in, w_out, land, dw_weight)]
    conv, lon_halo, left_halo, right_halo, near_fours, near_up, near_in, near_out = forward_conv(*far)
    mixed, d_conv, shares = listed_mlp(
        tile_list.reshape(-1), conv, near_fours, near_up, land, row(dw_bias), row(ln_gain), row(ln_bias), near_in, row(b_in), near_out,
        row(b_out), row(layer_scale))
    grouped, total = backward_conv(d_conv, near_fours, lon_halo, left_halo, right_halo, land, dw_weight, shares)
    place = lax.axis_index("lat").astype(jnp.int32).reshape(1)
    grad_input, g_win, g_wout, g_dw, g_channel, g_bin = finish(place, grouped, near_up, total)
    return mixed, grad_input, g_win.T, g_wout, g_dw.T, g_channel, g_bin.reshape(-1)


def solution(mesh):
    cells = P("lon", "lat", None)
    return jax.shard_map(
        per_device,
        mesh=mesh,
        in_specs=(cells, P("lon", "lat"), cells, cells) + (P(),) * 9,
        out_specs=(cells, cells, P(None, "lat"), P("lat", None), P(None, "lat"), P(None, "lat"), P("lat")),
        check_vma=False,
    )
```

```python
import functools
import math

import jax
import jax.numpy as jnp
from jax import lax
from jax.experimental import pallas as pl
from jax.experimental.pallas import tpu as pltpu
from jax.sharding import PartitionSpec as P

LN_EPSILON = 1e-06
MESH = pl.DeviceIdType.MESH
F32 = jnp.float32
BF16 = jnp.bfloat16
CLON, CLAT, C, FF = 96, 64, 128, 512
NI, NJ = CLON // 8, CLAT // 8
TILES = NI * NJ
TCAP = 72
NG = 8
ZR = 80
N_LON, N_LAT = 8, 16
SHIFTS = (-4, -2, 0, 2)
GRAD_SCALE = 1.0 / math.sqrt(768 * 1024)
VMEM_LIMIT = 34 * 1024 * 1024
ERF_COEFS = (0.7978697125817803, 0.03639228534613075, -8.782596074631976e-05, -3.669357312826199e-05,
             1.4250137713525853e-06)
PDF_SCALE = -0.5 / math.log(2.0)
PDF_SHIFT = -0.5 * math.log2(2.0 * math.pi)


def iota(shape, dim):
    return lax.broadcasted_iota(jnp.int32, shape, dim)


def build_weights(w_ref, W, flip):
    q_row, q_col = iota((56, 49), 0), iota((56, 49), 1)
    a, b = q_row // 8, q_row % 8
    tap = (6 - a) * 7 + (6 - b) if flip else a * 7 + b
    pick = jnp.where((q_col == tap) & (b < 7), 1.0, 0.0).astype(BF16)
    taps = jnp.dot(pick, w_ref[...].astype(BF16), preferred_element_type=F32).astype(BF16)
    lane_i = iota((8, 128), 1) // 16
    same = (iota((16, 128), 0) == iota((16, 128), 1) % 16).astype(F32)

    def group(g):
        spread = jnp.where(iota((128, 128), 0) == 16 * g + iota((128, 128), 1) % 16, 1.0, 0.0).astype(BF16)
        rep = jnp.dot(taps, spread, preferred_element_type=F32)
        for i_in in range(16):
            v = jnp.zeros((8, 128), F32)
            for a in range(7):
                if 0 <= i_in - 1 - a < 8:
                    v = jnp.where(lane_i == i_in - 1 - a, rep[8 * a : 8 * a + 8], v)
            base = (i_in // 8) * 512 + (i_in % 8) * 16
            W[g, base : base + 16, 0:128] = jnp.zeros((16, 128), BF16)
            for b in range(7):
                parity = (b + 1) % 2
                e = (b - 3 - parity + 4) // 2
                row = jnp.broadcast_to(v[b : b + 1], (16, 128)) * same
                W[g, base + 128 * e : base + 128 * e + 16, 128 * parity : 128 * parity + 128] = row.astype(BF16)

    for g in range(NG):
        group(g)


def build_permutation(PM):
    def clear(n, carry):
        PM[pl.ds(pl.multiple_of(64 * n, 64), 64), :] = jnp.zeros((64, 1024), BF16)
        return carry

    lax.fori_loop(0, 16, clear, 0)
    row, lane = iota((16, 128), 0), iota((16, 128), 1)
    for p in range(8):
        unit = jnp.where(lane == 16 * p + row, 1.0, 0.0).astype(BF16)
        for q in range(8):
            PM[128 * p + 16 * q : 128 * p + 16 * q + 16, 128 * q : 128 * q + 128] = unit


def expand_mask(land_ext, M, count):
    value = land_ext.astype(BF16)
    row, block = iota((128, 128), 0), iota((128, 128), 1) // 16

    for k in range(count):
        pick = jnp.where(row == 8 * k + block, 1.0, 0.0).astype(BF16)
        M[k] = jnp.dot(value, pick, preferred_element_type=F32)


def with_ones(land_t):
    lane = iota((CLAT, 128), 1)
    return jnp.where((lane < 4) | (lane >= CLON + 4), 1.0, pltpu.roll(land_t, 4, axis=1))


def pack_edges(X, EL, ER, masks):
    low = iota((8, 128), 0) < 4

    def block(n, carry):
        for east, E in ((0, EL), (1, ER)):
            out = []
            keep = None if masks is None else pltpu.roll(masks[east], lax.rem(128 - 8 * n, 128), axis=1)
            for m in range(4):
                pair = []
                for i in (2 * m, 2 * m + 1):
                    cells = X[2 * n + i // 4, i % 4, 48 * east : 48 * east + 16].astype(F32)
                    pair.append(cells[8 * east : 8 * east + 8])
                if east:
                    value = jnp.where(low, pltpu.roll(pair[0], 4, axis=0), pair[1])
                else:
                    value = jnp.where(low, pair[0], pltpu.roll(pair[1], 4, axis=0))
                if keep is not None:
                    value = value * jnp.broadcast_to(keep[:, 2 * m : 2 * m + 1], (8, 128))
                out.append(value)
            E[n] = jnp.concatenate(out, axis=0).astype(BF16)
        return carry

    lax.fori_loop(0, NI, block, 0)


def halo_copies(first, last, XH, EL, ER, LH, RH, send, recv, lon, lat):
    up, down = lax.rem(lon + 1, N_LON), lax.rem(lon + N_LON - 1, N_LON)
    east, west = lax.rem(lat + 1, N_LAT), lax.rem(lat + N_LAT - 1, N_LAT)
    plan = (
        (EL, RH.at[pl.ds(1, NI)], (lon, west)),
        (ER, LH.at[pl.ds(1, NI)], (lon, east)),
        (first, XH.at[1], (down, lat)),
        (last, XH.at[0], (up, lat)),
        (EL.at[0, pl.ds(0, 16)], RH.at[13, pl.ds(0, 16)], (down, west)),
        (EL.at[NI - 1, pl.ds(16, 16)], RH.at[0, pl.ds(16, 16)], (up, west)),
        (ER.at[0, pl.ds(0, 16)], LH.at[13, pl.ds(0, 16)], (down, east)),
        (ER.at[NI - 1, pl.ds(16, 16)], LH.at[0, pl.ds(16, 16)], (up, east)),
    )
    return [
        pltpu.make_async_remote_copy(
            src_ref=src, dst_ref=dst, send_sem=send.at[n], recv_sem=recv.at[n], device_id=where, device_id_type=MESH
        )
        for n, (src, dst, where) in enumerate(plan)
    ]


def neighbours(lon, lat):
    up, down = lax.rem(lon + 1, N_LON), lax.rem(lon + N_LON - 1, N_LON)
    east, west = lax.rem(lat + 1, N_LAT), lax.rem(lat + N_LAT - 1, N_LAT)
    return [(lon, west), (lon, east), (down, lat), (up, lat), (down, west), (up, west), (down, east), (up, east)]


def greet(places):
    barrier = pltpu.get_barrier_semaphore()
    for place in places:
        pl.semaphore_signal(barrier, inc=1, device_id=place, device_id_type=MESH)


def greeted(places):
    pl.semaphore_wait(pltpu.get_barrier_semaphore(), len(places))


def clear_margins(PS):
    def block(k, carry):
        PS[:, k, 8:16] = jnp.zeros((NG, 8, 128), F32)
        PS[:, k, 80:104] = jnp.zeros((NG, 24, 128), F32)
        return carry

    lax.fori_loop(0, NI + 1, block, 0)


def padded_cells(X, XH):
    def cells(k, i):
        at = 2 * k + i // 4 - 1
        if at < 0:
            return XH[0, i]
        return XH[1, i - 4] if at > 23 else X[at, i % 4]

    return cells


def group_blocks(cells, blocks, PM, PS, M):
    lhs = jnp.concatenate([jnp.concatenate([cells(k, i) for k in blocks], axis=0) for i in range(8)], axis=1)

    for n in range(NG // 2):
        both = jnp.dot(lhs, PM[:, 256 * n : 256 * n + 256], preferred_element_type=F32)
        for h in range(2):
            for m, k in enumerate(blocks):
                part = both[64 * m : 64 * m + 64, 128 * h : 128 * h + 128]
                PS[2 * n + h, k, 16:80] = part if M is None else part * M[k]


def group_halos(LH, RH, EH, PM, PS, lat):
    low = iota((8, 128), 0) < 4
    keep = jnp.where(low, jnp.where(lat < N_LAT - 1, 1.0, 0.0), jnp.where(lat > 0, 1.0, 0.0))

    def rows_of(k):
        rows = []
        for m in range(4):
            at = (16, 24, 0, 8)[m]
            left = LH[k + m // 2, at // 16 * 16 : at // 16 * 16 + 16].astype(F32)[at % 16 : at % 16 + 8]
            right = RH[k + m // 2, at // 16 * 16 : at // 16 * 16 + 16].astype(F32)[at % 16 : at % 16 + 8]
            rows.append(jnp.where(low, right, pltpu.roll(left, 4, axis=0)) * keep)
            rows.append(jnp.where(low, pltpu.roll(right, 4, axis=0), left) * keep)
        return rows

    for n in range(7):
        first = rows_of(2 * n)
        second = rows_of(2 * n + 1) if 2 * n + 1 <= NI else first
        for i in range(8):
            EH[n, :, 128 * i : 128 * i + 128] = jnp.concatenate([first[i], second[i]], axis=0).astype(BF16)

    edges = EH[...].reshape(112, 1024)
    for n in range(NG // 2):
        both = jnp.dot(edges, PM[:, 256 * n : 256 * n + 256], preferred_element_type=F32)
        for h in range(2):
            for k in range(NI + 1):
                part = both[8 * k : 8 * k + 8, 128 * h : 128 * h + 128]
                PS[2 * n + h, k, 8:16] = part
                PS[2 * n + h, k, 80:88] = part


def shift_blocks(PS, Z, g):
    for k in range(NI + 1):
        for e, shift in enumerate(SHIFTS):
            Z[g, k, :, 128 * e : 128 * e + 128] = PS[g, k, 16 + shift : 16 + shift + ZR].astype(BF16)


INNER = ((1, 2, 3, 4), (5, 6, 7, 8), (9, 10, 11))


def banded_conv(Z, W, AB, S, M, g):
    lhs = jnp.concatenate([Z[g, 0:NI].reshape(NI * ZR, 512), Z[g, 1 : NI + 1].reshape(NI * ZR, 512)], axis=1)
    both = jnp.dot(lhs, W[g], preferred_element_type=F32)
    AB[g % 2] = both[:, 128:256]
    for n in range(NI):
        value = both[n * ZR : n * ZR + 64, 0:128] + AB[g % 2, n * ZR + 1 : n * ZR + 65]
        S[g, n] = (value if M is None else value * M[n]).astype(BF16)


def ungroup(S, PM, blocks, put):
    rows = [jnp.concatenate([S[g, k] for k in blocks], axis=0) for g in range(NG)]
    lhs = jnp.concatenate(rows, axis=1)
    for n in range(NG // 2):
        put(n, jnp.dot(lhs, PM[:, 256 * n : 256 * n + 256], preferred_element_type=F32))


def conv_kernel(fields, upstream, w_in, w_out, land_far, w_far,
                conv_out, Z, X, near_up, near_in, near_out,
                land, w, EX, XH, EL, ER, LH, RH, EH, PS, W, PM, AB, S, M, land_pad, send, recv, load):
    lon, lat = lax.axis_index("lon"), lax.axis_index("lat")
    around = neighbours(lon, lat)
    greet(around)
    pairs = ((land_far, land), (fields, X), (w_far, w), (upstream, near_up), (w_in, near_in), (w_out, near_out))
    loads = [pltpu.make_async_copy(far, near, load.at[n]) for n, (far, near) in enumerate(pairs)]
    for copy in loads:
        copy.start()
    land_pad[...] = jnp.zeros((CLAT, 128), F32)
    loads[0].wait()
    land_pad[:, 0:CLON] = land[...].astype(F32)
    land_t = land_pad[...]
    expand_mask(with_ones(land_t), M, NI + 1)
    low = iota((8, 128), 0) < 4
    masks = []
    for east in range(2):
        edge = land_pad[56 * east : 56 * east + 8]
        turned = pltpu.roll(edge, 4, axis=0)
        edge = jnp.where(low, turned, edge) if east else jnp.where(low, edge, turned)
        masks.append(jnp.where(low, edge, pltpu.roll(edge, 127, axis=1)))
    loads[1].wait()
    pack_edges(X, EL, ER, masks)
    for at, first in ((0, 0), (23, CLON - 4)):
        for i in range(4):
            keep = jnp.broadcast_to(land_t[:, first + i : first + i + 1], (CLAT, C))
            EX[at // 23, i] = (X[at, i].astype(F32) * keep).astype(BF16)
    greeted(around)
    copies = halo_copies(EX.at[0], EX.at[1], XH, EL, ER, LH, RH, send, recv, lon, lat)
    for copy in copies:
        copy.start()
    build_permutation(PM)
    clear_margins(PS)
    cells = padded_cells(X, XH)

    for blocks in INNER:
        group_blocks(cells, blocks, PM, PS, M)
    loads[2].wait()
    build_weights(w, W, False)
    for copy in copies:
        copy.wait()
    group_blocks(cells, (0, NI), PM, PS, M)
    group_halos(LH, RH, EH, PM, PS, lat)
    for g in range(NG):
        shift_blocks(PS, Z, g)
        banded_conv(Z, W, AB, S, None, g)
    for first in range(0, NI, 4):

        def put(n, both, first=first):
            for m in range(4):
                for t in range(NJ):
                    at = 64 * m + 8 * t
                    value = jnp.concatenate([both[at : at + 8, 0:128], both[at : at + 8, 128:256]], axis=0)
                    conv_out[(first + m) * NJ + t, 16 * n : 16 * n + 16] = value.astype(BF16)

        ungroup(S, PM, range(first, first + 4), put)
    for copy in loads[3:]:
        copy.wait()


def vmem(n):
    return [pl.BlockSpec(memory_space=pltpu.VMEM)] * n


def hbm(n):
    return [pl.BlockSpec(memory_space=pl.ANY)] * n


def halo_scratch():
    return [
        pltpu.VMEM((2, 4, CLAT, C), BF16),
        pltpu.VMEM((NI, 32, C), BF16),
        pltpu.VMEM((NI, 32, C), BF16),
        pltpu.VMEM((14, 32, C), BF16),
        pltpu.VMEM((14, 32, C), BF16),
        pltpu.VMEM((7, 16, 1024), BF16),
        pltpu.VMEM((NG, NI + 1, 104, 128), F32),
        pltpu.VMEM((NG, 1024, 256), BF16),
        pltpu.VMEM((1024, 1024), BF16),
        pltpu.VMEM((2, NI * ZR, 128), F32),
        pltpu.VMEM((NG, NI, 64, 128), BF16),
        pltpu.VMEM((NI + 1, 64, 128), F32),
        pltpu.VMEM((CLAT, 128), F32),
    ]


def forward_conv(fields, upstream, w_in, w_out, land, w):
    dma = pltpu.SemaphoreType.DMA
    return pl.pallas_call(
        conv_kernel,
        name="forward_conv",
        out_shape=(
            pltpu.VMEM((TILES, 64, C), BF16),
            pltpu.VMEM((NG, NI + 1, ZR, 512), BF16),
            pltpu.VMEM((24, 4, CLAT, C), BF16),
            pltpu.VMEM((CLON, CLAT, C), BF16),
            pltpu.VMEM((C, FF), BF16),
            pltpu.VMEM((FF, C), BF16),
        ),
        in_specs=hbm(6),
        out_specs=tuple(vmem(6)),
        scratch_shapes=[
            pltpu.VMEM((CLAT, CLON), jnp.int32),
            pltpu.VMEM((49, C), F32),
            pltpu.VMEM((2, 4, CLAT, C), BF16),
        ]
        + halo_scratch()
        + [dma((8,)), dma((8,)), dma((6,))],
        compiler_params=pltpu.CompilerParams(collective_id=0, has_side_effects=True, vmem_limit_bytes=VMEM_LIMIT),
    )(fields, upstream, w_in, w_out, land, w)


def normal_cdf(h, square):
    q = jnp.full(h.shape, ERF_COEFS[-1], F32)
    for coef in ERF_COEFS[-2::-1]:
        q = q * square + coef
    return 0.5 + 0.5 * jnp.tanh(h * q)


def mlp_kernel(tile_ids, conv, fields, upstream, land, offset, gain, shift, w_in, b_in, w_out, b_out, scale,
               mixed, d_conv_out, shares, branch, d_conv, w_in_t, w_out_t, g_in, g_out, g_bin, sums, land_tr, mixed_part, store):
    slots = 18
    rows = slots * 64
    land_tr[...] = jnp.zeros((CLAT, 128), F32)
    land_tr[:, 0:CLON] = land[...].astype(F32)
    w_in_t[...] = w_in[...].astype(F32).T.astype(BF16)
    w_out_t[...] = w_out[...].astype(F32).T.astype(BF16)
    branch[...] = jnp.zeros(branch.shape, F32)
    d_conv[...] = jnp.zeros(d_conv.shape, F32)
    for acc in (g_in, g_out, g_bin, sums):
        acc[...] = jnp.zeros(acc.shape, F32)
    gain_row, shift_row, scale_row = gain[...], shift[...], scale[...]

    def step(n, carry):
        ids = [tile_ids[slots * n + q] for q in range(slots)]
        tiles = [jnp.maximum(t, 0) for t in ids]
        conv_parts, up_parts, active_parts = [], [], []
        for q in range(slots):
            t = tiles[q]
            big, small = t // NJ, lax.rem(t, NJ)
            conv_parts.append(conv[t].astype(F32))
            pair = upstream[pl.ds(8 * big, 8), pl.ds(16 * (small // 2), 16), :].astype(F32)
            odd = lax.rem(small, 2) == 1
            up_parts.append(jnp.where(odd, pair[:, 8:16], pair[:, 0:8]).reshape(64, C))
            strip = pltpu.roll(land_tr[pl.ds(8 * small, 8), :], lax.rem(128 - 8 * big, 128), axis=1)
            live = jnp.where(ids[q] >= 0, 1.0, 0.0)
            strip = strip * live
            active_parts += [jnp.broadcast_to(strip[:, i : i + 1], (8, C)) for i in range(8)]
        conv_rows = jnp.concatenate(conv_parts, axis=0) + offset[...]
        up = jnp.concatenate(up_parts, axis=0)
        active = jnp.concatenate(active_parts, axis=0)
        center = conv_rows - jnp.mean(conv_rows, axis=-1, keepdims=True)
        inv_std = lax.rsqrt(jnp.mean(center * center, axis=-1, keepdims=True) + LN_EPSILON)
        normed = center * inv_std
        normed_b = (normed * gain_row + shift_row).astype(BF16)
        hidden = jnp.dot(normed_b, w_in[...], preferred_element_type=F32) + b_in[...]
        square = hidden * hidden
        cdf = normal_cdf(hidden, square)
        activated = (hidden * cdf).astype(BF16)
        output = jnp.dot(activated, w_out[...], preferred_element_type=F32) + b_out[...]
        gate = active * scale_row
        branch_rows = gate * output
        d_out = gate * up
        d_out_b = d_out.astype(BF16)
        g_out[...] += lax.dot_general(d_out_b, activated, (((0,), (0,)), ((), ())), preferred_element_type=F32)
        pdf = jnp.exp2(square * PDF_SCALE + PDF_SHIFT)
        d_hidden = jnp.dot(d_out_b, w_out_t[...], preferred_element_type=F32) * (cdf + hidden * pdf)
        d_hidden_b = d_hidden.astype(BF16)
        g_in[...] += lax.dot_general(normed_b, d_hidden_b, (((0,), (0,)), ((), ())), preferred_element_type=F32)
        g_bin[...] += jnp.sum(d_hidden.reshape(rows // 8, 8, FF), axis=0)
        d_norm = jnp.dot(d_hidden_b, w_in_t[...], preferred_element_type=F32)
        d_scaled = d_norm * gain_row
        d_cells = inv_std * (
            d_scaled
            - jnp.mean(d_scaled, axis=-1, keepdims=True)
            - normed * jnp.mean(d_scaled * normed, axis=-1, keepdims=True)
        )
        for k, term in enumerate((d_cells, d_norm * normed, d_norm, d_out, active * output * up)):
            sums[k] += jnp.sum(term.reshape(rows // 8, 8, C), axis=0)
        for q in range(slots):
            to = jnp.where(ids[q] >= 0, ids[q], TILES)
            branch[to] = branch_rows[64 * q : 64 * q + 64]
            d_conv[to] = d_cells[64 * q : 64 * q + 64]

        return carry

    lax.fori_loop(0, TCAP // slots, step, 0)

    stores = [
        pltpu.make_async_copy(mixed_part.at[n], mixed.at[pl.ds(32 * n, 32)], store.at[n]) for n in range(3)
    ]
    for chunk in range(3):

        def mix(n, carry, chunk=chunk):
            for i in range(8):
                rows_i = jnp.concatenate([branch[n * NJ + t, 8 * i : 8 * i + 8] for t in range(NJ)], axis=0)
                total = fields[2 * n + i // 4, i % 4].astype(F32) + rows_i
                mixed_part[chunk, 8 * (n - 4 * chunk) + i] = total.astype(BF16)
                rows_i = jnp.concatenate([d_conv[n * NJ + t, 8 * i : 8 * i + 8] for t in range(NJ)], axis=0)
                d_conv_out[2 * n + i // 4, i % 4] = rows_i.astype(BF16)
            return carry

        lax.fori_loop(4 * chunk, 4 * chunk + 4, mix, 0)
        stores[chunk].start()
    bin_row = jnp.sum(g_bin[...], axis=0, keepdims=True)
    tail = jnp.concatenate([jnp.sum(sums[k], axis=0, keepdims=True) for k in range(5)], axis=0)
    for n in range(4):
        turned_in = g_in[:, 128 * n : 128 * n + 128].T
        turned_out = g_out[:, 128 * n : 128 * n + 128].T
        for m in range(4):
            q = 4 * n + m
            shares[q, 0:32] = turned_in[32 * m : 32 * m + 32].astype(BF16)
            shares[q, 32:64] = turned_out[32 * m : 32 * m + 32].astype(BF16)
            rest = [bin_row[:, 128 * n : 128 * n + 128], tail, jnp.zeros((10, 128), F32)]
            shares[q, 64:80] = jnp.concatenate(rest, axis=0).astype(BF16)
    for copy in stores:
        copy.wait()


def listed_mlp(tile_ids, conv, fields, upstream, land, offset, gain, shift, w_in, b_in, w_out, b_out, scale):
    return pl.pallas_call(
        mlp_kernel,
        name="listed_mlp",
        out_shape=(
            jax.ShapeDtypeStruct((CLON, CLAT, C), BF16),
            pltpu.VMEM((24, 4, CLAT, C), BF16),
            pltpu.VMEM((N_LAT, 80, 128), BF16),
        ),
        in_specs=[pl.BlockSpec(memory_space=pltpu.SMEM)] + vmem(12),
        out_specs=tuple(hbm(1) + vmem(2)),
        scratch_shapes=[
            pltpu.VMEM((TILES + 1, 64, C), F32),
            pltpu.VMEM((TILES + 1, 64, C), F32),
            pltpu.VMEM((FF, C), BF16),
            pltpu.VMEM((C, FF), BF16),
            pltpu.VMEM((C, FF), F32),
            pltpu.VMEM((C, FF), F32),
            pltpu.VMEM((8, FF), F32),
            pltpu.VMEM((5, 8, C), F32),
            pltpu.VMEM((CLAT, 128), F32),
            pltpu.VMEM((3, 32, CLAT, C), BF16),
            pltpu.SemaphoreType.DMA((3,)),
        ],
        compiler_params=pltpu.CompilerParams(vmem_limit_bytes=VMEM_LIMIT),
    )(tile_ids, conv, fields, upstream, land, offset, gain, shift, w_in, b_in, w_out, b_out, scale)


def pair_rows(PS, MP):
    for g in range(NG):
        for n in range(NI):
            MP[g, n, :, 0:128] = PS[g, n, 16 : 16 + ZR].astype(BF16)
            MP[g, n, :, 128:256] = PS[g, n, 15 : 15 + ZR].astype(BF16)


def tap_gradients(Z, MP, G, taps, groups):
    lane = iota((16, 128), 1)
    same = (iota((16, 128), 0) == lane % 16).astype(F32)
    block = lane // 16
    for g in groups:
        taps[g] = jnp.zeros(taps.shape[1:], F32)
        lhs = MP[g].reshape(NI * ZR, 256)
        for half in range(2):
            rhs = Z[g, half : half + NI].reshape(NI * ZR, 512)
            G[g % 2, half] = lax.dot_general(lhs, rhs, (((0,), (0,)), ((), ())), preferred_element_type=F32)
        for e in range(4):
            for parity in range(2):
                b = 3 + SHIFTS[e] + parity
                if not 0 <= b < 7:
                    continue
                for a in range(7):
                    total = None
                    for i_out in range(8):
                        half, k = divmod(i_out + a + 1, 8)
                        at = 128 * parity + 16 * i_out
                        piece = G[g % 2, half, at : at + 16, 128 * e : 128 * e + 128]
                        total = piece if total is None else jnp.where(block == k, piece, total)
                    taps[g, 7 * a + b : 7 * a + b + 1] = jnp.sum(total * same, axis=0, keepdims=True)


def gather_taps(taps, square, tap_shares):
    total = jnp.zeros((56, 128), F32)
    for g in range(NG):
        row, col = iota((128, 128), 0), iota((128, 128), 1)
        pick = jnp.where((col // 16 == g) & (row % 16 == col % 16), 1.0, 0.0).astype(BF16)
        value = taps[g]
        head = value.astype(BF16)
        tail = (value - head.astype(F32)).astype(BF16)
        total += jnp.dot(head, pick, preferred_element_type=F32) + jnp.dot(tail, pick, preferred_element_type=F32)
    square[...] = jnp.zeros((128, 128), F32)
    square[0:56] = total
    turned = square[...].T
    for q in range(N_LAT):
        tap_shares[q] = turned[8 * q : 8 * q + 8]


def grad_kernel(d_conv, ZM, land, w, shares,
                S, total_out,
                XH, EL, ER, LH, RH, EH, PS, W, PM, AB, M, land_pad,
                Z, MP, G, taps, square, tap_shares, parts, tap_parts, mine, whole, tap_mine, tap_whole,
                send, recv, send_one, recv_one, send_tap, recv_tap, send_two, recv_two, send_last, recv_last):
    lon, lat = lax.axis_index("lon"), lax.axis_index("lat")
    around = neighbours(lon, lat)
    around += [(lon, lax.rem(lat + d, N_LAT)) for d in range(2, N_LAT - 1)]
    around += [(lax.rem(lon + d, N_LON), lat) for d in range(2, N_LON - 1)]
    greet(around)
    pack_edges(d_conv, EL, ER, None)
    build_permutation(PM)
    clear_margins(PS)
    build_weights(w, W, True)
    land_pad[...] = jnp.zeros((CLAT, 128), F32)
    land_pad[:, 0:CLON] = land[...].astype(F32)
    expand_mask(land_pad[...], M, NI)
    greeted(around)
    copies = halo_copies(d_conv.at[0], d_conv.at[23], XH, EL, ER, LH, RH, send, recv, lon, lat)
    for copy in copies:
        copy.start()
    share_copies, tap_copies = [], []
    for d in range(1, N_LAT):
        to = lax.rem(lat + d, N_LAT)
        share_copies.append(pltpu.make_async_remote_copy(
            src_ref=shares.at[to], dst_ref=parts.at[d], send_sem=send_one.at[d], recv_sem=recv_one.at[d],
            device_id=(lon, to), device_id_type=MESH))
        tap_copies.append(pltpu.make_async_remote_copy(
            src_ref=tap_shares.at[to], dst_ref=tap_parts.at[d], send_sem=send_tap.at[d], recv_sem=recv_tap.at[d],
            device_id=(lon, to), device_id_type=MESH))
    for copy in share_copies:
        copy.start()
    for blocks in ((0, 1, 2, 3), (4, 5, 6, 7), (8, 9, 10, 11)):
        group_blocks(lambda k, i: d_conv[2 * k + i // 4, i % 4], blocks, PM, PS, None)
    pair_rows(PS, MP)
    for g in range(NG):
        tap_gradients(ZM, MP, G, taps, (g,))
    gather_taps(taps, square, tap_shares)
    for copy in tap_copies:
        copy.start()
    cells = padded_cells(d_conv, XH)
    for blocks in INNER:
        group_blocks(cells, blocks, PM, PS, None)
    for copy in copies:
        copy.wait()
    group_blocks(cells, (0, NI), PM, PS, None)
    group_halos(LH, RH, EH, PM, PS, lat)
    for copy in share_copies:
        copy.wait()
    total = shares[lat].astype(F32)
    for d in range(1, N_LAT):
        total += parts[d].astype(F32)
    mine[...] = total * GRAD_SCALE

    def spread(block, parts, send_sem, recv_sem):
        made = [
            pltpu.make_async_remote_copy(
                src_ref=block, dst_ref=parts.at[d], send_sem=send_sem.at[d], recv_sem=recv_sem.at[d],
                device_id=(lax.rem(lon + d, N_LON), lat), device_id_type=MESH)
            for d in range(1, N_LON)
        ]
        for copy in made:
            copy.start()
        return made

    last_copies = spread(mine, whole, send_two, recv_two)
    for g in range(2):
        shift_blocks(PS, Z, g)
        banded_conv(Z, W, AB, S, M, g)
    for copy in tap_copies:
        copy.wait()
    total = tap_shares[lat]
    for d in range(1, N_LAT):
        total += tap_parts[d]
    tap_mine[...] = total * GRAD_SCALE
    last_copies += spread(tap_mine, tap_whole, send_last, recv_last)
    for g in range(2, NG):
        shift_blocks(PS, Z, g)
        banded_conv(Z, W, AB, S, M, g)
    for copy in last_copies:
        copy.wait()
    total, tap_total = mine[...], tap_mine[...]
    for d in range(1, N_LON):
        total += whole[d]
        tap_total += tap_whole[d]
    total_out[0:80] = total
    total_out[80:88] = tap_total


def backward_conv(d_conv, shifted, land, w, shares):
    dma = pltpu.SemaphoreType.DMA
    scratch = halo_scratch()
    scratch.pop(10)
    return pl.pallas_call(
        grad_kernel,
        name="backward_conv",
        out_shape=(pltpu.VMEM((NG, NI, 64, 128), BF16), pltpu.VMEM((88, C), F32)),
        in_specs=vmem(5),
        out_specs=tuple(vmem(2)),
        scratch_shapes=scratch
        + [
            pltpu.VMEM((NG, NI + 1, ZR, 512), BF16),
            pltpu.VMEM((NG, NI, ZR, 256), BF16),
            pltpu.VMEM((2, 2, 256, 512), F32),
            pltpu.VMEM((NG, 56, 128), F32),
            pltpu.VMEM((128, 128), F32),
            pltpu.VMEM((N_LAT, 8, 128), F32),
            pltpu.VMEM((N_LAT, 80, 128), BF16),
            pltpu.VMEM((N_LAT, 8, 128), F32),
            pltpu.VMEM((80, 128), F32),
            pltpu.VMEM((N_LON, 80, 128), F32),
            pltpu.VMEM((8, 128), F32),
            pltpu.VMEM((N_LON, 8, 128), F32),
            dma((8,)), dma((8,)), dma((N_LAT,)), dma((N_LAT,)), dma((N_LAT,)), dma((N_LAT,)),
            dma((N_LON,)), dma((N_LON,)), dma((N_LON,)), dma((N_LON,)),
        ],
        compiler_params=pltpu.CompilerParams(collective_id=1, has_side_effects=True, vmem_limit_bytes=VMEM_LIMIT),
    )(d_conv, shifted, land, w, shares)


def finish_kernel(place, S, up, total, grad_input, out_win, out_wout, out_dw, out_channel, out_bin,
                  made, PM, store):
    copies = [
        pltpu.make_async_copy(made.at[n], grad_input.at[pl.ds(32 * n, 32)], store.at[n]) for n in range(3)
    ]
    build_permutation(PM)
    lat = place[0]
    out_win[...] = total[0:32]
    out_wout[...] = total[32:64]
    small = total[64:72]
    out_bin[...] = pltpu.roll(small, lax.rem(128 - 32 * lax.rem(lat, 4), 128), axis=1)[0:1, 0:32]
    out_channel[...] = pltpu.roll(small, lax.rem(128 - 8 * lat, 128), axis=1)[1:6, 0:8]
    out_dw[...] = total[80:88, 0:49]
    for chunk in range(3):

        def put(n, both, chunk=chunk):
            for m in range(4):
                for h in range(2):
                    at = 8 * m + 2 * n + h
                    value = up[32 * chunk + at].astype(F32) + both[64 * m : 64 * m + 64, 128 * h : 128 * h + 128]
                    made[chunk, at] = value.astype(BF16)

        ungroup(S, PM, range(4 * chunk, 4 * chunk + 4), put)
        copies[chunk].start()
    for copy in copies:
        copy.wait()


def finish(place, S, upstream, total):
    dma = pltpu.SemaphoreType.DMA
    return pl.pallas_call(
        finish_kernel,
        name="finish",
        out_shape=(
            jax.ShapeDtypeStruct((CLON, CLAT, C), BF16),
            jax.ShapeDtypeStruct((32, C), F32),
            jax.ShapeDtypeStruct((32, C), F32),
            jax.ShapeDtypeStruct((8, 49), F32),
            jax.ShapeDtypeStruct((5, 8), F32),
            jax.ShapeDtypeStruct((1, 32), F32),
        ),
        in_specs=[pl.BlockSpec(memory_space=pltpu.SMEM)] + vmem(3),
        out_specs=tuple(hbm(1) + vmem(5)),
        scratch_shapes=[
            pltpu.VMEM((3, 32, CLAT, C), BF16),
            pltpu.VMEM((1024, 1024), BF16),
            dma((3,)),
        ],
        compiler_params=pltpu.CompilerParams(vmem_limit_bytes=VMEM_LIMIT),
    )(place, S, upstream, total)


def per_device(fields, land_sea, tile_list, upstream, dw_weight, dw_bias, ln_gain, ln_bias, w_in, b_in, w_out, b_out,
               layer_scale):
    def row(v):
        return v.reshape(1, -1)

    fours = fields.reshape(24, 4, CLAT, C)
    land = land_sea.T
    far = [pltpu.with_memory_space_constraint(v, pltpu.HBM) for v in (fours, upstream, w_in, w_out, land, dw_weight)]
    conv, shifted, near_fours, near_up, near_in, near_out = forward_conv(*far)
    mixed, d_conv, shares = listed_mlp(
        tile_list.reshape(-1), conv, near_fours, near_up, land, row(dw_bias), row(ln_gain), row(ln_bias), near_in, row(b_in), near_out,
        row(b_out), row(layer_scale))
    grouped, total = backward_conv(d_conv, shifted, land, dw_weight, shares)
    place = lax.axis_index("lat").astype(jnp.int32).reshape(1)
    grad_input, g_win, g_wout, g_dw, g_channel, g_bin = finish(place, grouped, near_up, total)
    return mixed, grad_input, g_win.T, g_wout, g_dw.T, g_channel, g_bin.reshape(-1)


def solution(mesh):
    cells = P("lon", "lat", None)
    return jax.shard_map(
        per_device,
        mesh=mesh,
        in_specs=(cells, P("lon", "lat"), cells, cells) + (P(),) * 9,
        out_specs=(cells, cells, P(None, "lat"), P("lat", None), P(None, "lat"), P(None, "lat"), P("lat")),
        check_vma=False,
    )
```

```python
import functools
import math

import jax
import jax.numpy as jnp
from jax import lax
from jax.experimental import pallas as pl
from jax.experimental.pallas import tpu as pltpu
from jax.sharding import PartitionSpec as P

LN_EPSILON = 1e-06
MESH = pl.DeviceIdType.MESH
F32 = jnp.float32
BF16 = jnp.bfloat16
CLON, CLAT, C, FF = 96, 64, 128, 512
NI, NJ = CLON // 8, CLAT // 8
TILES = NI * NJ
TCAP = 72
NG = 8
ZR = 80
N_LON, N_LAT = 8, 16
SHIFTS = (-4, -2, 0, 2)
GRAD_SCALE = 1.0 / math.sqrt(768 * 1024)
VMEM_LIMIT = 34 * 1024 * 1024
ERF_COEFS = (0.7978697125817803, 0.03639228534613075, -8.782596074631976e-05, -3.669357312826199e-05,
             1.4250137713525853e-06)
PDF_SCALE = -0.5 / math.log(2.0)
PDF_SHIFT = -0.5 * math.log2(2.0 * math.pi)


def iota(shape, dim):
    return lax.broadcasted_iota(jnp.int32, shape, dim)


def build_weights(w_ref, W, flip):
    q_row, q_col = iota((56, 49), 0), iota((56, 49), 1)
    a, b = q_row // 8, q_row % 8
    tap = (6 - a) * 7 + (6 - b) if flip else a * 7 + b
    pick = jnp.where((q_col == tap) & (b < 7), 1.0, 0.0).astype(BF16)
    taps = jnp.dot(pick, w_ref[...].astype(BF16), preferred_element_type=F32).astype(BF16)
    lane_i = iota((8, 128), 1) // 16
    same = (iota((16, 128), 0) == iota((16, 128), 1) % 16).astype(F32)

    def group(g):
        spread = jnp.where(iota((128, 128), 0) == 16 * g + iota((128, 128), 1) % 16, 1.0, 0.0).astype(BF16)
        rep = jnp.dot(taps, spread, preferred_element_type=F32)
        for i_in in range(16):
            v = jnp.zeros((8, 128), F32)
            for a in range(7):
                if 0 <= i_in - 1 - a < 8:
                    v = jnp.where(lane_i == i_in - 1 - a, rep[8 * a : 8 * a + 8], v)
            base = (i_in // 8) * 512 + (i_in % 8) * 16
            W[g, base : base + 16, 0:128] = jnp.zeros((16, 128), BF16)
            for b in range(7):
                parity = (b + 1) % 2
                e = (b - 3 - parity + 4) // 2
                row = jnp.broadcast_to(v[b : b + 1], (16, 128)) * same
                W[g, base + 128 * e : base + 128 * e + 16, 128 * parity : 128 * parity + 128] = row.astype(BF16)

    for g in range(NG):
        group(g)


def build_permutation(PM):
    def clear(n, carry):
        PM[pl.ds(pl.multiple_of(64 * n, 64), 64), :] = jnp.zeros((64, 1024), BF16)
        return carry

    lax.fori_loop(0, 16, clear, 0)
    row, lane = iota((16, 128), 0), iota((16, 128), 1)
    for p in range(8):
        unit = jnp.where(lane == 16 * p + row, 1.0, 0.0).astype(BF16)
        for q in range(8):
            PM[128 * p + 16 * q : 128 * p + 16 * q + 16, 128 * q : 128 * q + 128] = unit


def expand_mask(land_ext, M, count):
    value = land_ext.astype(BF16)
    row, block = iota((128, 128), 0), iota((128, 128), 1) // 16

    for k in range(count):
        pick = jnp.where(row == 8 * k + block, 1.0, 0.0).astype(BF16)
        M[k] = jnp.dot(value, pick, preferred_element_type=F32)


def with_ones(land_t):
    lane = iota((CLAT, 128), 1)
    return jnp.where((lane < 4) | (lane >= CLON + 4), 1.0, pltpu.roll(land_t, 4, axis=1))


def pack_edges(X, EL, ER, masks):
    low = iota((8, 128), 0) < 4

    def block(n, carry):
        for east, E in ((0, EL), (1, ER)):
            out = []
            keep = None if masks is None else pltpu.roll(masks[east], lax.rem(128 - 8 * n, 128), axis=1)
            for m in range(4):
                pair = []
                for i in (2 * m, 2 * m + 1):
                    cells = X[2 * n + i // 4, i % 4, 48 * east : 48 * east + 16].astype(F32)
                    pair.append(cells[8 * east : 8 * east + 8])
                if east:
                    value = jnp.where(low, pltpu.roll(pair[0], 4, axis=0), pair[1])
                else:
                    value = jnp.where(low, pair[0], pltpu.roll(pair[1], 4, axis=0))
                if keep is not None:
                    value = value * jnp.broadcast_to(keep[:, 2 * m : 2 * m + 1], (8, 128))
                out.append(value)
            E[n] = jnp.concatenate(out, axis=0).astype(BF16)
        return carry

    lax.fori_loop(0, NI, block, 0)


def halo_copies(first, last, XH, EL, ER, LH, RH, send, recv, lon, lat):
    up, down = lax.rem(lon + 1, N_LON), lax.rem(lon + N_LON - 1, N_LON)
    east, west = lax.rem(lat + 1, N_LAT), lax.rem(lat + N_LAT - 1, N_LAT)
    plan = (
        (EL, RH.at[pl.ds(1, NI)], (lon, west)),
        (ER, LH.at[pl.ds(1, NI)], (lon, east)),
        (first, XH.at[1], (down, lat)),
        (last, XH.at[0], (up, lat)),
        (EL.at[0, pl.ds(0, 16)], RH.at[13, pl.ds(0, 16)], (down, west)),
        (EL.at[NI - 1, pl.ds(16, 16)], RH.at[0, pl.ds(16, 16)], (up, west)),
        (ER.at[0, pl.ds(0, 16)], LH.at[13, pl.ds(0, 16)], (down, east)),
        (ER.at[NI - 1, pl.ds(16, 16)], LH.at[0, pl.ds(16, 16)], (up, east)),
    )
    return [
        pltpu.make_async_remote_copy(
            src_ref=src, dst_ref=dst, send_sem=send.at[n], recv_sem=recv.at[n], device_id=where, device_id_type=MESH
        )
        for n, (src, dst, where) in enumerate(plan)
    ]


def neighbours(lon, lat):
    up, down = lax.rem(lon + 1, N_LON), lax.rem(lon + N_LON - 1, N_LON)
    east, west = lax.rem(lat + 1, N_LAT), lax.rem(lat + N_LAT - 1, N_LAT)
    return [(lon, west), (lon, east), (down, lat), (up, lat), (down, west), (up, west), (down, east), (up, east)]


def greet(places):
    barrier = pltpu.get_barrier_semaphore()
    for place in places:
        pl.semaphore_signal(barrier, inc=1, device_id=place, device_id_type=MESH)


def greeted(places):
    pl.semaphore_wait(pltpu.get_barrier_semaphore(), len(places))


def clear_margins(PS):
    def block(k, carry):
        PS[:, k, 8:16] = jnp.zeros((NG, 8, 128), F32)
        PS[:, k, 80:104] = jnp.zeros((NG, 24, 128), F32)
        return carry

    lax.fori_loop(0, NI + 1, block, 0)


def padded_cells(X, XH):
    def cells(k, i):
        at = 2 * k + i // 4 - 1
        if at < 0:
            return XH[0, i]
        return XH[1, i - 4] if at > 23 else X[at, i % 4]

    return cells


def group_blocks(cells, blocks, PM, PS, M):
    lhs = jnp.concatenate([jnp.concatenate([cells(k, i) for k in blocks], axis=0) for i in range(8)], axis=1)

    for n in range(NG // 2):
        both = jnp.dot(lhs, PM[:, 256 * n : 256 * n + 256], preferred_element_type=F32)
        for h in range(2):
            for m, k in enumerate(blocks):
                part = both[64 * m : 64 * m + 64, 128 * h : 128 * h + 128]
                PS[2 * n + h, k, 16:80] = part if M is None else part * M[k]


def group_halos(LH, RH, EH, PM, PS, lat):
    low = iota((8, 128), 0) < 4
    keep = jnp.where(low, jnp.where(lat < N_LAT - 1, 1.0, 0.0), jnp.where(lat > 0, 1.0, 0.0))

    def rows_of(k):
        rows = []
        for m in range(4):
            at = (16, 24, 0, 8)[m]
            left = LH[k + m // 2, at // 16 * 16 : at // 16 * 16 + 16].astype(F32)[at % 16 : at % 16 + 8]
            right = RH[k + m // 2, at // 16 * 16 : at // 16 * 16 + 16].astype(F32)[at % 16 : at % 16 + 8]
            rows.append(jnp.where(low, right, pltpu.roll(left, 4, axis=0)) * keep)
            rows.append(jnp.where(low, pltpu.roll(right, 4, axis=0), left) * keep)
        return rows

    for n in range(7):
        first = rows_of(2 * n)
        second = rows_of(2 * n + 1) if 2 * n + 1 <= NI else first
        for i in range(8):
            EH[n, :, 128 * i : 128 * i + 128] = jnp.concatenate([first[i], second[i]], axis=0).astype(BF16)

    edges = EH[...].reshape(112, 1024)
    for n in range(NG // 2):
        both = jnp.dot(edges, PM[:, 256 * n : 256 * n + 256], preferred_element_type=F32)
        for h in range(2):
            for k in range(NI + 1):
                part = both[8 * k : 8 * k + 8, 128 * h : 128 * h + 128]
                PS[2 * n + h, k, 8:16] = part
                PS[2 * n + h, k, 80:88] = part


def shift_blocks(PS, Z, g):
    for k in range(NI + 1):
        for e, shift in enumerate(SHIFTS):
            Z[g, k, :, 128 * e : 128 * e + 128] = PS[g, k, 16 + shift : 16 + shift + ZR].astype(BF16)


INNER = ((1, 2, 3, 4), (5, 6, 7, 8), (9, 10, 11))


def banded_conv(Z, W, AB, S, M, g):
    lhs = jnp.concatenate([Z[g, 0:NI].reshape(NI * ZR, 512), Z[g, 1 : NI + 1].reshape(NI * ZR, 512)], axis=1)
    both = jnp.dot(lhs, W[g], preferred_element_type=F32)
    AB[g % 2] = both[:, 128:256]
    for n in range(NI):
        value = both[n * ZR : n * ZR + 64, 0:128] + AB[g % 2, n * ZR + 1 : n * ZR + 65]
        S[g, n] = (value if M is None else value * M[n]).astype(BF16)


def ungroup(S, PM, blocks, put):
    rows = [jnp.concatenate([S[g, k] for k in blocks], axis=0) for g in range(NG)]
    lhs = jnp.concatenate(rows, axis=1)
    for n in range(NG // 2):
        put(n, jnp.dot(lhs, PM[:, 256 * n : 256 * n + 256], preferred_element_type=F32))


def conv_kernel(fields, upstream, w_in, w_out, land_far, w_far,
                conv_out, Z, X, near_up, near_in, near_out,
                land, w, EX, XH, EL, ER, LH, RH, EH, PS, W, PM, AB, S, M, land_pad, send, recv, load):
    lon, lat = lax.axis_index("lon"), lax.axis_index("lat")
    around = neighbours(lon, lat)
    greet(around)
    pairs = ((land_far, land), (fields, X), (w_far, w), (upstream, near_up), (w_in, near_in), (w_out, near_out))
    loads = [pltpu.make_async_copy(far, near, load.at[n]) for n, (far, near) in enumerate(pairs)]
    for copy in loads:
        copy.start()
    land_pad[...] = jnp.zeros((CLAT, 128), F32)
    loads[0].wait()
    land_pad[:, 0:CLON] = land[...].astype(F32)
    land_t = land_pad[...]
    expand_mask(with_ones(land_t), M, NI + 1)
    low = iota((8, 128), 0) < 4
    masks = []
    for east in range(2):
        edge = land_pad[56 * east : 56 * east + 8]
        turned = pltpu.roll(edge, 4, axis=0)
        edge = jnp.where(low, turned, edge) if east else jnp.where(low, edge, turned)
        masks.append(jnp.where(low, edge, pltpu.roll(edge, 127, axis=1)))
    loads[1].wait()
    pack_edges(X, EL, ER, masks)
    for at, first in ((0, 0), (23, CLON - 4)):
        for i in range(4):
            keep = jnp.broadcast_to(land_t[:, first + i : first + i + 1], (CLAT, C))
            EX[at // 23, i] = (X[at, i].astype(F32) * keep).astype(BF16)
    greeted(around)
    copies = halo_copies(EX.at[0], EX.at[1], XH, EL, ER, LH, RH, send, recv, lon, lat)
    for copy in copies:
        copy.start()
    build_permutation(PM)
    clear_margins(PS)
    cells = padded_cells(X, XH)

    for blocks in INNER:
        group_blocks(cells, blocks, PM, PS, M)
    loads[2].wait()
    build_weights(w, W, False)
    for copy in copies:
        copy.wait()
    group_blocks(cells, (0, NI), PM, PS, M)
    group_halos(LH, RH, EH, PM, PS, lat)
    for g in range(NG):
        shift_blocks(PS, Z, g)
        banded_conv(Z, W, AB, S, None, g)
    for first in range(0, NI, 4):

        def put(n, both, first=first):
            for m in range(4):
                for t in range(NJ):
                    at = 64 * m + 8 * t
                    value = jnp.concatenate([both[at : at + 8, 0:128], both[at : at + 8, 128:256]], axis=0)
                    conv_out[(first + m) * NJ + t, 16 * n : 16 * n + 16] = value.astype(BF16)

        ungroup(S, PM, range(first, first + 4), put)
    for copy in loads[3:]:
        copy.wait()


def vmem(n):
    return [pl.BlockSpec(memory_space=pltpu.VMEM)] * n


def hbm(n):
    return [pl.BlockSpec(memory_space=pl.ANY)] * n


def halo_scratch():
    return [
        pltpu.VMEM((2, 4, CLAT, C), BF16),
        pltpu.VMEM((NI, 32, C), BF16),
        pltpu.VMEM((NI, 32, C), BF16),
        pltpu.VMEM((14, 32, C), BF16),
        pltpu.VMEM((14, 32, C), BF16),
        pltpu.VMEM((7, 16, 1024), BF16),
        pltpu.VMEM((NG, NI + 1, 104, 128), F32),
        pltpu.VMEM((NG, 1024, 256), BF16),
        pltpu.VMEM((1024, 1024), BF16),
        pltpu.VMEM((2, NI * ZR, 128), F32),
        pltpu.VMEM((NG, NI, 64, 128), BF16),
        pltpu.VMEM((NI + 1, 64, 128), F32),
        pltpu.VMEM((CLAT, 128), F32),
    ]


def forward_conv(fields, upstream, w_in, w_out, land, w):
    dma = pltpu.SemaphoreType.DMA
    return pl.pallas_call(
        conv_kernel,
        name="forward_conv",
        out_shape=(
            pltpu.VMEM((TILES, 64, C), BF16),
            pltpu.VMEM((NG, NI + 1, ZR, 512), BF16),
            pltpu.VMEM((24, 4, CLAT, C), BF16),
            pltpu.VMEM((CLON, CLAT, C), BF16),
            pltpu.VMEM((C, FF), BF16),
            pltpu.VMEM((FF, C), BF16),
        ),
        in_specs=hbm(6),
        out_specs=tuple(vmem(6)),
        scratch_shapes=[
            pltpu.VMEM((CLAT, CLON), jnp.int32),
            pltpu.VMEM((49, C), F32),
            pltpu.VMEM((2, 4, CLAT, C), BF16),
        ]
        + halo_scratch()
        + [dma((8,)), dma((8,)), dma((6,))],
        compiler_params=pltpu.CompilerParams(collective_id=0, has_side_effects=True, vmem_limit_bytes=VMEM_LIMIT),
    )(fields, upstream, w_in, w_out, land, w)


def normal_cdf(h, square):
    q = jnp.full(h.shape, ERF_COEFS[-1], F32)
    for coef in ERF_COEFS[-2::-1]:
        q = q * square + coef
    return 0.5 + 0.5 * jnp.tanh(h * q)


def mlp_kernel(tile_ids, conv, fields, upstream, land, offset, gain, shift, w_in, b_in, w_out, b_out, scale,
               mixed, d_conv_out, shares, branch, d_conv, w_in_t, w_out_t, g_in, g_out, g_bin, sums, land_tr, mixed_part, store):
    slots = 18
    rows = slots * 64
    land_tr[...] = jnp.zeros((CLAT, 128), F32)
    land_tr[:, 0:CLON] = land[...].astype(F32)
    w_in_t[...] = w_in[...].astype(F32).T.astype(BF16)
    w_out_t[...] = w_out[...].astype(F32).T.astype(BF16)
    branch[...] = jnp.zeros(branch.shape, F32)
    d_conv[...] = jnp.zeros(d_conv.shape, F32)
    for acc in (g_in, g_out, g_bin, sums):
        acc[...] = jnp.zeros(acc.shape, F32)
    gain_row, shift_row, scale_row = gain[...], shift[...], scale[...]

    def step(n, carry):
        ids = [tile_ids[slots * n + q] for q in range(slots)]
        tiles = [jnp.maximum(t, 0) for t in ids]
        conv_parts, up_parts, active_parts = [], [], []
        for q in range(slots):
            t = tiles[q]
            big, small = t // NJ, lax.rem(t, NJ)
            conv_parts.append(conv[t].astype(F32))
            pair = upstream[pl.ds(8 * big, 8), pl.ds(16 * (small // 2), 16), :].astype(F32)
            odd = lax.rem(small, 2) == 1
            up_parts.append(jnp.where(odd, pair[:, 8:16], pair[:, 0:8]).reshape(64, C))
            strip = pltpu.roll(land_tr[pl.ds(8 * small, 8), :], lax.rem(128 - 8 * big, 128), axis=1)
            live = jnp.where(ids[q] >= 0, 1.0, 0.0)
            strip = strip * live
            active_parts += [jnp.broadcast_to(strip[:, i : i + 1], (8, C)) for i in range(8)]
        conv_rows = jnp.concatenate(conv_parts, axis=0) + offset[...]
        up = jnp.concatenate(up_parts, axis=0)
        active = jnp.concatenate(active_parts, axis=0)
        center = conv_rows - jnp.mean(conv_rows, axis=-1, keepdims=True)
        inv_std = lax.rsqrt(jnp.mean(center * center, axis=-1, keepdims=True) + LN_EPSILON)
        normed = center * inv_std
        normed_b = (normed * gain_row + shift_row).astype(BF16)
        hidden = jnp.dot(normed_b, w_in[...], preferred_element_type=F32) + b_in[...]
        square = hidden * hidden
        cdf = normal_cdf(hidden, square)
        activated = (hidden * cdf).astype(BF16)
        output = jnp.dot(activated, w_out[...], preferred_element_type=F32) + b_out[...]
        gate = active * scale_row
        branch_rows = gate * output
        d_out = gate * up
        d_out_b = d_out.astype(BF16)
        g_out[...] += lax.dot_general(d_out_b, activated, (((0,), (0,)), ((), ())), preferred_element_type=F32)
        pdf = jnp.exp2(square * PDF_SCALE + PDF_SHIFT)
        d_hidden = jnp.dot(d_out_b, w_out_t[...], preferred_element_type=F32) * (cdf + hidden * pdf)
        d_hidden_b = d_hidden.astype(BF16)
        g_in[...] += lax.dot_general(normed_b, d_hidden_b, (((0,), (0,)), ((), ())), preferred_element_type=F32)
        g_bin[...] += jnp.sum(d_hidden.reshape(rows // 8, 8, FF), axis=0)
        d_norm = jnp.dot(d_hidden_b, w_in_t[...], preferred_element_type=F32)
        d_scaled = d_norm * gain_row
        d_cells = inv_std * (
            d_scaled
            - jnp.mean(d_scaled, axis=-1, keepdims=True)
            - normed * jnp.mean(d_scaled * normed, axis=-1, keepdims=True)
        )
        for k, term in enumerate((d_cells, d_norm * normed, d_norm, d_out, active * output * up)):
            sums[k] += jnp.sum(term.reshape(rows // 8, 8, C), axis=0)
        for q in range(slots):
            to = jnp.where(ids[q] >= 0, ids[q], TILES)
            branch[to] = branch_rows[64 * q : 64 * q + 64]
            d_conv[to] = d_cells[64 * q : 64 * q + 64]

        return carry

    lax.fori_loop(0, TCAP // slots, step, 0)

    stores = [
        pltpu.make_async_copy(mixed_part.at[n], mixed.at[pl.ds(32 * n, 32)], store.at[n]) for n in range(3)
    ]
    for chunk in range(3):

        def mix(n, carry, chunk=chunk):
            for i in range(8):
                rows_i = jnp.concatenate([branch[n * NJ + t, 8 * i : 8 * i + 8] for t in range(NJ)], axis=0)
                total = fields[2 * n + i // 4, i % 4].astype(F32) + rows_i
                mixed_part[chunk, 8 * (n - 4 * chunk) + i] = total.astype(BF16)
                rows_i = jnp.concatenate([d_conv[n * NJ + t, 8 * i : 8 * i + 8] for t in range(NJ)], axis=0)
                d_conv_out[2 * n + i // 4, i % 4] = rows_i.astype(BF16)
            return carry

        lax.fori_loop(4 * chunk, 4 * chunk + 4, mix, 0)
        stores[chunk].start()
    bin_row = jnp.sum(g_bin[...], axis=0, keepdims=True)
    tail = jnp.concatenate([jnp.sum(sums[k], axis=0, keepdims=True) for k in range(5)], axis=0)
    for n in range(4):
        turned_in = g_in[:, 128 * n : 128 * n + 128].T
        turned_out = g_out[:, 128 * n : 128 * n + 128].T
        for m in range(4):
            q = 4 * n + m
            shares[q, 0:32] = turned_in[32 * m : 32 * m + 32].astype(BF16)
            shares[q, 32:64] = turned_out[32 * m : 32 * m + 32].astype(BF16)
            rest = [bin_row[:, 128 * n : 128 * n + 128], tail, jnp.zeros((10, 128), F32)]
            shares[q, 64:80] = jnp.concatenate(rest, axis=0).astype(BF16)
    for copy in stores:
        copy.wait()


def listed_mlp(tile_ids, conv, fields, upstream, land, offset, gain, shift, w_in, b_in, w_out, b_out, scale):
    return pl.pallas_call(
        mlp_kernel,
        name="listed_mlp",
        out_shape=(
            jax.ShapeDtypeStruct((CLON, CLAT, C), BF16),
            pltpu.VMEM((24, 4, CLAT, C), BF16),
            pltpu.VMEM((N_LAT, 80, 128), BF16),
        ),
        in_specs=[pl.BlockSpec(memory_space=pltpu.SMEM)] + vmem(12),
        out_specs=tuple(hbm(1) + vmem(2)),
        scratch_shapes=[
            pltpu.VMEM((TILES + 1, 64, C), F32),
            pltpu.VMEM((TILES + 1, 64, C), F32),
            pltpu.VMEM((FF, C), BF16),
            pltpu.VMEM((C, FF), BF16),
            pltpu.VMEM((C, FF), F32),
            pltpu.VMEM((C, FF), F32),
            pltpu.VMEM((8, FF), F32),
            pltpu.VMEM((5, 8, C), F32),
            pltpu.VMEM((CLAT, 128), F32),
            pltpu.VMEM((3, 32, CLAT, C), BF16),
            pltpu.SemaphoreType.DMA((3,)),
        ],
        compiler_params=pltpu.CompilerParams(vmem_limit_bytes=VMEM_LIMIT),
    )(tile_ids, conv, fields, upstream, land, offset, gain, shift, w_in, b_in, w_out, b_out, scale)


def pair_rows(PS, MP):
    for g in range(NG):
        for n in range(NI):
            MP[g, n, :, 0:128] = PS[g, n, 16 : 16 + ZR].astype(BF16)
            MP[g, n, :, 128:256] = PS[g, n, 15 : 15 + ZR].astype(BF16)


def tap_gradients(Z, MP, G, taps, groups):
    lane = iota((16, 128), 1)
    same = (iota((16, 128), 0) == lane % 16).astype(F32)
    block = lane // 16
    for g in groups:
        taps[g] = jnp.zeros(taps.shape[1:], F32)
        lhs = MP[g].reshape(NI * ZR, 256)
        for half in range(2):
            rhs = Z[g, half : half + NI].reshape(NI * ZR, 512)
            G[g % 2, half] = lax.dot_general(lhs, rhs, (((0,), (0,)), ((), ())), preferred_element_type=F32)
        for e in range(4):
            for parity in range(2):
                b = 3 + SHIFTS[e] + parity
                if not 0 <= b < 7:
                    continue
                for a in range(7):
                    total = None
                    for i_out in range(8):
                        half, k = divmod(i_out + a + 1, 8)
                        at = 128 * parity + 16 * i_out
                        piece = G[g % 2, half, at : at + 16, 128 * e : 128 * e + 128]
                        total = piece if total is None else jnp.where(block == k, piece, total)
                    taps[g, 7 * a + b : 7 * a + b + 1] = jnp.sum(total * same, axis=0, keepdims=True)


def gather_taps(taps, square, tap_shares):
    total = jnp.zeros((56, 128), F32)
    for g in range(NG):
        row, col = iota((128, 128), 0), iota((128, 128), 1)
        pick = jnp.where((col // 16 == g) & (row % 16 == col % 16), 1.0, 0.0).astype(BF16)
        value = taps[g]
        head = value.astype(BF16)
        tail = (value - head.astype(F32)).astype(BF16)
        total += jnp.dot(head, pick, preferred_element_type=F32) + jnp.dot(tail, pick, preferred_element_type=F32)
    square[...] = jnp.zeros((128, 128), F32)
    square[0:56] = total
    turned = square[...].T
    for q in range(N_LAT):
        tap_shares[q] = turned[8 * q : 8 * q + 8]


def grad_kernel(d_conv, ZM, land, w, shares,
                S, total_out,
                XH, EL, ER, LH, RH, EH, PS, W, PM, AB, M, land_pad,
                Z, MP, G, taps, square, tap_shares, parts, tap_parts, mine, whole, tap_mine, tap_whole,
                send, recv, send_one, recv_one, send_tap, recv_tap, send_two, recv_two, send_last, recv_last):
    lon, lat = lax.axis_index("lon"), lax.axis_index("lat")
    around = neighbours(lon, lat)
    around += [(lon, lax.rem(lat + d, N_LAT)) for d in range(2, N_LAT - 1)]
    around += [(lax.rem(lon + d, N_LON), lat) for d in range(2, N_LON - 1)]
    greet(around)
    pack_edges(d_conv, EL, ER, None)
    build_permutation(PM)
    clear_margins(PS)
    build_weights(w, W, True)
    land_pad[...] = jnp.zeros((CLAT, 128), F32)
    land_pad[:, 0:CLON] = land[...].astype(F32)
    expand_mask(land_pad[...], M, NI)
    greeted(around)
    copies = halo_copies(d_conv.at[0], d_conv.at[23], XH, EL, ER, LH, RH, send, recv, lon, lat)
    for copy in copies:
        copy.start()
    share_copies, tap_copies = [], []
    for d in range(1, N_LAT):
        to = lax.rem(lat + d, N_LAT)
        share_copies.append(pltpu.make_async_remote_copy(
            src_ref=shares.at[to], dst_ref=parts.at[d], send_sem=send_one.at[d], recv_sem=recv_one.at[d],
            device_id=(lon, to), device_id_type=MESH))
        tap_copies.append(pltpu.make_async_remote_copy(
            src_ref=tap_shares.at[to], dst_ref=tap_parts.at[d], send_sem=send_tap.at[d], recv_sem=recv_tap.at[d],
            device_id=(lon, to), device_id_type=MESH))
    for copy in share_copies:
        copy.start()
    for blocks in ((0, 1, 2, 3), (4, 5, 6, 7), (8, 9, 10, 11)):
        group_blocks(lambda k, i: d_conv[2 * k + i // 4, i % 4], blocks, PM, PS, None)
    pair_rows(PS, MP)
    for g in range(NG):
        tap_gradients(ZM, MP, G, taps, (g,))
    gather_taps(taps, square, tap_shares)
    for copy in tap_copies:
        copy.start()
    cells = padded_cells(d_conv, XH)
    for blocks in INNER:
        group_blocks(cells, blocks, PM, PS, None)
    for copy in copies:
        copy.wait()
    group_blocks(cells, (0, NI), PM, PS, None)
    group_halos(LH, RH, EH, PM, PS, lat)
    for copy in share_copies:
        copy.wait()
    total = shares[lat].astype(F32)
    for d in range(1, N_LAT):
        total += parts[d].astype(F32)
    mine[...] = (total * GRAD_SCALE).astype(BF16)

    def spread(block, parts, send_sem, recv_sem):
        made = [
            pltpu.make_async_remote_copy(
                src_ref=block, dst_ref=parts.at[d], send_sem=send_sem.at[d], recv_sem=recv_sem.at[d],
                device_id=(lax.rem(lon + d, N_LON), lat), device_id_type=MESH)
            for d in range(1, N_LON)
        ]
        for copy in made:
            copy.start()
        return made

    last_copies = spread(mine, whole, send_two, recv_two)
    for g in range(2):
        shift_blocks(PS, Z, g)
        banded_conv(Z, W, AB, S, M, g)
    for copy in tap_copies:
        copy.wait()
    total = tap_shares[lat]
    for d in range(1, N_LAT):
        total += tap_parts[d]
    tap_mine[...] = total * GRAD_SCALE
    last_copies += spread(tap_mine, tap_whole, send_last, recv_last)
    for g in range(2, NG):
        shift_blocks(PS, Z, g)
        banded_conv(Z, W, AB, S, M, g)
    for copy in last_copies:
        copy.wait()
    total, tap_total = mine[...].astype(F32), tap_mine[...]
    for d in range(1, N_LON):
        total += whole[d].astype(F32)
        tap_total += tap_whole[d]
    total_out[0:80] = total
    total_out[80:88] = tap_total


def backward_conv(d_conv, shifted, land, w, shares):
    dma = pltpu.SemaphoreType.DMA
    scratch = halo_scratch()
    scratch.pop(10)
    return pl.pallas_call(
        grad_kernel,
        name="backward_conv",
        out_shape=(pltpu.VMEM((NG, NI, 64, 128), BF16), pltpu.VMEM((88, C), F32)),
        in_specs=vmem(5),
        out_specs=tuple(vmem(2)),
        scratch_shapes=scratch
        + [
            pltpu.VMEM((NG, NI + 1, ZR, 512), BF16),
            pltpu.VMEM((NG, NI, ZR, 256), BF16),
            pltpu.VMEM((2, 2, 256, 512), F32),
            pltpu.VMEM((NG, 56, 128), F32),
            pltpu.VMEM((128, 128), F32),
            pltpu.VMEM((N_LAT, 8, 128), F32),
            pltpu.VMEM((N_LAT, 80, 128), BF16),
            pltpu.VMEM((N_LAT, 8, 128), F32),
            pltpu.VMEM((80, 128), BF16),
            pltpu.VMEM((N_LON, 80, 128), BF16),
            pltpu.VMEM((8, 128), F32),
            pltpu.VMEM((N_LON, 8, 128), F32),
            dma((8,)), dma((8,)), dma((N_LAT,)), dma((N_LAT,)), dma((N_LAT,)), dma((N_LAT,)),
            dma((N_LON,)), dma((N_LON,)), dma((N_LON,)), dma((N_LON,)),
        ],
        compiler_params=pltpu.CompilerParams(collective_id=1, has_side_effects=True, vmem_limit_bytes=VMEM_LIMIT),
    )(d_conv, shifted, land, w, shares)


def finish_kernel(place, S, up, total, grad_input, out_win, out_wout, out_dw, out_channel, out_bin,
                  made, PM, store):
    copies = [
        pltpu.make_async_copy(made.at[n], grad_input.at[pl.ds(32 * n, 32)], store.at[n]) for n in range(3)
    ]
    build_permutation(PM)
    lat = place[0]
    out_win[...] = total[0:32]
    out_wout[...] = total[32:64]
    small = total[64:72]
    out_bin[...] = pltpu.roll(small, lax.rem(128 - 32 * lax.rem(lat, 4), 128), axis=1)[0:1, 0:32]
    out_channel[...] = pltpu.roll(small, lax.rem(128 - 8 * lat, 128), axis=1)[1:6, 0:8]
    out_dw[...] = total[80:88, 0:49]
    for chunk in range(3):

        def put(n, both, chunk=chunk):
            for m in range(4):
                for h in range(2):
                    at = 8 * m + 2 * n + h
                    value = up[32 * chunk + at].astype(F32) + both[64 * m : 64 * m + 64, 128 * h : 128 * h + 128]
                    made[chunk, at] = value.astype(BF16)

        ungroup(S, PM, range(4 * chunk, 4 * chunk + 4), put)
        copies[chunk].start()
    for copy in copies:
        copy.wait()


def finish(place, S, upstream, total):
    dma = pltpu.SemaphoreType.DMA
    return pl.pallas_call(
        finish_kernel,
        name="finish",
        out_shape=(
            jax.ShapeDtypeStruct((CLON, CLAT, C), BF16),
            jax.ShapeDtypeStruct((32, C), F32),
            jax.ShapeDtypeStruct((32, C), F32),
            jax.ShapeDtypeStruct((8, 49), F32),
            jax.ShapeDtypeStruct((5, 8), F32),
            jax.ShapeDtypeStruct((1, 32), F32),
        ),
        in_specs=[pl.BlockSpec(memory_space=pltpu.SMEM)] + vmem(3),
        out_specs=tuple(hbm(1) + vmem(5)),
        scratch_shapes=[
            pltpu.VMEM((3, 32, CLAT, C), BF16),
            pltpu.VMEM((1024, 1024), BF16),
            dma((3,)),
        ],
        compiler_params=pltpu.CompilerParams(vmem_limit_bytes=VMEM_LIMIT),
    )(place, S, upstream, total)


def per_device(fields, land_sea, tile_list, upstream, dw_weight, dw_bias, ln_gain, ln_bias, w_in, b_in, w_out, b_out,
               layer_scale):
    def row(v):
        return v.reshape(1, -1)

    fours = fields.reshape(24, 4, CLAT, C)
    land = land_sea.T
    far = [pltpu.with_memory_space_constraint(v, pltpu.HBM) for v in (fours, upstream, w_in, w_out, land, dw_weight)]
    conv, shifted, near_fours, near_up, near_in, near_out = forward_conv(*far)
    mixed, d_conv, shares = listed_mlp(
        tile_list.reshape(-1), conv, near_fours, near_up, land, row(dw_bias), row(ln_gain), row(ln_bias), near_in, row(b_in), near_out,
        row(b_out), row(layer_scale))
    grouped, total = backward_conv(d_conv, shifted, land, dw_weight, shares)
    place = lax.axis_index("lat").astype(jnp.int32).reshape(1)
    grad_input, g_win, g_wout, g_dw, g_channel, g_bin = finish(place, grouped, near_up, total)
    return mixed, grad_input, g_win.T, g_wout, g_dw.T, g_channel, g_bin.reshape(-1)


def solution(mesh):
    cells = P("lon", "lat", None)
    return jax.shard_map(
        per_device,
        mesh=mesh,
        in_specs=(cells, P("lon", "lat"), cells, cells) + (P(),) * 9,
        out_specs=(cells, cells, P(None, "lat"), P("lat", None), P(None, "lat"), P(None, "lat"), P("lat")),
        check_vma=False,
    )
```
